32 devices in a mesh: dp: 8 (over z, y), seq: 4 (over x, core).
Axes of the slice: x: 2, y: 2, z: 4, core: 2. Of those that a mesh axis runs over, the one named last changes fastest.
Arguments:
- tokens: bfloat16 [16, 1024, 1024], P('dp', 'seq'), may hold values from -6 to 6
- bins: int32 [16], P('dp'), may hold values from 0 to 127
- plan: float32 [128], replicated, may hold values from 1 to 300
- w_qkv: bfloat16 [1024, 3072], P('dp', 'seq'), may hold values from -0.1875 to 0.1875
- w_out: bfloat16 [1024, 1024], P('seq', 'dp'), may hold values from -1.5 to 1.5
- w_up: bfloat16 [1024, 4096], P('dp', 'seq'), may hold values from -0.1875 to 0.1875
- w_down: bfloat16 [4096, 1024], P('seq', 'dp'), may hold values from -0.09375 to 0.09375
- w_time: bfloat16 [256, 2048], P(('dp', 'seq')), may hold values from -0.1875 to 0.1875
- cotangent: bfloat16 [16, 1024, 1024], P('dp', 'seq'), may hold values from -6 to 6
Outputs:
- output: bfloat16 [16, 1024, 1024], P('dp', 'seq')
- grad_tokens: bfloat16 [16, 1024, 1024], P('dp', 'seq')
- grad_qkv: float32 [1024, 3072], P('dp', 'seq')
- grad_out: float32 [1024, 1024], P('seq', 'dp')
- grad_up: float32 [1024, 4096], P('dp', 'seq')
- grad_down: float32 [4096, 1024], P('seq', 'dp')
- grad_time: float32 [256, 2048], P(('dp', 'seq'))
The draws below stay inside these ranges and needn't reach their ends.
All inputs are finite; a program needn't handle non-finite values.
Results may differ from the reference program's by a relative error of at most 0.02.
Values may be sent and summed in bfloat16 or wider, within the bound.
A program may use at most 192 MiB of HBM per device.

```python
import math
import jax
import jax.numpy as jnp
from jax import lax

D = 1024
H = 16
HD = 64
FF = 4096
TF = 256
BINS = 128
LEN = 1024
BATCH = 16


def place_ends(drawn, stream_key, least, high):
    longest = drawn.shape.index(max(drawn.shape))
    spots = []
    for shift in (0, 1):
        where = [jax.random.randint(jax.random.fold_in(stream_key, axis), (), 0, length) for axis, length in enumerate(drawn.shape)]
        where[longest] = (where[longest] + shift) % drawn.shape[longest]
        spots.append(tuple(where))
    return drawn.at[spots[0]].set(least).at[spots[1]].set(high)


def shard_levels(key, extent, cuts, smallest, top_value):
    def one(dim, shards_of):
        heights = jax.random.uniform(jax.random.fold_in(jax.random.fold_in(key, 6), dim), (shards_of,), jnp.float32, smallest / len(cuts), top_value / len(cuts))
        return jnp.repeat(jnp.exp(heights), extent[dim] // shards_of).reshape((-1,) + (1,) * (len(extent) - dim - 1))

    level = one(*cuts[0])
    for cut in cuts[1:]:
        level = level * one(*cut)
    return level


def gaussian(stream_key, shape, scale, limit, cuts=(), kind=jnp.bfloat16):
    loudness = shard_levels(stream_key, shape, cuts, -0.22, 0.18) if cuts else 1.0
    drawn = jax.random.normal(stream_key, shape, jnp.float32) * scale * loudness
    return jnp.minimum(jnp.maximum(drawn, -limit), limit).astype(kind)


def setup_inputs(seed: int = 0) -> dict:
    seeds = jax.random.split(jax.random.key(seed), 10)
    return {
        "tokens": gaussian(seeds[0], (BATCH, LEN, D), 1.0, 6.0, ((0, 8), (1, 4))),
        "bins": place_ends(jax.random.randint(seeds[1], (BATCH,), 0, BINS), jax.random.fold_in(seeds[1], 1), 0, BINS - 1).astype(jnp.int32),
        "plan": jnp.clip(jnp.exp(jax.random.uniform(seeds[2], (BINS,), jnp.float32, math.log(1.0), math.log(300.0))), 1.0, 300.0),
        "w_qkv": gaussian(seeds[3], (D, 3 * D), D ** -0.5, 0.1875, ((0, 8), (1, 4))),
        "w_out": gaussian(seeds[4], (D, D), (D * 16 // LEN) ** -0.5, 1.5, ((0, 4), (1, 8))),
        "w_up": gaussian(seeds[5], (D, FF), D ** -0.5, 0.1875, ((0, 8), (1, 4))),
        "w_down": gaussian(seeds[6], (FF, D), FF ** -0.5, 0.09375, ((0, 4), (1, 8))),
        "w_time": gaussian(seeds[7], (TF, 2 * D), (4 * TF) ** -0.5, 0.1875, ((0, 32),)),
        "cotangent": gaussian(seeds[8], (BATCH, LEN, D), 1.0, 6.0, ((0, 8), (1, 4))),
    }


@jax.custom_vjp
def low(v):
    return lax.optimization_barrier(v.astype(jnp.bfloat16)).astype(jnp.float32)

@jax.custom_vjp
def low_back(v):
    return v

def low_keep(v):
    return (low(v), None)

def low_pass(kept, grad):
    return (grad,)

def back_keep(v):
    return (v, None)

def back_low(kept, grad):
    return (low(grad),)
low.defvjp(low_keep, low_pass)
low_back.defvjp(back_keep, back_low)
EPSILON = 1e-05
HIGHEST = lax.Precision.HIGHEST

def time_features(plan, bins):
    sigma = jnp.take(plan, bins, axis=0)
    level = 0.25 * jnp.log(sigma)
    count = TF // 2
    freqs = jnp.exp(jnp.arange(count, dtype=jnp.float32) * (math.log(1000.0) / count))
    angles = level[:, None] * freqs[None, :]
    return jnp.concatenate([jnp.sin(angles), jnp.cos(angles)], axis=1)

def normalize(field):
    centered = field - lax.optimization_barrier(jnp.mean(field, axis=-1, keepdims=True))
    spread = lax.optimization_barrier(jnp.mean(centered * centered, axis=-1, keepdims=True))
    return centered * lax.rsqrt(spread + EPSILON)

def rotary_tables(length):
    half = HD // 2
    places = jnp.arange(length, dtype=jnp.float32)
    inverse = jnp.exp(jnp.arange(half, dtype=jnp.float32) * (-math.log(10000.0) / half))
    angle = places[:, None] * inverse[None, :]
    return (jnp.cos(angle)[:, None, None, :], jnp.sin(angle)[:, None, None, :])

def rotate(field, cosine, sine):
    half = HD // 2
    first = field[..., :half]
    second = field[..., half:]
    return jnp.concatenate([first * cosine - second * sine, second * cosine + first * sine], axis=-1)

def attend_block(query_blk, keys, values):
    scores = low_back(HD ** (-0.5) * jnp.einsum('gqhd,gkhd->ghqk', query_blk, keys, precision=HIGHEST))
    probs = jax.nn.softmax(scores, axis=-1)
    return jnp.einsum('ghqk,gkhd->gqhd', low(probs), values, precision=HIGHEST)

def layer(field, w_qkv, w_out, w_up, w_down, w_time, feats):
    group = field.shape[0]
    modul = jnp.dot(low(feats), w_time, precision=HIGHEST)
    scale_one = 1.0 + modul[:, None, :D]
    scale_two = 1.0 + modul[:, None, D:]
    h_one = low(normalize(field) * scale_one)
    raw = low_back(jnp.einsum('gtd,de->gte', h_one, w_qkv, precision=HIGHEST))
    raw = raw.reshape(group, LEN, H, 3, HD)
    cosine, sine = rotary_tables(LEN)
    turned = rotate(raw[:, :, :, 0:2], cosine, sine)
    packed = low_back(low(jnp.concatenate([turned, raw[:, :, :, 2:3]], axis=3)))
    query = packed[:, :, :, 0]
    keys = packed[:, :, :, 1]
    values = packed[:, :, :, 2]
    block = min(512, LEN)
    count = LEN // block
    query_blocks = jnp.transpose(query.reshape(group, count, block, H, HD), (1, 0, 2, 3, 4))
    checked = jax.checkpoint(attend_block)
    attended = lax.map(lambda piece: checked(piece, keys, values), query_blocks)
    attended = jnp.transpose(attended, (1, 0, 2, 3, 4)).reshape(group, LEN, D)
    attended = low_back(low(attended))
    branch = low_back(jnp.einsum('gtd,de->gte', attended, w_out, precision=HIGHEST))
    middle = field + branch
    h_two = low(normalize(middle) * scale_two)
    upper = low_back(jnp.einsum('gtd,df->gtf', h_two, w_up, precision=HIGHEST))
    active = low(jax.nn.gelu(upper, approximate=False))
    return middle + jnp.einsum('gtf,fd->gtd', active, w_down, precision=HIGHEST)

def reference(tokens, bins, plan, w_qkv, w_out, w_up, w_down, w_time, cotangent):
    feats_all = time_features(plan, bins)
    total = tokens.shape[0]
    group = math.gcd(total, 4)
    steps_count = total // group
    weights = tuple((w.astype(jnp.float32) for w in (w_qkv, w_out, w_up, w_down, w_time)))

    def one_group(carry, pieces):
        field, grads_in, feats = pieces

        def forward(inputs, *params):
            return layer(inputs, *params, feats)
        result, pull = jax.vjp(forward, field.astype(jnp.float32), *weights)
        grads = pull(grads_in.astype(jnp.float32))
        updated = tuple((c + g for c, g in zip(carry, grads[1:])))
        return (updated, (result.astype(jnp.bfloat16), grads[0].astype(jnp.bfloat16)))
    start = tuple((jnp.zeros(w.shape, jnp.float32) for w in weights))
    stacked = (tokens.reshape(steps_count, group, LEN, D), cotangent.reshape(steps_count, group, LEN, D), feats_all.reshape(steps_count, group, TF))
    sums, (outputs, input_grads) = lax.scan(one_group, start, stacked)
    return (outputs.reshape(total, LEN, D), input_grads.reshape(total, LEN, D), sums[0], sums[1], sums[2], sums[3], sums[4])
```

```python
import functools
import math

import jax
import jax.numpy as jnp
from jax import lax
from jax.experimental import pallas as pl
from jax.experimental.pallas import tpu as pltpu
from jax.sharding import PartitionSpec as P

D = 1024
HD = 64
TF = 256
LEN = 1024


EPSILON = 1e-05
HIGHEST = lax.Precision.HIGHEST
ROOT_HALF = 0.7071067811865476
DENSITY = 0.3989422804014327


def time_features(plan, bins):
    table = jnp.arange(plan.shape[0], dtype=jnp.int32)
    picked = jnp.where(bins[:, None] == table[None, :], plan[None, :], 0.0)
    sigma = jnp.sum(picked, axis=1)
    level = 0.25 * jnp.log(sigma)
    count = TF // 2
    freqs = jnp.exp(jnp.arange(count, dtype=jnp.float32) * (math.log(1000.0) / count))
    angles = level[:, None] * freqs[None, :]
    return jnp.concatenate([jnp.sin(angles), jnp.cos(angles)], axis=1)


def normalize(field):
    centered = field - jnp.mean(field, axis=-1, keepdims=True)
    spread = jnp.mean(centered * centered, axis=-1, keepdims=True)
    inverse = lax.rsqrt(spread + EPSILON)
    return (centered * inverse, inverse)


def norm_backward(grad_scaled, normed, inverse, scale):
    grad_normed = grad_scaled * scale
    grad_scale = jnp.sum(grad_scaled * normed, axis=1)
    inner = jnp.mean(grad_normed * normed, axis=-1, keepdims=True)
    grad_field = inverse * (
        grad_normed - jnp.mean(grad_normed, axis=-1, keepdims=True) - normed * inner
    )
    return (grad_field, grad_scale)


def rotate(field, cosine, sine):
    half = HD // 2
    first = field[..., :half]
    second = field[..., half:]
    return jnp.concatenate(
        [first * cosine - second * sine, second * cosine + first * sine], axis=-1
    )


def rotary_tables(places):
    half = HD // 2
    inverse = jnp.exp(jnp.arange(half, dtype=jnp.float32) * (-math.log(10000.0) / half))
    angle = places[:, None] * inverse[None, :]
    return (jnp.cos(angle)[:, None, None, :], jnp.sin(angle)[:, None, None, :])


def pack_heads(h_one, qkv_weight, cosine, sine):
    seqs, rows, width = h_one.shape
    raw = jnp.einsum("std,de->ste", h_one, qkv_weight, preferred_element_type=jnp.float32)
    local_heads = qkv_weight.shape[1] // (3 * HD)
    raw = raw.reshape(seqs, rows, local_heads, 3, HD)
    turned = rotate(raw[:, :, :, 0:2], cosine, sine)
    packed = jnp.concatenate([turned, raw[:, :, :, 2:3]], axis=3).astype(jnp.bfloat16)
    return packed.reshape(seqs, rows, local_heads * 3 * HD)


def unpack_grads(grad_packed, cosine, sine):
    seqs, rows, width = grad_packed.shape
    local_heads = width // (3 * HD)
    grad_fields = grad_packed.reshape(seqs, rows, local_heads, 3, HD).astype(jnp.float32)
    unturned = rotate(grad_fields[:, :, :, 0:2], cosine, -sine)
    grad_raw = jnp.concatenate([unturned, grad_fields[:, :, :, 2:3]], axis=3).astype(jnp.bfloat16)
    return grad_raw.reshape(seqs, rows, width)


def gelu_slope(upper):
    return 0.5 * (1.0 + lax.erf(upper * ROOT_HALF)) + upper * DENSITY * jnp.exp(
        -0.5 * upper * upper
    )


def attend_sequence(fields):
    local_heads = fields.shape[1]
    block = min(512, LEN)
    count = LEN // block
    keys = fields[:, :, 1]
    values = fields[:, :, 2]
    query_blocks = fields[:, :, 0].reshape(count, block, local_heads, HD)

    def attend_one_block(query_blk):
        scores = jnp.einsum(
            "qhd,khd->hqk", query_blk, keys, preferred_element_type=jnp.float32
        ) * HD ** (-0.5)
        top = jnp.max(scores, axis=-1, keepdims=True)
        expo = jnp.exp(scores - top)
        totals = jnp.sum(expo, axis=-1, keepdims=True)
        probs = (expo / totals).astype(jnp.bfloat16)
        result = jnp.einsum("hqk,khd->qhd", probs, values, preferred_element_type=jnp.float32)
        return (result.astype(jnp.bfloat16), (top + jnp.log(totals))[:, :, 0])

    results, logsums = lax.map(attend_one_block, query_blocks)
    logsums = jnp.transpose(logsums, (1, 0, 2)).reshape(local_heads, LEN)
    return (results.reshape(LEN, local_heads, HD), logsums)


def attend_all(packed_heads):
    items = packed_heads.shape[0]
    local_heads = packed_heads.shape[2] // (3 * HD)
    fields = packed_heads.reshape(items, LEN, local_heads, 3, HD)
    results, logsums = lax.map(attend_sequence, fields)
    return (results.reshape(items, LEN, local_heads * HD), logsums)


def back_sequence(pieces):
    fields, logsums, grad_heads = pieces
    local_heads = fields.shape[1]
    block = min(512, LEN)
    count = LEN // block
    keys = fields[:, :, 1]
    values = fields[:, :, 2]
    query_blocks = fields[:, :, 0].reshape(count, block, local_heads, HD)
    grad_blocks = grad_heads.reshape(count, block, local_heads, HD)
    sum_blocks = jnp.transpose(logsums.reshape(local_heads, count, block), (1, 0, 2))

    def back_one_block(carry, piece):
        key_acc, value_acc = carry
        query_blk, grad_blk, sum_blk = piece
        scores = jnp.einsum(
            "qhd,khd->hqk", query_blk, keys, preferred_element_type=jnp.float32
        ) * HD ** (-0.5)
        probs = jnp.exp(scores - sum_blk[:, :, None])
        grad_probs = jnp.einsum(
            "qhd,khd->hqk", grad_blk, values, preferred_element_type=jnp.float32
        )
        inner = jnp.sum(probs * grad_probs, axis=-1, keepdims=True)
        grad_scores = (probs * (grad_probs - inner)).astype(jnp.bfloat16)
        grad_query = jnp.einsum(
            "hqk,khd->qhd", grad_scores, keys, preferred_element_type=jnp.float32
        ) * HD ** (-0.5)
        key_acc = key_acc + jnp.einsum(
            "hqk,qhd->khd", grad_scores, query_blk, preferred_element_type=jnp.float32
        ) * HD ** (-0.5)
        value_acc = value_acc + jnp.einsum(
            "hqk,qhd->khd", probs.astype(jnp.bfloat16), grad_blk, preferred_element_type=jnp.float32
        )
        return ((key_acc, value_acc), grad_query)

    empty = jnp.zeros((LEN, local_heads, HD), jnp.float32)
    (grad_keys, grad_values), grad_queries = lax.scan(
        back_one_block, (empty, empty), (query_blocks, grad_blocks, sum_blocks)
    )
    grad_queries = grad_queries.reshape(LEN, local_heads, HD)
    return jnp.stack([grad_queries, grad_keys, grad_values], axis=2).astype(jnp.bfloat16)


def back_all(packed_heads, logsums, grad_heads):
    items = packed_heads.shape[0]
    local_heads = packed_heads.shape[2] // (3 * HD)
    fields = packed_heads.reshape(items, LEN, local_heads, 3, HD)
    grads = grad_heads.reshape(items, LEN, local_heads, HD)
    result = lax.map(back_sequence, (fields, logsums, grads))
    return result.reshape(items, LEN, local_heads * 3 * HD)


def data_layer(
    tokens, cotangent, w_qkv, w_up, w_out, w_down, scale_one, scale_two, norm_one, inverse_one
):
    seqs, local_len, width = tokens.shape
    wide = (
        lax.all_gather(w_qkv, "seq", axis=1, tiled=True),
        lax.all_gather(w_up, "seq", axis=1, tiled=True),
        lax.all_gather(w_out, "seq", axis=0, tiled=True),
        lax.all_gather(w_down, "seq", axis=0, tiled=True),
    )
    full_qkv, full_up, full_out, full_down = (
        lax.all_gather(wide[0], "dp", axis=0, tiled=True),
        lax.all_gather(wide[1], "dp", axis=0, tiled=True),
        lax.all_gather(wide[2], "dp", axis=1, tiled=True),
        lax.all_gather(wide[3], "dp", axis=1, tiled=True),
    )
    field = tokens.astype(jnp.float32)
    h_one = (norm_one * scale_one).astype(jnp.bfloat16)
    places = (lax.axis_index("seq") * local_len + jnp.arange(local_len, dtype=jnp.int32)).astype(
        jnp.float32
    )
    cosine, sine = rotary_tables(places)
    packed = pack_heads(h_one, full_qkv, cosine, sine)
    packed_heads = lax.all_to_all(packed, "seq", split_axis=2, concat_axis=1, tiled=True)
    results, logsums = attend_all(packed_heads)
    back_tokens = lax.all_to_all(results, "seq", split_axis=1, concat_axis=2, tiled=True)
    middle = field + jnp.einsum(
        "std,de->ste", back_tokens, full_out, preferred_element_type=jnp.float32
    )
    norm_two, inverse_two = normalize(middle)
    h_two = (norm_two * scale_two).astype(jnp.bfloat16)
    upper = jnp.einsum("std,df->stf", h_two, full_up, preferred_element_type=jnp.float32)
    active = jax.nn.gelu(upper, approximate=False).astype(jnp.bfloat16)
    output = (
        middle + jnp.einsum("stf,fd->std", active, full_down, preferred_element_type=jnp.float32)
    ).astype(jnp.bfloat16)
    grad_down = jnp.einsum("stf,std->fd", active, cotangent, preferred_element_type=jnp.float32)
    grad_active = jnp.einsum(
        "std,fd->stf", cotangent, full_down, preferred_element_type=jnp.float32
    )
    grad_upper = (grad_active * gelu_slope(upper)).astype(jnp.bfloat16)
    grad_up = jnp.einsum("std,stf->df", h_two, grad_upper, preferred_element_type=jnp.float32)
    grad_htwo = jnp.einsum("stf,df->std", grad_upper, full_up, preferred_element_type=jnp.float32)
    grad_middle, grad_scale_two = norm_backward(grad_htwo, norm_two, inverse_two, scale_two)
    grad_middle = grad_middle + cotangent.astype(jnp.float32)
    grad_branch = grad_middle.astype(jnp.bfloat16)
    grad_out = jnp.einsum(
        "std,ste->de", back_tokens, grad_branch, preferred_element_type=jnp.float32
    )
    grad_attended = jnp.einsum(
        "ste,de->std", grad_branch, full_out, preferred_element_type=jnp.float32
    ).astype(jnp.bfloat16)
    grad_heads = lax.all_to_all(grad_attended, "seq", split_axis=2, concat_axis=1, tiled=True)
    grad_packed_heads = back_all(packed_heads, logsums, grad_heads)
    grad_packed = lax.all_to_all(grad_packed_heads, "seq", split_axis=1, concat_axis=2, tiled=True)
    grad_raw = unpack_grads(grad_packed, cosine, sine)
    grad_qkv = jnp.einsum("std,ste->de", h_one, grad_raw, preferred_element_type=jnp.float32)
    grad_hone = jnp.einsum("ste,de->std", grad_raw, full_qkv, preferred_element_type=jnp.float32)
    grad_field, grad_scale_one = norm_backward(grad_hone, norm_one, inverse_one, scale_one)
    grad_tokens = (grad_middle + grad_field).astype(jnp.bfloat16)
    partial_sums = (
        lax.psum_scatter(
            grad_qkv.astype(jnp.bfloat16), "dp", scatter_dimension=0, tiled=True
        ).astype(jnp.float32),
        lax.psum_scatter(
            grad_up.astype(jnp.bfloat16), "dp", scatter_dimension=0, tiled=True
        ).astype(jnp.float32),
        lax.psum_scatter(
            grad_out.astype(jnp.bfloat16), "dp", scatter_dimension=1, tiled=True
        ).astype(jnp.float32),
        lax.psum_scatter(
            grad_down.astype(jnp.bfloat16), "dp", scatter_dimension=1, tiled=True
        ).astype(jnp.float32),
    )
    sums = (
        lax.psum_scatter(
            partial_sums[0].astype(jnp.bfloat16), "seq", scatter_dimension=1, tiled=True
        ).astype(jnp.float32),
        lax.psum_scatter(
            partial_sums[1].astype(jnp.bfloat16), "seq", scatter_dimension=1, tiled=True
        ).astype(jnp.float32),
        lax.psum_scatter(
            partial_sums[2].astype(jnp.bfloat16), "seq", scatter_dimension=0, tiled=True
        ).astype(jnp.float32),
        lax.psum_scatter(
            partial_sums[3].astype(jnp.bfloat16), "seq", scatter_dimension=0, tiled=True
        ).astype(jnp.float32),
    )
    return (output, grad_tokens, grad_scale_one, grad_scale_two, sums)


def shards(tokens, bins, plan, w_qkv, w_out, w_up, w_down, w_time, cotangent):
    feats = time_features(plan, bins).astype(jnp.bfloat16)
    full_time = lax.all_gather(w_time, ("dp", "seq"), axis=0, tiled=True)
    modul = jnp.dot(feats, full_time, preferred_element_type=jnp.float32)
    scale_one = 1.0 + modul[:, None, :D]
    scale_two = 1.0 + modul[:, None, D:]
    norm_one, inverse_one = normalize(tokens.astype(jnp.float32))
    output, grad_tokens, grad_scale_one, grad_scale_two, sums = data_layer(
        tokens, cotangent, w_qkv, w_up, w_out, w_down, scale_one, scale_two, norm_one, inverse_one
    )
    grad_scales = jnp.concatenate([grad_scale_one, grad_scale_two], axis=1)
    grad_time = jnp.dot(feats.astype(jnp.float32).T, grad_scales, precision=HIGHEST)
    time_sum = lax.psum_scatter(grad_time, ("dp", "seq"), scatter_dimension=0, tiled=True)
    return (output, grad_tokens, sums[0], sums[2], sums[1], sums[3], time_sum)


BF = jnp.bfloat16
F32 = jnp.float32
MESHID = pl.DeviceIdType.MESH
VMEM_LIMIT = 60 * 1024 * 1024


def mm(a, b):
    return lax.dot_general(a, b, (((1,), (0,)), ((), ())), preferred_element_type=F32)


def mm_nt(a, b):
    return lax.dot_general(a, b, (((1,), (1,)), ((), ())), preferred_element_type=F32)


def mm_tn(a, b):
    return lax.dot_general(a, b, (((0,), (0,)), ((), ())), preferred_element_type=F32)


def peers():
    g = lax.axis_index("dp")
    s = lax.axis_index("seq")
    core = lax.rem(s, 2)
    return g, s, core, s + 1 - 2 * core, lax.rem(s + 2, 4), 3 - s


def remote(src, dst, ss, rs, i, dev):
    return pltpu.make_async_remote_copy(
        src_ref=src,
        dst_ref=dst,
        send_sem=ss.at[i],
        recv_sem=rs.at[i],
        device_id=dev,
        device_id_type=MESHID,
    )


def greet(devices):
    barrier = pltpu.get_barrier_semaphore()
    for dev in devices:
        pl.semaphore_signal(barrier, inc=1, device_id=dev, device_id_type=MESHID)
    pl.semaphore_wait(barrier, len(devices))


def moments(field):
    centered = field - jnp.mean(field, axis=-1, keepdims=True)
    spread = jnp.mean(centered * centered, axis=-1, keepdims=True)
    inverse = lax.rsqrt(spread + EPSILON)
    return centered * inverse, inverse


def ring_place(g):
    z, y = g // 2, lax.rem(g, 2)
    return z + y * (7 - 2 * z)


def ring_index(p):
    p = lax.rem(p + 16, 8)
    return 2 * p + (p // 4) * (15 - 4 * p)


WAYS = (1, -1)


class Gather:
    def __init__(self, own, view, ss, rs, first):
        self.own, self.view, self.ss, self.rs, self.first = own, view, ss, rs, first

    def hop(self, k, way):
        g, s = lax.axis_index("dp"), lax.axis_index("seq")
        p = ring_place(g)
        j = ring_index(p - way * (k - 1))
        half = None if k < 4 else (0 if way > 0 else 1)
        dst = self.view(j, half)
        src = self.own if k == 1 else dst
        i = self.first + 2 * (k - 1) + (way < 0)
        return remote(src, dst, self.ss, self.rs, i, (ring_index(p + way), s))

    def start(self):
        for way in WAYS:
            self.hop(1, way).start()

    def forward(self, k):
        for way in WAYS:
            self.hop(k - 1, way).wait_recv()
            self.hop(k, way).start()

    def arrive(self):
        for way in WAYS:
            self.hop(4, way).wait_recv()

    def drain(self):
        for k in (1, 2, 3, 4):
            for way in WAYS:
                self.hop(k, way).wait_send()


class Scatter:
    def __init__(self, view, halves, wholes, ss, rs, first):
        self.view, self.halves, self.wholes = view, halves, wholes
        self.ss, self.rs, self.first = ss, rs, first

    def hop(self, k, way):
        g, s = lax.axis_index("dp"), lax.axis_index("seq")
        p = ring_place(g)
        side = 0 if way > 0 else 1
        j = ring_index(p + way * (5 - k))
        src = self.view(j, side if k == 1 else None)
        dst = self.halves.at[side] if k == 1 else self.wholes.at[3 * side + k - 2]
        i = self.first + 2 * (k - 1) + side
        return remote(src, dst, self.ss, self.rs, i, (ring_index(p + way), s))

    def start(self):
        for way in WAYS:
            self.hop(1, way).start()

    def forward(self, k):
        p = ring_place(lax.axis_index("dp"))
        for way in WAYS:
            side = 0 if way > 0 else 1
            self.hop(k - 1, way).wait_recv()
            got = self.halves.at[side] if k == 2 else self.wholes.at[3 * side + k - 3]
            mine = self.view(ring_index(p + way * (5 - k)), side if k == 2 else None)
            mine[...] = (mine[...].astype(F32) + got[...].astype(F32)).astype(BF)
            self.hop(k, way).start()

    def result(self):
        for way in WAYS:
            self.hop(4, way).wait_recv()
        mine = self.view(lax.axis_index("dp"), None)
        return mine[...].astype(F32) + (self.wholes[2].astype(F32) + self.wholes[5].astype(F32))

    def drain(self):
        for k in (1, 2, 3, 4):
            for way in WAYS:
                self.hop(k, way).wait_send()


def rows_of(ref, half, size):
    return ref if half is None else ref.at[half * (size // 2) : (half + 1) * (size // 2)]


def k1_body(
    tok, wt, fs, w_qkv, w_out, w_up, w_down, cs, sn, cot,
    tok_all, modul, wq, out_all, up_all, down_all, h_out, qkv, lse, own, attn_all, cot_all,
    tokv, wtime, pbuf, ls, ss, rs, gs, gr, fs_, fr_,
):
    g, s, core, s1, s2, s3 = peers()
    p = ring_place(g)
    greet([(g, s1), (g, s2), (g, s3), (ring_index(p + 1), s), (ring_index(p - 1), s)])
    nb, tl = tok.shape[0], tok.shape[1]
    rows = 4 * tl
    blk = 256
    nq = rows // blk
    heads = own.shape[2] // HD
    nr, nc = w_out.shape[0], w_out.shape[1]

    def lanes(j, size):
        return pl.ds(pl.multiple_of(j * size, size), size)

    def view_out(other):
        def view(j, half):
            lo, size = (0, nr) if half is None else (half * (nr // 2), nr // 2)
            return out_all.at[pl.ds(pl.multiple_of(other * nr + lo, size), size), lanes(j, nc)]

        return view

    def view_down(j, half):
        size = w_down.shape[0]
        lo, n = (0, size) if half is None else (half * (size // 2), size // 2)
        return down_all.at[lo : lo + n, lanes(j, w_down.shape[1])]

    def view_rows(ref, size):
        def view(j, half):
            lo, n = (0, size) if half is None else (half * (size // 2), size // 2)
            return ref.at[pl.ds(pl.multiple_of(j * size + lo, n), n)]

        return view

    def view_time(j, half):
        return wtime.at[j] if half is None else wtime.at[j, :, half * D : (half + 1) * D]

    here = view_out(s)(g, None)
    time_ring = Gather(wt, view_time, gs, gr, 0)
    qkv_ring = Gather(w_qkv, view_rows(wq, w_qkv.shape[0]), gs, gr, 8)
    up_ring = Gather(w_up, view_rows(up_all, w_up.shape[0]), gs, gr, 16)
    down_ring = Gather(w_down, view_down, gs, gr, 24)
    out_ring = Gather(w_out, view_out(s), gs, gr, 32)
    far_ring = Gather(view_out(s2)(g, None), view_out(s2), gs, gr, 40)

    time_ring.start()
    qkv_ring.start()
    pair_out = remote(w_out, here, ss, rs, 0, (g, s2))
    pair_out.start()
    far, near, passed = [], [], []
    for b in range(nb):
        cp = remote(tok.at[b], tokv.at[b, s], ss, rs, 1 + b, (g, s2))
        cp.start()
        far.append(cp)
    for b in range(nb):
        cp = remote(tok.at[b], tokv.at[b, s], ss, rs, 3 + b, (g, s1))
        cp.start()
        near.append(cp)
    local = [
        pltpu.make_async_copy(tok, tokv.at[:, s], ls.at[0]),
        pltpu.make_async_copy(w_qkv, view_rows(wq, w_qkv.shape[0])(g, None), ls.at[1]),
        pltpu.make_async_copy(w_up, view_rows(up_all, w_up.shape[0])(g, None), ls.at[2]),
        pltpu.make_async_copy(w_down, view_down(g, None), ls.at[3]),
        pltpu.make_async_copy(w_out, here, ls.at[4]),
        pltpu.make_async_copy(cot, cot_all.at[:, s], ls.at[5]),
    ]
    for cp in local:
        cp.start()
    wtime[g] = wt[...]
    for k in (2, 3, 4):
        time_ring.forward(k)
        qkv_ring.forward(k)
    up_ring.start()
    time_ring.arrive()
    weights = wtime[...].astype(F32)
    parts = [
        jnp.sum(jnp.sum(weights * fs[b], axis=0), axis=0, keepdims=True) for b in range(nb)
    ]
    pbuf[0] = jnp.concatenate(parts, axis=0)
    small = []
    for e, other in ((1, s1), (2, s2), (3, s3)):
        cp = remote(pbuf.at[0], pbuf.at[e], ss, rs, 4 + e, (g, other))
        cp.start()
        small.append(cp)
    down_ring.start()
    out_ring.start()
    pair_out.wait_recv()
    far_ring.start()
    for b in range(nb):
        far[b].wait_recv()
        cp = remote(tokv.at[b, s2], tokv.at[b, s2], ss, rs, 8 + b, (g, s1))
        cp.start()
        passed.append(cp)
        if b == 0:
            for c in small:
                c.wait_recv()
            modul[...] = (pbuf[0] + pbuf[1]) + (pbuf[2] + pbuf[3])
            qkv_ring.arrive()
            local[0].wait()
            local[1].wait()
    cot_far, cot_near, cot_pass = [], [], []
    for b in range(nb):
        cp = remote(cot.at[b], cot_all.at[b, s], ss, rs, 10 + b, (g, s2))
        cp.start()
        cot_far.append(cp)
    for b in range(nb):
        cp = remote(cot.at[b], cot_all.at[b, s], ss, rs, 12 + b, (g, s1))
        cp.start()
        cot_near.append(cp)
    for cp in near + passed:
        cp.wait_recv()
    keep_tok = pltpu.make_async_copy(tokv, tok_all, ls.at[6])
    keep_tok.start()

    def attn_copy(kind, it):
        b, q = it // nq, lax.rem(it, nq)
        r = pl.ds(pl.multiple_of(q * blk, blk), blk)
        if kind == 2:
            ref = attn_all.at[b, s2, r]
            return remote(ref, ref, fs_.at[2], fr_.at[2], it, (g, s1))
        return remote(
            own.at[b, r], attn_all.at[b, s, r], fs_.at[kind], fr_.at[kind], it, (g, (s2, s1)[kind])
        )

    lane = lax.broadcasted_iota(jnp.int32, (1, 2 * 128), 1)

    def project(b):
        scale = 1.0 + modul[pl.ds(b, 1), :D]

        def one(i, _):
            r = pl.ds(pl.multiple_of(i * blk, blk), blk)
            normed, _inv = moments(tokv[b, i].astype(F32))
            h = (normed * scale).astype(BF)
            h_out[b, r] = h
            raw = mm(h, wq[...])
            c, n = cs[r], sn[r]
            qa, qb = raw[:, :128] * 0.125, raw[:, 128:256] * 0.125
            ka, kb = raw[:, 256:384], raw[:, 384:512]
            qkv[b, 0, r] = jnp.concatenate([qa * c - qb * n, qb * c + qa * n], axis=1).astype(BF)
            qkv[b, 1, r] = jnp.concatenate([ka * c - kb * n, kb * c + ka * n], axis=1).astype(BF)
            qkv[b, 2, r] = raw[:, 512:].astype(BF)
            return 0

        lax.fori_loop(0, nq, one, 0)

    def step(it, _):
        b, q = it // nq, lax.rem(it, nq)

        @pl.when(q == 0)
        def _():
            project(b)

        for when, ring, k in (
            (1, up_ring, 2), (2, down_ring, 2), (2, out_ring, 2), (3, far_ring, 2),
            (4, up_ring, 3), (5, down_ring, 3), (5, out_ring, 3), (6, far_ring, 3),
            (7, up_ring, 4),
        ):

            @pl.when(it == when)
            def _(ring=ring, k=k):
                ring.forward(k)

        r = pl.ds(pl.multiple_of(q * blk, blk), blk)
        query = qkv[b, 0, r]
        keys, values = qkv[b, 1], qkv[b, 2]
        out = jnp.zeros((blk, heads * HD), F32)
        stats = jnp.zeros((blk, 128), F32)
        for h in range(heads):
            mask = lax.rem(lane, 128) // 32 == h
            scores = mm_nt(jnp.where(mask, query, jnp.zeros_like(query)), keys)
            top = jnp.max(scores, axis=1, keepdims=True)
            expo = jnp.exp(scores - top)
            total = jnp.sum(expo, axis=1, keepdims=True)
            res = mm(expo.astype(BF), values) * (1.0 / total)
            out = jnp.where(lane // HD == h, res, out)
            stats = jnp.where(lane[:, :128] == h, top + jnp.log(total), stats)
        own[b, r] = out.astype(BF)
        lse[b, :, r] = stats.T[:8]
        attn_copy(0, it).start()
        attn_copy(1, it).start()
        return 0

    lax.fori_loop(0, nb * nq, step, 0)
    keep = pltpu.make_async_copy(own, attn_all.at[:, s], ls.at[7])
    keep.start()
    for ring in (down_ring, out_ring, far_ring):
        ring.forward(4)
    for b in range(nb):
        cot_far[b].wait_recv()
        cp = remote(cot_all.at[b, s2], cot_all.at[b, s2], ss, rs, 14 + b, (g, s1))
        cp.start()
        cot_pass.append(cp)

    def forward(it, _):
        attn_copy(0, it).wait_recv()
        attn_copy(2, it).start()
        return 0

    lax.fori_loop(0, nb * nq, forward, 0)
    for ring in (up_ring, down_ring, out_ring, far_ring):
        ring.arrive()
    local[4].wait()
    cross = []
    for e, other in ((0, s), (1, s2)):
        ref = out_all.at[pl.ds(pl.multiple_of(other * nr, nr), nr)]
        cp = remote(ref, ref, ss, rs, 16 + e, (g, s1))
        cp.start()
        cross.append(cp)

    def finish(it, _):
        attn_copy(0, it).wait_send()
        attn_copy(1, it).wait()
        attn_copy(2, it).wait()
        return 0

    lax.fori_loop(0, nb * nq, finish, 0)
    for cp in cot_near + cot_pass + cross:
        cp.wait()
    for cp in cot_far + far + near + passed + small + [pair_out]:
        cp.wait_send()
    for ring in (time_ring, qkv_ring, up_ring, down_ring, out_ring, far_ring):
        ring.drain()
    for i in (2, 3, 5):
        local[i].wait()
    keep_tok.wait()
    keep.wait()


def run_k1(nd, tokens, w_time, fs, w_qkv, w_out, w_up, w_down, cs, sn, cot):
    nb, tl, width = tokens.shape
    rows = 4 * tl
    cols = w_qkv.shape[1] // 3
    hidden = w_up.shape[1]
    vm = pl.BlockSpec(memory_space=pltpu.VMEM)
    hb = pl.BlockSpec(memory_space=pl.ANY)
    steps = nb * (rows // 256)
    sds = jax.ShapeDtypeStruct
    dma = pltpu.SemaphoreType.DMA
    return pl.pallas_call(
        k1_body,
        out_shape=(
            sds((nb, 4, tl, width), BF),
            sds((nb, 2 * width), F32),
            sds((width, 3 * cols), BF),
            sds((width, width), BF),
            sds((width, hidden), BF),
            sds((hidden, width), BF),
            sds((nb, rows, width), BF),
            sds((nb, 3, rows, cols), BF),
            sds((nb, 8, rows), F32),
            sds((nb, rows, cols), BF),
            sds((nb, 4, rows, cols), BF),
            sds((nb, 4, tl, width), BF),
        ),
        in_specs=[hb, vm, vm, hb, hb, hb, hb, vm, vm, hb],
        out_specs=(hb, vm, vm, hb, hb, hb, vm, vm, vm, vm, hb, hb),
        scratch_shapes=[
            pltpu.VMEM((nb, 4, tl, width), BF),
            pltpu.VMEM((nd,) + w_time.shape, BF),
            pltpu.VMEM((4, nb, 2 * width), F32),
            dma((8,)),
            dma((18,)),
            dma((18,)),
            dma((48,)),
            dma((48,)),
            dma((3, steps)),
            dma((3, steps)),
        ],
        compiler_params=pltpu.CompilerParams(
            collective_id=0, has_side_effects=True, vmem_limit_bytes=VMEM_LIMIT
        ),
        name="attention_forward",
    )(tokens, w_time, fs, w_qkv, w_out, w_up, w_down, cs, sn, cot)


def k2_body(
    tok, attn, cot, modul, w_out, w_up, w_down,
    grad_down, grad_up, grad_out, d_mid, base, osend, d_heads, dsc,
    act, htwo, dup, mids, pa, pb_, ra, rb, xs, xr, dat, stage,
    ls, ss, rs, gs,
):
    g, s, core, s1, s2, s3 = peers()
    chip = s // 2
    greet([(g, s1), (g, s2), (g, s3)])
    nb, tl = tok.shape[0], tok.shape[2]

    def block(b, owner, slot):
        scale = 1.0 + modul[pl.ds(b, 1), D:]
        r = pl.ds(pl.multiple_of(owner * tl, tl), tl)
        a = jnp.concatenate([attn[b, j, r] for j in range(4)], axis=1)
        mid = tok[b, owner].astype(F32) + mm(a, w_out[...])
        normed, _inv = moments(mid)
        h = (normed * scale).astype(BF)
        upper = mm(h, w_up[...])
        phi = 0.5 * (1.0 + lax.erf(upper * ROOT_HALF))
        active = (upper * phi).astype(BF)
        slope = phi + upper * (DENSITY * jnp.exp(-0.5 * upper * upper))
        d_act = mm_nt(cot[b, owner], w_down[...])
        d_up = (d_act * slope).astype(BF)
        i = b * 4 + owner
        act[i] = active
        htwo[i] = h
        dup[i] = d_up
        return mid, mm_nt(d_up, w_up[...]), mm(active, w_down[...])

    def pair_copies(jp):
        return (
            remote(pa.at[jp], ra.at[jp], ss, rs, jp, (g, s1)),
            remote(pb_.at[jp], rb.at[jp], ss, rs, 4 + jp, (g, s1)),
        )

    def far_copy(b):
        return remote(xs.at[b], xr.at[b], ss, rs, 8 + b, (g, s2))

    def pair(jp, _):
        phase, b = jp // nb, lax.rem(jp, nb)
        where = chip + (1 - phase) * (1 - 2 * chip)
        _mid, dh, out = block(b, 2 * where + 1 - core, jp)
        pa[jp] = dh.astype(BF)
        pb_[jp] = out.astype(BF)
        ca, cb = pair_copies(jp)
        ca.start()
        cb.start()
        mid, dh, out = block(b, 2 * where + core, jp)
        ca.wait_recv()
        cb.wait_recv()
        dh = dh + ra[jp].astype(F32)
        out = out + rb[jp].astype(F32)

        @pl.when(phase == 0)
        def _():
            xs[b] = dh.astype(BF)
            osend[b] = out.astype(BF)
            far_copy(b).start()

        @pl.when(phase == 1)
        def _():
            d_mid[b] = dh
            mids[b] = mid
            base[b] = out + mid

        return 0

    lax.fori_loop(0, 2 * nb, pair, 0)

    def tail(b, _):
        scale = 1.0 + modul[pl.ds(b, 1), D:]
        far_copy(b).wait_recv()
        dh = d_mid[b] + xr[b].astype(F32)
        normed, inverse = moments(mids[b])
        dsc[pl.ds(b, 1)] = jnp.sum(dh * normed, axis=0, keepdims=True)
        dn = dh * scale
        inner = jnp.mean(dn * normed, axis=-1, keepdims=True)
        dm = cot[b, s].astype(F32) + inverse * (
            dn - jnp.mean(dn, axis=-1, keepdims=True) - normed * inner
        )
        d_mid[b] = dm
        branch = dm.astype(BF)
        xs2 = mm_nt(branch, w_out[...]).astype(BF)
        for j in range(4):
            dat[j, b] = xs2[:, j * 256 : (j + 1) * 256]
        return 0

    lax.fori_loop(0, nb, tail, 0)
    copies = []
    for e, other in ((2, s2), (3, s3), (1, s1)):
        cp = remote(dat.at[other], d_heads.at[s], ss, rs, 9 + e, (g, other))
        cp.start()
        copies.append(cp)
    keep = pltpu.make_async_copy(dat.at[s], d_heads.at[s], ls)
    keep.start()

    own_rows = pl.ds(pl.multiple_of(s * tl, tl), tl)
    branch = d_mid[...].astype(BF).reshape(nb * tl, D)
    for j in range(4):
        a = jnp.concatenate([attn[b, j, own_rows] for b in range(nb)], axis=0)
        stage[j] = mm_tn(a, branch).astype(BF)
        pltpu.make_async_copy(stage.at[j], grad_out.at[j], gs.at[j]).start()

    def out_copy(which, i):
        r = pl.ds(pl.multiple_of(i * 256, 256), 256)
        k = 2 * lax.rem(i, 2) + which
        return pltpu.make_async_copy(stage.at[k], (grad_down, grad_up)[which].at[r], gs.at[k])

    def grads(i, _):
        r = pl.ds(pl.multiple_of(i * 256, 256), 256)
        left = act[:, :, r].reshape(4 * nb * tl, 256)
        res = mm_tn(left, cot[...].reshape(4 * nb * tl, D)).astype(BF)
        out_copy(0, i).wait()
        stage[2 * lax.rem(i, 2)] = res
        out_copy(0, i).start()
        left = htwo[:, :, r].reshape(4 * nb * tl, 256)
        res = mm_tn(left, dup[...].reshape(4 * nb * tl, dup.shape[2])).astype(BF)
        out_copy(1, i).wait()
        stage[2 * lax.rem(i, 2) + 1] = res
        out_copy(1, i).start()
        return 0

    lax.fori_loop(0, D // 256, grads, 0)
    for i in range(D // 256 - 2, D // 256):
        out_copy(0, i).wait()
        out_copy(1, i).wait()

    def done(jp, _):
        ca, cb = pair_copies(jp)
        ca.wait_send()
        cb.wait_send()
        return 0

    lax.fori_loop(0, 2 * nb, done, 0)
    for b in range(nb):
        far_copy(b).wait_send()
    for cp in copies:
        cp.wait()
    keep.wait()


def run_k2(tok_all, attn_all, cot_all, modul, w_out, w_up, w_down):
    nb, _, tl, width = tok_all.shape
    hidden = w_up.shape[1]
    cols = attn_all.shape[3]
    vm = pl.BlockSpec(memory_space=pltpu.VMEM)
    hb = pl.BlockSpec(memory_space=pl.ANY)
    sds = jax.ShapeDtypeStruct
    return pl.pallas_call(
        k2_body,
        out_shape=(
            sds((hidden, width), BF),
            sds((width, hidden), BF),
            sds((4, cols, width), BF),
            sds((nb, tl, width), F32),
            sds((nb, tl, width), F32),
            sds((nb, tl, width), BF),
            sds((4, nb, tl, cols), BF),
            sds((nb, width), F32),
        ),
        in_specs=[vm] * 7,
        out_specs=(hb, hb, hb, vm, vm, vm, hb, vm),
        scratch_shapes=[
            pltpu.VMEM((4 * nb, tl, hidden), BF),
            pltpu.VMEM((4 * nb, tl, width), BF),
            pltpu.VMEM((4 * nb, tl, hidden), BF),
            pltpu.VMEM((nb, tl, width), F32),
            pltpu.VMEM((2 * nb, tl, width), BF),
            pltpu.VMEM((2 * nb, tl, width), BF),
            pltpu.VMEM((2 * nb, tl, width), BF),
            pltpu.VMEM((2 * nb, tl, width), BF),
            pltpu.VMEM((nb, tl, width), BF),
            pltpu.VMEM((nb, tl, width), BF),
            pltpu.VMEM((4, nb, tl, cols), BF),
            pltpu.VMEM((4, 256, width), BF),
            pltpu.SemaphoreType.DMA,
            pltpu.SemaphoreType.DMA((13,)),
            pltpu.SemaphoreType.DMA((13,)),
            pltpu.SemaphoreType.DMA((4,)),
        ],
        compiler_params=pltpu.CompilerParams(
            collective_id=1, has_side_effects=True, vmem_limit_bytes=VMEM_LIMIT
        ),
        name="feed_forward",
    )(tok_all, attn_all, cot_all, modul, w_out, w_up, w_down)


def k3_body(
    qkv, lse, own, d_heads, w, h_one, tok, modul, cs, sn, d_mid, base, osend,
    g_down, g_up, g_out, dsc_two, feats,
    output, grad_tok, s_qkv, s_out, s_up, s_down, s_time,
    orecv, dqt, draw, pa, ra, xs, xr, sumh, dhb,
    vd, vu, vo, vq, oa, ob, ox, osum, down_h, down_w, up_h, up_w, out_h, out_w, qkv_h, qkv_w,
    dpart, dall,
    ls, ss, rs, gs, gr,
):
    g, s, core, s1, s2, s3 = peers()
    chip = s // 2
    p = ring_place(g)
    nd = dall.shape[0]
    others = [(lax.rem(g + d, nd), s) for d in range(1, nd)]
    loads = [
        pltpu.make_async_copy(g_down, vd, ls.at[0]),
        pltpu.make_async_copy(g_up, vu, ls.at[1]),
        pltpu.make_async_copy(g_out, oa, ls.at[2]),
    ]
    for cp in loads:
        cp.start()
    greet([(g, s1), (g, s2), (g, s3)] + others)
    nb, tl = tok.shape[0], tok.shape[1]
    rows, cols = own.shape[1], own.shape[2]
    heads = cols // HD
    blk = 256
    nk = rows // blk
    pc = D // nd

    def lanes(j, size):
        return pl.ds(pl.multiple_of(j * size, size), size)

    def view_cols(ref, size):
        def view(j, half):
            lo, n = (0, size) if half is None else (half * (size // 2), size // 2)
            return ref.at[lo : lo + n, lanes(j, pc)]

        return view

    def view_rows(ref):
        def view(j, half):
            lo, n = (0, pc) if half is None else (half * (pc // 2), pc // 2)
            return ref.at[pl.ds(pl.multiple_of(j * pc + lo, n), n)]

        return view

    down_ring = Scatter(view_cols(vd, vd.shape[0]), down_h, down_w, gs, gr, 0)
    up_ring = Scatter(view_rows(vu), up_h, up_w, gs, gr, 8)
    out_ring = Scatter(view_cols(vo, vo.shape[0]), out_h, out_w, gs, gr, 16)
    qkv_ring = Scatter(view_rows(vq), qkv_h, qkv_w, gs, gr, 24)
    loads[0].wait()
    down_ring.start()
    back = []
    for b in range(nb):
        cp = remote(osend.at[b], orecv.at[b], ss, rs, b, (g, s2))
        cp.start()
        back.append(cp)
    loads[2].wait()
    cross = []
    for phase in range(2):
        where = chip if phase else 1 - chip
        cp = remote(oa.at[2 * where + 1 - core], ob.at[phase], ss, rs, 8 + phase, (g, s1))
        cp.start()
        cross.append(cp)
    loads[1].wait()
    up_ring.start()
    over = remote(osum, ox, ss, rs, 10, (g, s2))

    def out_pair():
        for cp in cross:
            cp.wait_recv()
        osum[...] = (oa[2 * (1 - chip) + core].astype(F32) + ob[0].astype(F32)).astype(BF)
        over.start()

    def out_own():
        over.wait_recv()
        vo[...] = (
            (oa[s].astype(F32) + ob[1].astype(F32)) + ox[...].astype(F32)
        ).astype(BF)
        out_ring.start()

    lane = lax.broadcasted_iota(jnp.int32, (1, cols), 1)
    pick = (
        lax.broadcasted_iota(jnp.int32, (8, cols), 1) // HD
        == lax.broadcasted_iota(jnp.int32, (8, cols), 0)
    ).astype(F32)

    def near_copy(b, phase):
        i = 2 * b + phase
        return remote(pa.at[i], ra.at[i], ss, rs, 2 + i, (g, s1))

    def far_copy(b):
        return remote(xs.at[b], xr.at[b], ss, rs, 6 + b, (g, s2))

    def sequence(b, _):
        for j in range(4):
            dhb[j * tl : (j + 1) * tl] = d_heads[j, b]
        query = qkv[b, 0]
        d_out = dhb[...]
        prod = d_out.astype(F32) * own[b].astype(F32)
        delta = lax.dot_general(
            pick, prod, (((1,), (1,)), ((), ())), precision=HIGHEST, preferred_element_type=F32
        )
        dqt[...] = jnp.zeros_like(dqt)

        def keys_block(i, _):
            it = b * nk + i
            for when, act in (
                (1, out_pair),
                (1, lambda: down_ring.forward(2)),
                (2, lambda: up_ring.forward(2)),
                (3, lambda: down_ring.forward(3)),
                (4, lambda: up_ring.forward(3)),
                (5, lambda: down_ring.forward(4)),
                (6, lambda: up_ring.forward(4)),
                (7, out_own),
            ):

                @pl.when(it == when)
                def _(act=act):
                    act()

            r = pl.ds(pl.multiple_of(i * blk, blk), blk)
            keys, values = qkv[b, 1, r], qkv[b, 2, r]
            dk = jnp.zeros((blk, cols), F32)
            dv = jnp.zeros((blk, cols), F32)
            for h in range(heads):
                mask = lax.rem(lane, 128) // 32 == h
                mask_v = lane // HD == h
                km = jnp.where(mask, keys, jnp.zeros_like(keys))
                vmask = jnp.where(mask_v, values, jnp.zeros_like(values))
                probs = jnp.exp(mm_nt(km, query) - lse[b, h : h + 1])
                d_probs = mm_nt(vmask, d_out)
                ds = (probs * (d_probs - delta[h : h + 1])).astype(BF)
                dv = jnp.where(mask_v, mm(probs.astype(BF), d_out), dv)
                dk = jnp.where(mask, mm(ds, query), dk)
                dqt[...] += mm_tn(km, ds)
            c, n = cs[r], sn[r]
            da, db = dk[:, :128], dk[:, 128:]
            draw[b, r, 256:512] = jnp.concatenate([da * c + db * n, db * c - da * n], axis=1).astype(BF)
            draw[b, r, 512:768] = dv.astype(BF)
            return 0

        lax.fori_loop(0, nk, keys_block, 0)
        dq = dqt[...].T * 0.125
        da, db = dq[:, :128], dq[:, 128:]
        c, n = cs[...], sn[...]
        draw[b, :, 0:256] = jnp.concatenate([da * c + db * n, db * c - da * n], axis=1).astype(BF)

        def part(owner):
            r = pl.ds(pl.multiple_of(owner * tl, tl), tl)
            return mm_nt(draw[b, r], w[...])

        for phase in range(2):
            where = chip if phase else 1 - chip
            pa[2 * b + phase] = part(2 * where + 1 - core).astype(BF)
            near_copy(b, phase).start()
            kept = part(2 * where + core)
            near_copy(b, phase).wait_recv()
            kept = kept + ra[2 * b + phase].astype(F32)
            if phase == 0:
                xs[b] = kept.astype(BF)
                far_copy(b).start()
            else:
                sumh[b] = kept
        return 0

    lax.fori_loop(0, nb, sequence, 0)

    def grads(i, _):
        r = pl.ds(pl.multiple_of(i * 256, 256), 256)
        left = h_one[:, :, r].reshape(nb * rows, 256)
        vq[r] = mm_tn(left, draw[...].reshape(nb * rows, 3 * cols)).astype(BF)
        return 0

    lax.fori_loop(0, D // 256, grads, 0)
    qkv_ring.start()
    out_ring.forward(2)
    s_down[...] = down_ring.result()
    s_up[...] = up_ring.result()
    out_ring.forward(3)
    qkv_ring.forward(2)
    for b in range(nb):
        back[b].wait_recv()
        output[b] = (base[b] + orecv[b].astype(F32)).astype(BF)
    out_ring.forward(4)
    qkv_ring.forward(3)

    def tail(b, _):
        scale = 1.0 + modul[pl.ds(b, 1), :D]
        far_copy(b).wait_recv()
        dh = sumh[b] + xr[b].astype(F32)
        normed, inverse = moments(tok[b].astype(F32))
        dpart[0, pl.ds(b, 1), :D] = jnp.sum(dh * normed, axis=0, keepdims=True)
        dn = dh * scale
        inner = jnp.mean(dn * normed, axis=-1, keepdims=True)
        grad_tok[b] = (
            d_mid[b]
            + inverse * (dn - jnp.mean(dn, axis=-1, keepdims=True) - normed * inner)
        ).astype(BF)
        return 0

    lax.fori_loop(0, nb, tail, 0)
    dpart[0, :, D:] = dsc_two[...]
    small = []
    for e, other in ((1, s1), (2, s2), (3, s3)):
        cp = remote(dpart.at[0], dpart.at[e], ss, rs, 10 + e, (g, other))
        cp.start()
        small.append(cp)
    qkv_ring.forward(4)
    for cp in small:
        cp.wait_recv()
    dall[0, :, : 2 * D] = (dpart[0] + dpart[1]) + (dpart[2] + dpart[3])
    dall[0, :, 2 * D :] = feats[...]
    wide = []
    for d in range(1, nd):
        cp = remote(dall.at[0], dall.at[d], ss, rs, 13 + d, others[d - 1])
        cp.start()
        wide.append(cp)
    s_out[...] = out_ring.result()
    s_qkv[...] = qkv_ring.result()
    for cp in wide:
        cp.wait_recv()
    depth = s_time.shape[0]
    place = (4 * g + s) * depth
    hit = (
        lax.broadcasted_iota(jnp.int32, (depth, TF), 1)
        == lax.broadcasted_iota(jnp.int32, (depth, TF), 0) + place
    )
    total = jnp.zeros((depth, 2 * D), F32)
    for d in range(nd):
        for b in range(nb):
            row = dall[d, b : b + 1]
            column = jnp.sum(jnp.where(hit, row[:, 2 * D :], 0.0), axis=1, keepdims=True)
            total = total + column * row[:, : 2 * D]
    s_time[...] = total
    for b in range(nb):
        back[b].wait_send()
        far_copy(b).wait_send()
        for phase in range(2):
            near_copy(b, phase).wait_send()
    for cp in cross + small + wide + [over]:
        cp.wait_send()
    for ring in (down_ring, up_ring, out_ring, qkv_ring):
        ring.drain()


def run_k3(
    nd, qkv, lse, own, d_heads, w, h_one, tokens, modul, cs, sn, d_mid, base, osend,
    g_down, g_up, g_out, dsc_two, feats,
):
    nb, tl, width = tokens.shape
    rows, cols = own.shape[1], own.shape[2]
    hidden = g_up.shape[1]
    pc = width // nd
    vm = pl.BlockSpec(memory_space=pltpu.VMEM)
    hb = pl.BlockSpec(memory_space=pl.ANY)
    sds = jax.ShapeDtypeStruct
    v = pltpu.VMEM
    dma = pltpu.SemaphoreType.DMA
    return pl.pallas_call(
        k3_body,
        out_shape=(
            sds((nb, tl, width), BF),
            sds((nb, tl, width), BF),
            sds((pc, 3 * cols), F32),
            sds((cols, pc), F32),
            sds((pc, hidden), F32),
            sds((hidden, pc), F32),
            sds((TF // (4 * nd), 2 * width), F32),
        ),
        in_specs=[vm] * 12 + [hb, hb, hb, hb, vm, vm],
        out_specs=(vm,) * 7,
        scratch_shapes=[
            v((nb, tl, width), BF),
            v((cols, rows), F32),
            v((nb, rows, 3 * cols), BF),
            v((2 * nb, tl, width), BF),
            v((2 * nb, tl, width), BF),
            v((nb, tl, width), BF),
            v((nb, tl, width), BF),
            v((nb, tl, width), F32),
            v((rows, cols), BF),
            v((hidden, width), BF),
            v((width, hidden), BF),
            v((cols, width), BF),
            v((width, 3 * cols), BF),
            v((4, cols, width), BF),
            v((2, cols, width), BF),
            v((cols, width), BF),
            v((cols, width), BF),
            v((2, hidden // 2, pc), BF),
            v((6, hidden, pc), BF),
            v((2, pc // 2, hidden), BF),
            v((6, pc, hidden), BF),
            v((2, cols // 2, pc), BF),
            v((6, cols, pc), BF),
            v((2, pc // 2, 3 * cols), BF),
            v((6, pc, 3 * cols), BF),
            v((4, nb, 2 * width), F32),
            v((nd, nb, 2 * width + TF), F32),
            dma((3,)),
            dma((21,)),
            dma((21,)),
            dma((32,)),
            dma((32,)),
        ],
        compiler_params=pltpu.CompilerParams(
            collective_id=2, has_side_effects=True, vmem_limit_bytes=VMEM_LIMIT
        ),
        name="attention_backward",
    )(
        qkv, lse, own, d_heads, w, h_one, tokens, modul, cs, sn, d_mid, base, osend,
        g_down, g_up, g_out, dsc_two, feats,
    )


def order_columns(w):
    rows = w.shape[0]
    heads = w.shape[1] // (3 * HD)
    w = w.reshape(rows, heads, 3, HD)
    turned = w[:, :, 0:2].reshape(rows, heads, 2, 2, HD // 2)
    turned = jnp.transpose(turned, (0, 2, 3, 1, 4)).reshape(rows, 2 * heads * HD)
    return jnp.concatenate([turned, w[:, :, 2].reshape(rows, heads * HD)], axis=1)


def restore_columns(w):
    rows = w.shape[0]
    heads = w.shape[1] // (3 * HD)
    turned = w[:, : 2 * heads * HD].reshape(rows, 2, 2, heads, HD // 2)
    turned = jnp.transpose(turned, (0, 3, 1, 2, 4)).reshape(rows, heads, 2, HD)
    values = w[:, 2 * heads * HD :].reshape(rows, heads, 1, HD)
    return jnp.concatenate([turned, values], axis=2).reshape(rows, heads * 3 * HD)


def fast_shards(nd, tokens, bins, plan, w_qkv, w_out, w_up, w_down, w_time, cotangent):
    s = lax.axis_index("seq")
    nb, tl, width = tokens.shape
    rows = 4 * tl
    feats = time_features(plan, bins).astype(BF).astype(F32)
    depth = w_time.shape[0]
    table = feats.reshape(nb, nd, 4, depth)
    fs = lax.dynamic_index_in_dim(table, s, axis=2, keepdims=False)[:, :, :, None]
    half = HD // 2
    inverse = jnp.exp(jnp.arange(half, dtype=F32) * (-math.log(10000.0) / half))
    angle = jnp.arange(rows, dtype=F32)[:, None] * inverse[None, :]
    cs = jnp.tile(jnp.cos(angle), (1, 128 // half))
    sn = jnp.tile(jnp.sin(angle), (1, 128 // half))
    (
        tok_all, modul, full_qkv, full_out, full_up, full_down,
        h_one, qkv, lse, own, attn_all, cot_all,
    ) = run_k1(
        nd, tokens, w_time, fs, order_columns(w_qkv), w_out, w_up, w_down, cs, sn, cotangent
    )
    grad_down, grad_up, grad_out, d_mid, base, osend, d_heads, dsc_two = run_k2(
        tok_all, attn_all, cot_all, modul, full_out, full_up, full_down
    )
    output, grad_tokens, sum_qkv, sum_out, sum_up, sum_down, grad_time = run_k3(
        nd, qkv, lse, own, d_heads, full_qkv, h_one, tokens, modul, cs, sn, d_mid, base, osend,
        grad_down, grad_up, grad_out, dsc_two, feats,
    )
    return (
        output, grad_tokens, restore_columns(sum_qkv), sum_out, sum_up, sum_down, grad_time
    )


def solution(mesh):
    nd, ns = mesh.shape["dp"], mesh.shape["seq"]
    fast = nd == 8 and ns == 4
    return jax.shard_map(
        functools.partial(fast_shards, nd) if fast else shards,
        mesh=mesh,
        in_specs=(
            P("dp", "seq", None),
            P("dp"),
            P(),
            P("dp", "seq"),
            P("seq", "dp"),
            P("dp", "seq"),
            P("seq", "dp"),
            P(("dp", "seq"), None),
            P("dp", "seq", None),
        ),
        out_specs=(
            P("dp", "seq", None),
            P("dp", "seq", None),
            P("dp", "seq"),
            P("seq", "dp"),
            P("dp", "seq"),
            P("seq", "dp"),
            P(("dp", "seq"), None),
        ),
        check_vma=False,
    )
```

```python
import functools
import math

import jax
import jax.numpy as jnp
from jax import lax
from jax.experimental import pallas as pl
from jax.experimental.pallas import tpu as pltpu
from jax.sharding import PartitionSpec as P

D = 1024
HD = 64
TF = 256
LEN = 1024


EPSILON = 1e-05
HIGHEST = lax.Precision.HIGHEST
ROOT_HALF = 0.7071067811865476
DENSITY = 0.3989422804014327


def time_features(plan, bins):
    table = jnp.arange(plan.shape[0], dtype=jnp.int32)
    picked = jnp.where(bins[:, None] == table[None, :], plan[None, :], 0.0)
    sigma = jnp.sum(picked, axis=1)
    level = 0.25 * jnp.log(sigma)
    count = TF // 2
    freqs = jnp.exp(jnp.arange(count, dtype=jnp.float32) * (math.log(1000.0) / count))
    angles = level[:, None] * freqs[None, :]
    return jnp.concatenate([jnp.sin(angles), jnp.cos(angles)], axis=1)


def normalize(field):
    centered = field - jnp.mean(field, axis=-1, keepdims=True)
    spread = jnp.mean(centered * centered, axis=-1, keepdims=True)
    inverse = lax.rsqrt(spread + EPSILON)
    return (centered * inverse, inverse)


def norm_backward(grad_scaled, normed, inverse, scale):
    grad_normed = grad_scaled * scale
    grad_scale = jnp.sum(grad_scaled * normed, axis=1)
    inner = jnp.mean(grad_normed * normed, axis=-1, keepdims=True)
    grad_field = inverse * (
        grad_normed - jnp.mean(grad_normed, axis=-1, keepdims=True) - normed * inner
    )
    return (grad_field, grad_scale)


def rotate(field, cosine, sine):
    half = HD // 2
    first = field[..., :half]
    second = field[..., half:]
    return jnp.concatenate(
        [first * cosine - second * sine, second * cosine + first * sine], axis=-1
    )


def rotary_tables(places):
    half = HD // 2
    inverse = jnp.exp(jnp.arange(half, dtype=jnp.float32) * (-math.log(10000.0) / half))
    angle = places[:, None] * inverse[None, :]
    return (jnp.cos(angle)[:, None, None, :], jnp.sin(angle)[:, None, None, :])


def pack_heads(h_one, qkv_weight, cosine, sine):
    seqs, rows, width = h_one.shape
    raw = jnp.einsum("std,de->ste", h_one, qkv_weight, preferred_element_type=jnp.float32)
    local_heads = qkv_weight.shape[1] // (3 * HD)
    raw = raw.reshape(seqs, rows, local_heads, 3, HD)
    turned = rotate(raw[:, :, :, 0:2], cosine, sine)
    packed = jnp.concatenate([turned, raw[:, :, :, 2:3]], axis=3).astype(jnp.bfloat16)
    return packed.reshape(seqs, rows, local_heads * 3 * HD)


def unpack_grads(grad_packed, cosine, sine):
    seqs, rows, width = grad_packed.shape
    local_heads = width // (3 * HD)
    grad_fields = grad_packed.reshape(seqs, rows, local_heads, 3, HD).astype(jnp.float32)
    unturned = rotate(grad_fields[:, :, :, 0:2], cosine, -sine)
    grad_raw = jnp.concatenate([unturned, grad_fields[:, :, :, 2:3]], axis=3).astype(jnp.bfloat16)
    return grad_raw.reshape(seqs, rows, width)


def gelu_slope(upper):
    return 0.5 * (1.0 + lax.erf(upper * ROOT_HALF)) + upper * DENSITY * jnp.exp(
        -0.5 * upper * upper
    )


def attend_sequence(fields):
    local_heads = fields.shape[1]
    block = min(512, LEN)
    count = LEN // block
    keys = fields[:, :, 1]
    values = fields[:, :, 2]
    query_blocks = fields[:, :, 0].reshape(count, block, local_heads, HD)

    def attend_one_block(query_blk):
        scores = jnp.einsum(
            "qhd,khd->hqk", query_blk, keys, preferred_element_type=jnp.float32
        ) * HD ** (-0.5)
        top = jnp.max(scores, axis=-1, keepdims=True)
        expo = jnp.exp(scores - top)
        totals = jnp.sum(expo, axis=-1, keepdims=True)
        probs = (expo / totals).astype(jnp.bfloat16)
        result = jnp.einsum("hqk,khd->qhd", probs, values, preferred_element_type=jnp.float32)
        return (result.astype(jnp.bfloat16), (top + jnp.log(totals))[:, :, 0])

    results, logsums = lax.map(attend_one_block, query_blocks)
    logsums = jnp.transpose(logsums, (1, 0, 2)).reshape(local_heads, LEN)
    return (results.reshape(LEN, local_heads, HD), logsums)


def attend_all(packed_heads):
    items = packed_heads.shape[0]
    local_heads = packed_heads.shape[2] // (3 * HD)
    fields = packed_heads.reshape(items, LEN, local_heads, 3, HD)
    results, logsums = lax.map(attend_sequence, fields)
    return (results.reshape(items, LEN, local_heads * HD), logsums)


def back_sequence(pieces):
    fields, logsums, grad_heads = pieces
    local_heads = fields.shape[1]
    block = min(512, LEN)
    count = LEN // block
    keys = fields[:, :, 1]
    values = fields[:, :, 2]
    query_blocks = fields[:, :, 0].reshape(count, block, local_heads, HD)
    grad_blocks = grad_heads.reshape(count, block, local_heads, HD)
    sum_blocks = jnp.transpose(logsums.reshape(local_heads, count, block), (1, 0, 2))

    def back_one_block(carry, piece):
        key_acc, value_acc = carry
        query_blk, grad_blk, sum_blk = piece
        scores = jnp.einsum(
            "qhd,khd->hqk", query_blk, keys, preferred_element_type=jnp.float32
        ) * HD ** (-0.5)
        probs = jnp.exp(scores - sum_blk[:, :, None])
        grad_probs = jnp.einsum(
            "qhd,khd->hqk", grad_blk, values, preferred_element_type=jnp.float32
        )
        inner = jnp.sum(probs * grad_probs, axis=-1, keepdims=True)
        grad_scores = (probs * (grad_probs - inner)).astype(jnp.bfloat16)
        grad_query = jnp.einsum(
            "hqk,khd->qhd", grad_scores, keys, preferred_element_type=jnp.float32
        ) * HD ** (-0.5)
        key_acc = key_acc + jnp.einsum(
            "hqk,qhd->khd", grad_scores, query_blk, preferred_element_type=jnp.float32
        ) * HD ** (-0.5)
        value_acc = value_acc + jnp.einsum(
            "hqk,qhd->khd", probs.astype(jnp.bfloat16), grad_blk, preferred_element_type=jnp.float32
        )
        return ((key_acc, value_acc), grad_query)

    empty = jnp.zeros((LEN, local_heads, HD), jnp.float32)
    (grad_keys, grad_values), grad_queries = lax.scan(
        back_one_block, (empty, empty), (query_blocks, grad_blocks, sum_blocks)
    )
    grad_queries = grad_queries.reshape(LEN, local_heads, HD)
    return jnp.stack([grad_queries, grad_keys, grad_values], axis=2).astype(jnp.bfloat16)


def back_all(packed_heads, logsums, grad_heads):
    items = packed_heads.shape[0]
    local_heads = packed_heads.shape[2] // (3 * HD)
    fields = packed_heads.reshape(items, LEN, local_heads, 3, HD)
    grads = grad_heads.reshape(items, LEN, local_heads, HD)
    result = lax.map(back_sequence, (fields, logsums, grads))
    return result.reshape(items, LEN, local_heads * 3 * HD)


def data_layer(
    tokens, cotangent, w_qkv, w_up, w_out, w_down, scale_one, scale_two, norm_one, inverse_one
):
    seqs, local_len, width = tokens.shape
    wide = (
        lax.all_gather(w_qkv, "seq", axis=1, tiled=True),
        lax.all_gather(w_up, "seq", axis=1, tiled=True),
        lax.all_gather(w_out, "seq", axis=0, tiled=True),
        lax.all_gather(w_down, "seq", axis=0, tiled=True),
    )
    full_qkv, full_up, full_out, full_down = (
        lax.all_gather(wide[0], "dp", axis=0, tiled=True),
        lax.all_gather(wide[1], "dp", axis=0, tiled=True),
        lax.all_gather(wide[2], "dp", axis=1, tiled=True),
        lax.all_gather(wide[3], "dp", axis=1, tiled=True),
    )
    field = tokens.astype(jnp.float32)
    h_one = (norm_one * scale_one).astype(jnp.bfloat16)
    places = (lax.axis_index("seq") * local_len + jnp.arange(local_len, dtype=jnp.int32)).astype(
        jnp.float32
    )
    cosine, sine = rotary_tables(places)
    packed = pack_heads(h_one, full_qkv, cosine, sine)
    packed_heads = lax.all_to_all(packed, "seq", split_axis=2, concat_axis=1, tiled=True)
    results, logsums = attend_all(packed_heads)
    back_tokens = lax.all_to_all(results, "seq", split_axis=1, concat_axis=2, tiled=True)
    middle = field + jnp.einsum(
        "std,de->ste", back_tokens, full_out, preferred_element_type=jnp.float32
    )
    norm_two, inverse_two = normalize(middle)
    h_two = (norm_two * scale_two).astype(jnp.bfloat16)
    upper = jnp.einsum("std,df->stf", h_two, full_up, preferred_element_type=jnp.float32)
    active = jax.nn.gelu(upper, approximate=False).astype(jnp.bfloat16)
    output = (
        middle + jnp.einsum("stf,fd->std", active, full_down, preferred_element_type=jnp.float32)
    ).astype(jnp.bfloat16)
    grad_down = jnp.einsum("stf,std->fd", active, cotangent, preferred_element_type=jnp.float32)
    grad_active = jnp.einsum(
        "std,fd->stf", cotangent, full_down, preferred_element_type=jnp.float32
    )
    grad_upper = (grad_active * gelu_slope(upper)).astype(jnp.bfloat16)
    grad_up = jnp.einsum("std,stf->df", h_two, grad_upper, preferred_element_type=jnp.float32)
    grad_htwo = jnp.einsum("stf,df->std", grad_upper, full_up, preferred_element_type=jnp.float32)
    grad_middle, grad_scale_two = norm_backward(grad_htwo, norm_two, inverse_two, scale_two)
    grad_middle = grad_middle + cotangent.astype(jnp.float32)
    grad_branch = grad_middle.astype(jnp.bfloat16)
    grad_out = jnp.einsum(
        "std,ste->de", back_tokens, grad_branch, preferred_element_type=jnp.float32
    )
    grad_attended = jnp.einsum(
        "ste,de->std", grad_branch, full_out, preferred_element_type=jnp.float32
    ).astype(jnp.bfloat16)
    grad_heads = lax.all_to_all(grad_attended, "seq", split_axis=2, concat_axis=1, tiled=True)
    grad_packed_heads = back_all(packed_heads, logsums, grad_heads)
    grad_packed = lax.all_to_all(grad_packed_heads, "seq", split_axis=1, concat_axis=2, tiled=True)
    grad_raw = unpack_grads(grad_packed, cosine, sine)
    grad_qkv = jnp.einsum("std,ste->de", h_one, grad_raw, preferred_element_type=jnp.float32)
    grad_hone = jnp.einsum("ste,de->std", grad_raw, full_qkv, preferred_element_type=jnp.float32)
    grad_field, grad_scale_one = norm_backward(grad_hone, norm_one, inverse_one, scale_one)
    grad_tokens = (grad_middle + grad_field).astype(jnp.bfloat16)
    partial_sums = (
        lax.psum_scatter(
            grad_qkv.astype(jnp.bfloat16), "dp", scatter_dimension=0, tiled=True
        ).astype(jnp.float32),
        lax.psum_scatter(
            grad_up.astype(jnp.bfloat16), "dp", scatter_dimension=0, tiled=True
        ).astype(jnp.float32),
        lax.psum_scatter(
            grad_out.astype(jnp.bfloat16), "dp", scatter_dimension=1, tiled=True
        ).astype(jnp.float32),
        lax.psum_scatter(
            grad_down.astype(jnp.bfloat16), "dp", scatter_dimension=1, tiled=True
        ).astype(jnp.float32),
    )
    sums = (
        lax.psum_scatter(
            partial_sums[0].astype(jnp.bfloat16), "seq", scatter_dimension=1, tiled=True
        ).astype(jnp.float32),
        lax.psum_scatter(
            partial_sums[1].astype(jnp.bfloat16), "seq", scatter_dimension=1, tiled=True
        ).astype(jnp.float32),
        lax.psum_scatter(
            partial_sums[2].astype(jnp.bfloat16), "seq", scatter_dimension=0, tiled=True
        ).astype(jnp.float32),
        lax.psum_scatter(
            partial_sums[3].astype(jnp.bfloat16), "seq", scatter_dimension=0, tiled=True
        ).astype(jnp.float32),
    )
    return (output, grad_tokens, grad_scale_one, grad_scale_two, sums)


def shards(tokens, bins, plan, w_qkv, w_out, w_up, w_down, w_time, cotangent):
    feats = time_features(plan, bins).astype(jnp.bfloat16)
    full_time = lax.all_gather(w_time, ("dp", "seq"), axis=0, tiled=True)
    modul = jnp.dot(feats, full_time, preferred_element_type=jnp.float32)
    scale_one = 1.0 + modul[:, None, :D]
    scale_two = 1.0 + modul[:, None, D:]
    norm_one, inverse_one = normalize(tokens.astype(jnp.float32))
    output, grad_tokens, grad_scale_one, grad_scale_two, sums = data_layer(
        tokens, cotangent, w_qkv, w_up, w_out, w_down, scale_one, scale_two, norm_one, inverse_one
    )
    grad_scales = jnp.concatenate([grad_scale_one, grad_scale_two], axis=1)
    grad_time = jnp.dot(feats.astype(jnp.float32).T, grad_scales, precision=HIGHEST)
    time_sum = lax.psum_scatter(grad_time, ("dp", "seq"), scatter_dimension=0, tiled=True)
    return (output, grad_tokens, sums[0], sums[2], sums[1], sums[3], time_sum)


BF = jnp.bfloat16
F32 = jnp.float32
MESHID = pl.DeviceIdType.MESH
QUERY_SCALE = HD**-0.5 / math.log(2.0)
VMEM_LIMIT = 60 * 1024 * 1024


def mm(a, b):
    return lax.dot_general(a, b, (((1,), (0,)), ((), ())), preferred_element_type=F32)


def mm_nt(a, b):
    return lax.dot_general(a, b, (((1,), (1,)), ((), ())), preferred_element_type=F32)


def mm_tn(a, b):
    return lax.dot_general(a, b, (((0,), (0,)), ((), ())), preferred_element_type=F32)


def peers():
    g = lax.axis_index("dp")
    s = lax.axis_index("seq")
    core = lax.rem(s, 2)
    return g, s, core, s + 1 - 2 * core, lax.rem(s + 2, 4), 3 - s


def remote(src, dst, ss, rs, i, dev):
    return pltpu.make_async_remote_copy(
        src_ref=src,
        dst_ref=dst,
        send_sem=ss.at[i],
        recv_sem=rs.at[i],
        device_id=dev,
        device_id_type=MESHID,
    )


def greet(devices):
    barrier = pltpu.get_barrier_semaphore()
    for dev in devices:
        pl.semaphore_signal(barrier, inc=1, device_id=dev, device_id_type=MESHID)
    pl.semaphore_wait(barrier, len(devices))


def moments(field):
    centered = field - jnp.mean(field, axis=-1, keepdims=True)
    spread = jnp.mean(centered * centered, axis=-1, keepdims=True)
    inverse = lax.rsqrt(spread + EPSILON)
    return centered * inverse, inverse


def ring_place(g):
    z, y = g // 2, lax.rem(g, 2)
    return z + y * (7 - 2 * z)


def ring_index(p):
    p = lax.rem(p + 16, 8)
    return 2 * p + (p // 4) * (15 - 4 * p)


WAYS = (1, -1)


class Gather:
    def __init__(self, own, view, ss, rs, first):
        self.own, self.view, self.ss, self.rs, self.first = own, view, ss, rs, first

    def hop(self, k, way):
        g, s = lax.axis_index("dp"), lax.axis_index("seq")
        p = ring_place(g)
        j = ring_index(p - way * (k - 1))
        half = None if k < 4 else (0 if way > 0 else 1)
        dst = self.view(j, half)
        src = self.own if k == 1 else dst
        i = self.first + 2 * (k - 1) + (way < 0)
        return remote(src, dst, self.ss, self.rs, i, (ring_index(p + way), s))

    def start(self):
        for way in WAYS:
            self.hop(1, way).start()

    def forward(self, k):
        for way in WAYS:
            self.hop(k - 1, way).wait_recv()
            self.hop(k, way).start()

    def arrive(self):
        for way in WAYS:
            self.hop(4, way).wait_recv()

    def drain(self):
        for k in (1, 2, 3, 4):
            for way in WAYS:
                self.hop(k, way).wait_send()


class Scatter:
    def __init__(self, view, halves, wholes, ss, rs, first):
        self.view, self.halves, self.wholes = view, halves, wholes
        self.ss, self.rs, self.first = ss, rs, first

    def hop(self, k, way):
        g, s = lax.axis_index("dp"), lax.axis_index("seq")
        p = ring_place(g)
        side = 0 if way > 0 else 1
        j = ring_index(p + way * (5 - k))
        src = self.view(j, side if k == 1 else None)
        dst = self.halves.at[side] if k == 1 else self.wholes.at[3 * side + k - 2]
        i = self.first + 2 * (k - 1) + side
        return remote(src, dst, self.ss, self.rs, i, (ring_index(p + way), s))

    def start(self):
        for way in WAYS:
            self.hop(1, way).start()

    def forward(self, k):
        p = ring_place(lax.axis_index("dp"))
        for way in WAYS:
            side = 0 if way > 0 else 1
            self.hop(k - 1, way).wait_recv()
            got = self.halves.at[side] if k == 2 else self.wholes.at[3 * side + k - 3]
            mine = self.view(ring_index(p + way * (5 - k)), side if k == 2 else None)
            mine[...] = (mine[...].astype(F32) + got[...].astype(F32)).astype(BF)
            self.hop(k, way).start()

    def result(self):
        for way in WAYS:
            self.hop(4, way).wait_recv()
        mine = self.view(lax.axis_index("dp"), None)
        return mine[...].astype(F32) + (self.wholes[2].astype(F32) + self.wholes[5].astype(F32))

    def drain(self):
        for k in (1, 2, 3, 4):
            for way in WAYS:
                self.hop(k, way).wait_send()


def rows_of(ref, half, size):
    return ref if half is None else ref.at[half * (size // 2) : (half + 1) * (size // 2)]


def k1_body(
    tok, wt, fs, w_qkv, w_out, w_up, w_down, cs, sn, cot,
    modul, wq_out, out_all, up_all, down_all, n_out, qkv_out, lse, attn_heads, attn_rows, cot_all,
    act_out, slope_out, htwo_out, mid_out,
    tokv, wtime, pbuf, vt, cotv, wq, nv, qkv, attn, outv, upv, act, slope, htwo, mids, csv, snv,
    ks, ls, ss, rs, gs, gr, fs_, fr_, os_,
):
    g, s, core, s1, s2, s3 = peers()
    p = ring_place(g)
    nb, tl = tok.shape[0], tok.shape[1]
    rows = 4 * tl
    blk = 256
    nq = rows // blk
    heads = attn.shape[3] // HD
    nr, nc = w_out.shape[0], w_out.shape[1]

    def lanes(j, size):
        return pl.ds(pl.multiple_of(j * size, size), size)

    def view_out(other):
        def view(j, half):
            lo, size = (0, nr) if half is None else (half * (nr // 2), nr // 2)
            return outv.at[pl.ds(pl.multiple_of(other * nr + lo, size), size), lanes(j, nc)]

        return view

    def view_down(j, half):
        size = w_down.shape[0]
        lo, n = (0, size) if half is None else (half * (size // 2), size // 2)
        return down_all.at[lo : lo + n, lanes(j, w_down.shape[1])]

    def view_rows(ref, size):
        def view(j, half):
            lo, n = (0, size) if half is None else (half * (size // 2), size // 2)
            return ref.at[pl.ds(pl.multiple_of(j * size + lo, n), n)]

        return view

    def view_time(j, half):
        return wtime.at[j] if half is None else wtime.at[j, :, half * D : (half + 1) * D]

    def view_qkv(side):
        size = w_qkv.shape[0]

        def view(j, half):
            lo, n = (0, size // 2) if half is None else (half * (size // 4), size // 4)
            at = pl.multiple_of(j * size + side * (size // 2) + lo, n)
            return wq.at[pl.ds(at, n)]

        return view

    here = view_out(s)(g, None)
    time_ring = Gather(wt, view_time, gs, gr, 0)
    part = w_qkv.shape[0] // 2
    qkv_rings = [
        Gather(w_qkv.at[i * part : (i + 1) * part], view_qkv(i), gs, gr, 8 + 40 * i)
        for i in range(2)
    ]
    up_ring = Gather(w_up, view_rows(upv, w_up.shape[0]), gs, gr, 16)
    down_ring = Gather(w_down, view_down, gs, gr, 24)
    out_ring = Gather(w_out, view_out(s), gs, gr, 32)
    far_ring = Gather(view_out(s2)(g, None), view_out(s2), gs, gr, 40)

    local = [
        pltpu.make_async_copy(tok, tokv.at[:, s], ls.at[0]),
        pltpu.make_async_copy(w_qkv, view_rows(wq, w_qkv.shape[0])(g, None), ls.at[1]),
        pltpu.make_async_copy(w_up, view_rows(upv, w_up.shape[0])(g, None), ls.at[2]),
        pltpu.make_async_copy(w_down, view_down(g, None), ls.at[3]),
        pltpu.make_async_copy(w_out, here, ls.at[4]),
        pltpu.make_async_copy(cot, cotv, ls.at[5]),
        pltpu.make_async_copy(cs, csv, ls.at[6]),
        pltpu.make_async_copy(sn, snv, ls.at[7]),
    ]
    greet([(g, s1), (g, s2), (g, s3), (ring_index(p + 1), s), (ring_index(p - 1), s)])
    time_ring.start()
    for ring in qkv_rings:
        ring.start()
    out_ring.start()
    pair_out = remote(w_out, here, ss, rs, 0, (g, s2))
    pair_out.start()
    far = [remote(tok.at[b], tokv.at[b, s], ss, rs, 1 + b, (g, s2)) for b in range(nb)]
    near = []
    far[0].start()
    for b in range(nb):
        cp = remote(tok.at[b], tokv.at[b, s], ss, rs, 3 + b, (g, s1))
        cp.start()
        near.append(cp)
    for cp in local:
        cp.start()
    wtime[g] = wt[...]
    half_rows = tl // 2

    def cot_piece(k):
        r = slice((k % 2) * half_rows, (k % 2 + 1) * half_rows)
        return remote(
            cotv.at[k // 2, r], cot_all.at[k // 2, s, r], ss, rs, 18 + k, (g, s2)
        )

    local[5].wait()
    cot_far = [cot_piece(k) for k in range(2 * nb)]
    cot_far[0].start()
    for k in (2, 3, 4):
        time_ring.forward(k)
        for ring in qkv_rings:
            ring.forward(k)
        out_ring.forward(k)
    pair_out.wait_recv()
    far_ring.start()
    up_ring.start()
    time_ring.arrive()
    weights = wtime[...].astype(F32)
    parts = [
        jnp.sum(jnp.sum(weights * fs[b], axis=0), axis=0, keepdims=True) for b in range(nb)
    ]
    pbuf[0] = jnp.concatenate(parts, axis=0)
    small = []
    for e, other in ((1, s1), (2, s2), (3, s3)):
        cp = remote(pbuf.at[0], pbuf.at[e], ss, rs, 4 + e, (g, other))
        cp.start()
        small.append(cp)
    far[1].start()
    cot_far[1].start()
    passed = [
        remote(tokv.at[b, s2], tokv.at[b, s2], ss, rs, 8 + b, (g, s1)) for b in range(nb)
    ]
    cot_near = [remote(cotv.at[b], cot_all.at[b, s], ss, rs, 12 + b, (g, s1)) for b in range(nb)]
    cot_pass = [
        remote(cot_all.at[b, s2], cot_all.at[b, s2], ss, rs, 14 + b, (g, s1)) for b in range(nb)
    ]
    far[0].wait_recv()
    passed[0].start()
    for c in small:
        c.wait_recv()
    modul[...] = (pbuf[0] + pbuf[1]) + (pbuf[2] + pbuf[3])
    for ring in qkv_rings:
        ring.arrive()
    for i in (0, 1, 6, 7):
        local[i].wait()
    keep_w = pltpu.make_async_copy(wq, wq_out, ls.at[8])
    keep_w.start()
    keep_cot = pltpu.make_async_copy(cotv, cot_all.at[:, s], ls.at[9])
    keep_cot.start()

    def attn_copy(kind, it):
        b, q = it // nq, lax.rem(it, nq)
        r = pl.ds(pl.multiple_of(q * blk, blk), blk)
        ref = attn.at[b, s2 if kind == 2 else s, r]
        return remote(ref, ref, fs_.at[kind], fr_.at[kind], it, (g, s2 if kind == 0 else s1))

    lane = lax.broadcasted_iota(jnp.int32, (1, 2 * 128), 1)

    def keep_fields(b):
        return (
            pltpu.make_async_copy(nv.at[b], n_out.at[b], ks.at[0, b]),
            pltpu.make_async_copy(qkv.at[b], qkv_out.at[b], ks.at[1, b]),
        )

    def project(b):
        scale = 1.0 + modul[pl.ds(b, 1), :D]

        def one(i, _):
            r = pl.ds(pl.multiple_of(i * blk, blk), blk)
            normed, _inv = moments(tokv[b, i].astype(F32))
            nv[b, r] = normed.astype(BF)
            raw = mm((normed * scale).astype(BF), wq[...])
            c, n = csv[r], snv[r]
            qa, qb = raw[:, :128] * QUERY_SCALE, raw[:, 128:256] * QUERY_SCALE
            ka, kb = raw[:, 256:384], raw[:, 384:512]
            qkv[b, 0, r] = jnp.concatenate([qa * c - qb * n, qb * c + qa * n], axis=1).astype(BF)
            qkv[b, 1, r] = jnp.concatenate([ka * c - kb * n, kb * c + ka * n], axis=1).astype(BF)
            qkv[b, 2, r] = raw[:, 512:].astype(BF)
            return 0

        lax.fori_loop(0, nq, one, 0)

    def pass_attn(lo, hi):
        def forward(it, _):
            attn_copy(0, it).wait_recv()
            attn_copy(2, it).start()
            return 0

        lax.fori_loop(lo, hi, forward, 0)

    def arrive_attn(lo, hi):
        def forward(it, _):
            attn_copy(1, it).wait_recv()
            attn_copy(2, it).wait_recv()
            return 0

        lax.fori_loop(lo, hi, forward, 0)

    def tokens_of(b):
        near[b].wait_recv()
        passed[b].wait_recv()

    def second_tokens():
        far[1].wait_recv()
        passed[1].start()

    def step(it, _):
        b, q = it // nq, lax.rem(it, nq)
        for i in range(nb):

            @pl.when(it == i * nq)
            def _(i=i):
                tokens_of(i)

        @pl.when(q == 0)
        def _():
            project(b)
            vt[...] = qkv[b, 2].T
            for cp in keep_fields(b):
                cp.start()

        for when, action in (
            (1, lambda: up_ring.forward(2)),
            (1, lambda: far_ring.forward(2)),
            (2, second_tokens),
            (3, lambda: up_ring.forward(3)),
            (3, lambda: far_ring.forward(3)),
            (4, lambda: up_ring.forward(4)),
            (4, down_ring.start),
            (5, lambda: far_ring.forward(4)),
            (6, lambda: pass_attn(0, nq)),
        ):

            @pl.when(it == when)
            def _(action=action):
                action()

        r = pl.ds(pl.multiple_of(q * blk, blk), blk)
        query, keys = qkv[b, 0, r], qkv[b, 1]
        outs, stats = [], []
        for h in range(heads):
            mask = lax.rem(lane, 128) // 32 == h
            scores = mm_nt(keys, jnp.where(mask, query, jnp.zeros_like(query)))
            top = jnp.max(scores, axis=0, keepdims=True)
            expo = jnp.exp2(scores - top)
            total = jnp.sum(expo, axis=0, keepdims=True)
            outs.append(mm(vt[h * HD : (h + 1) * HD], expo.astype(BF)) * (1.0 / total))
            stats.append(top + jnp.log2(total))
        attn[b, s, r] = jnp.concatenate(outs, axis=0).T.astype(BF)
        lse[b, :, r] = jnp.concatenate(stats + [jnp.zeros((8 - heads, blk), F32)], axis=0)
        attn_copy(0, it).start()
        attn_copy(1, it).start()
        return 0

    lax.fori_loop(0, nb * nq, step, 0)
    for cp in cot_far[2:] + cot_near:
        cp.start()
    keep = pltpu.make_async_copy(attn.at[:, s], attn_heads, ls.at[10])
    keep.start()
    out_ring.arrive()
    far_ring.arrive()
    local[4].wait()
    cross = []
    for e, other in ((0, s), (1, s2)):
        ref = outv.at[pl.ds(pl.multiple_of(other * nr, nr), nr)]
        cp = remote(ref, ref, ss, rs, 16 + e, (g, s1))
        cp.start()
        cross.append(cp)
    up_ring.arrive()
    local[2].wait()
    for cp in cross:
        cp.wait_recv()
    arrive_attn(0, nq)
    keep_out = pltpu.make_async_copy(outv, out_all, ls.at[11])
    keep_out.start()
    keep_up = pltpu.make_async_copy(upv, up_all, ls.at[12])
    keep_up.start()

    def keep_block(i):
        return (
            pltpu.make_async_copy(act.at[i], act_out.at[i], os_.at[0, i]),
            pltpu.make_async_copy(slope.at[i], slope_out.at[i], os_.at[1, i]),
            pltpu.make_async_copy(htwo.at[i], htwo_out.at[i], os_.at[2, i]),
        )

    def feed(i, _):
        b, owner = i // 4, lax.rem(i, 4)
        for when, action in (
            (1, lambda: down_ring.forward(2)),
            (3, lambda: pass_attn(nq, 2 * nq)),
            (3, lambda: down_ring.forward(3)),
            (4, lambda: arrive_attn(nq, 2 * nq)),
            (6, lambda: down_ring.forward(4)),
        ):

            @pl.when(i == when)
            def _(action=action):
                action()

        scale = 1.0 + modul[pl.ds(b, 1), D:]
        r = pl.ds(pl.multiple_of(owner * tl, tl), tl)
        joined = jnp.concatenate([attn[b, j, r] for j in range(4)], axis=1)
        mid = tokv[b, owner].astype(F32) + mm(joined, outv[...])
        normed, _inv = moments(mid)
        h = (normed * scale).astype(BF)
        upper = mm(h, upv[...])
        phi = 0.5 * (1.0 + lax.erf(upper * ROOT_HALF))
        act[i] = (upper * phi).astype(BF)
        slope[i] = (phi + upper * (DENSITY * jnp.exp(-0.5 * upper * upper))).astype(BF)
        htwo[i] = h

        @pl.when(owner == s)
        def _():
            mids[b] = mid

        for cp in keep_block(i):
            cp.start()
        return 0

    lax.fori_loop(0, 4 * nb, feed, 0)
    keep_mid = pltpu.make_async_copy(mids, mid_out, ls.at[13])
    keep_mid.start()
    own_rows = pl.ds(pl.multiple_of(s * tl, tl), tl)
    keep_rows = pltpu.make_async_copy(attn.at[:, :, own_rows], attn_rows, ls.at[14])
    keep_rows.start()
    for b in range(nb):
        cot_far[2 * b].wait_recv()
        cot_far[2 * b + 1].wait_recv()
        cot_pass[b].start()

    def finish(it, _):
        attn_copy(0, it).wait_send()
        attn_copy(1, it).wait_send()
        attn_copy(2, it).wait_send()
        return 0

    lax.fori_loop(0, nb * nq, finish, 0)

    def kept(i, _):
        for cp in keep_block(i):
            cp.wait()
        return 0

    lax.fori_loop(0, 4 * nb, kept, 0)
    down_ring.arrive()
    for cp in cot_near + cot_pass:
        cp.wait()
    for cp in cot_far + far + near + passed + small + cross + [pair_out]:
        cp.wait_send()
    for ring in [time_ring, up_ring, down_ring, out_ring, far_ring] + qkv_rings:
        ring.drain()
    local[3].wait()
    for cp in (keep_cot, keep, keep_w, keep_out, keep_up, keep_mid, keep_rows):
        cp.wait()
    for b in range(nb):
        for cp in keep_fields(b):
            cp.wait()


def run_k1(nd, tokens, w_time, fs, w_qkv, w_out, w_up, w_down, cs, sn, cot):
    nb, tl, width = tokens.shape
    rows = 4 * tl
    cols = w_qkv.shape[1] // 3
    hidden = w_up.shape[1]
    vm = pl.BlockSpec(memory_space=pltpu.VMEM)
    hb = pl.BlockSpec(memory_space=pl.ANY)
    steps = nb * (rows // 256)
    sds = jax.ShapeDtypeStruct
    dma = pltpu.SemaphoreType.DMA
    v = pltpu.VMEM
    return pl.pallas_call(
        k1_body,
        out_shape=(
            sds((nb, 2 * width), F32),
            sds((width, 3 * cols), BF),
            sds((width, width), BF),
            sds((width, hidden), BF),
            sds((hidden, width), BF),
            sds((nb, rows, width), BF),
            sds((nb, 3, rows, cols), BF),
            sds((nb, 8, rows), F32),
            sds((nb, rows, cols), BF),
            sds((nb, 4, tl, cols), BF),
            sds((nb, 4, tl, width), BF),
            sds((4 * nb, tl, hidden), BF),
            sds((4 * nb, tl, hidden), BF),
            sds((4 * nb, tl, width), BF),
            sds((nb, tl, width), F32),
        ),
        in_specs=[hb, vm, vm, hb, vm, vm, vm, hb, hb, hb],
        out_specs=(vm, hb, hb, hb, hb, hb, hb, vm) + (hb,) * 7,
        scratch_shapes=[
            v((nb, 4, tl, width), BF),
            v((nd,) + w_time.shape, BF),
            v((4, nb, 2 * width), F32),
            v((cols, rows), BF),
            v((nb, tl, width), BF),
            v((width, 3 * cols), BF),
            v((nb, rows, width), BF),
            v((nb, 3, rows, cols), BF),
            v((nb, 4, rows, cols), BF),
            v((width, width), BF),
            v((width, hidden), BF),
            v((4 * nb, tl, hidden), BF),
            v((4 * nb, tl, hidden), BF),
            v((4 * nb, tl, width), BF),
            v((nb, tl, width), F32),
            v(cs.shape, F32),
            v(sn.shape, F32),
            dma((2, nb)),
            dma((15,)),
            dma((22,)),
            dma((22,)),
            dma((56,)),
            dma((56,)),
            dma((3, steps)),
            dma((3, steps)),
            dma((3, 4 * nb)),
        ],
        compiler_params=pltpu.CompilerParams(
            collective_id=0, has_side_effects=True, vmem_limit_bytes=VMEM_LIMIT
        ),
        name="attention_forward",
    )(tokens, w_time, fs, w_qkv, w_out, w_up, w_down, cs, sn, cot)


def k2_body(
    act_h, slope_h, htwo_h, mid_h, attn_h, cot_h, modul, w_out_h, w_up_h, w_down_h,
    grad_up, grad_out, d_mid_h, base_h, osend_h, d_heads, dsc, s_down,
    act, dup, htwo, mids, attn, cot, w_out, w_up, w_down, d_mid, base, osend,
    pa, pb_, ra, rb, xs, xr, dat, stage, gdv, down_h, down_w,
    ls, ss, rs, os_, ins, keeps, bs, gs, gr,
):
    g, s, core, s1, s2, s3 = peers()
    p = ring_place(g)
    chip = s // 2
    nb, tl = cot.shape[0], cot.shape[2]

    def pull(jp, which):
        phase, b = jp // nb, lax.rem(jp, nb)
        where = chip + (1 - phase) * (1 - 2 * chip)
        owner = 2 * where + (1 - core if which == 0 else core)
        i = b * 4 + owner
        k = 2 * jp + which
        return (
            pltpu.make_async_copy(cot_h.at[b, owner], cot.at[b, owner], bs.at[0, k]),
            pltpu.make_async_copy(slope_h.at[i], dup.at[i], bs.at[1, k]),
            pltpu.make_async_copy(act_h.at[i], act.at[i], bs.at[2, k]),
        )

    loads = []
    for i, (src, dst) in enumerate(
        (
            (w_down_h, w_down), (w_up_h, w_up),
            (mid_h, mids), (w_out_h, w_out), (htwo_h, htwo), (attn_h, attn),
        )
    ):
        loads.append(pltpu.make_async_copy(src, dst, ins.at[i]))
    first = pull(0, 0)
    loads[0].start()
    for cp in first:
        cp.start()
    loads[1].start()
    for jp in range(2 * nb):
        for which in (0, 1):
            if jp + which:
                for cp in pull(jp, which):
                    cp.start()
    for cp in loads[2:]:
        cp.start()
    greet([(g, s1), (g, s2), (g, s3), (ring_index(p + 1), s), (ring_index(p - 1), s)])
    hidden = act.shape[2]
    pc = s_down.shape[1]

    def view_down(j, half):
        lo, n = (0, hidden) if half is None else (half * (hidden // 2), hidden // 2)
        return gdv.at[lo : lo + n, pl.ds(pl.multiple_of(j * pc, pc), pc)]

    down_ring = Scatter(view_down, down_h, down_w, gs, gr, 0)

    def block(b, owner):
        i = b * 4 + owner
        d_act = mm_nt(cot[b, owner], w_down[...])
        d_up = (d_act * dup[i].astype(F32)).astype(BF)
        dup[i] = d_up
        return mm_nt(d_up, w_up[...]), mm(act[i], w_down[...])

    def pair_copies(jp):
        return (
            remote(pa.at[jp], ra.at[jp], ss, rs, jp, (g, s1)),
            remote(pb_.at[jp], rb.at[jp], ss, rs, 4 + jp, (g, s1)),
        )

    def far_copy(b):
        return remote(xs.at[b], xr.at[b], ss, rs, 8 + b, (g, s2))

    def place(jp):
        phase, b = jp // nb, lax.rem(jp, nb)
        return phase, b, chip + (1 - phase) * (1 - 2 * chip)

    def give(jp, _):
        phase, b, where = place(jp)

        @pl.when(phase == 0)
        def _():
            for cp in pull(jp, 0):
                cp.wait()

        dh, out = block(b, 2 * where + 1 - core)
        pa[jp] = dh.astype(BF)
        pb_[jp] = out.astype(BF)
        for cp in pair_copies(jp):
            cp.start()
        return 0

    def take(jp, _):
        phase, b, where = place(jp)

        @pl.when(phase == 0)
        def _():
            for cp in pull(jp, 1):
                cp.wait()

        dh, out = block(b, 2 * where + core)
        for cp in pair_copies(jp):
            cp.wait_recv()
        dh = dh + ra[jp].astype(F32)
        out = out + rb[jp].astype(F32)

        @pl.when(phase == 0)
        def _():
            xs[b] = dh.astype(BF)
            osend[b] = out.astype(BF)
            far_copy(b).start()

        @pl.when(phase == 1)
        def _():
            d_mid[b] = dh
            base[b] = out + mids[b]

        return 0

    def down_grads(i, _):
        r = pl.ds(pl.multiple_of(i * 256, 256), 256)
        left = act[:, :, r].reshape(4 * nb * tl, 256)
        gdv[r] = mm_tn(left, cot[...].reshape(4 * nb * tl, D)).astype(BF)
        return 0

    def up_copy(i):
        r = pl.ds(pl.multiple_of(i * 256, 256), 256)
        return pltpu.make_async_copy(stage.at[i], grad_up.at[r], os_.at[i])

    def up_grads(i, _):
        r = pl.ds(pl.multiple_of(i * 256, 256), 256)
        left = htwo[:, :, r].reshape(4 * nb * tl, 256)
        stage[i] = mm_tn(left, dup[...].reshape(4 * nb * tl, hidden)).astype(BF)
        up_copy(i).start()
        return 0

    def spread(e, other, b):
        return remote(dat.at[other, b], d_heads.at[s, b], ss, rs, 10 + 2 * e + b, (g, other))

    def tail(b, _):
        scale = 1.0 + modul[pl.ds(b, 1), D:]
        far_copy(b).wait_recv()
        dh = d_mid[b] + xr[b].astype(F32)
        normed, inverse = moments(mids[b])
        dsc[pl.ds(b, 1)] = jnp.sum(dh * normed, axis=0, keepdims=True)
        dn = dh * scale
        inner = jnp.mean(dn * normed, axis=-1, keepdims=True)
        dm = cot[b, s].astype(F32) + inverse * (
            dn - jnp.mean(dn, axis=-1, keepdims=True) - normed * inner
        )
        d_mid[b] = dm
        branch = mm_nt(dm.astype(BF), w_out[...]).astype(BF)
        for j in range(4):
            dat[j, b] = branch[:, j * 256 : (j + 1) * 256]
        for e, other in ((0, s2), (1, s3), (2, s1)):
            spread(e, other, b).start()
        return 0

    for cp in loads[:2]:
        cp.wait()
    half = D // 512
    lax.fori_loop(0, nb, give, 0)
    lax.fori_loop(0, nb, take, 0)
    for jp in range(nb, 2 * nb):
        for which in (0, 1):
            for cp in pull(jp, which):
                cp.wait()
    lax.fori_loop(0, hidden // 256, down_grads, 0)
    down_ring.start()
    for cp in loads[2:]:
        cp.wait()
    lax.fori_loop(nb, 2 * nb, give, 0)
    lax.fori_loop(nb, 2 * nb, take, 0)
    down_ring.forward(2)
    lax.fori_loop(0, nb - 1, tail, 0)
    lax.fori_loop(0, half, up_grads, 0)
    down_ring.forward(3)
    lax.fori_loop(nb - 1, nb, tail, 0)
    lax.fori_loop(half, 2 * half, up_grads, 0)
    keep_all = []
    for i, (src, dst) in enumerate(
        ((d_mid, d_mid_h), (base, base_h), (osend, osend_h), (dat.at[s], d_heads.at[s]))
    ):
        cp = pltpu.make_async_copy(src, dst, keeps.at[i])
        cp.start()
        keep_all.append(cp)
    down_ring.forward(4)
    branch = d_mid[...].astype(BF).reshape(nb * tl, D)
    for j in range(4):
        left = jnp.concatenate([attn[b, j] for b in range(nb)], axis=0)
        up_copy(j).wait()
        stage[j] = mm_tn(left, branch).astype(BF)
        pltpu.make_async_copy(stage.at[j], grad_out.at[j], os_.at[j]).start()

    def done(jp, _):
        ca, cb = pair_copies(jp)
        ca.wait_send()
        cb.wait_send()
        return 0

    lax.fori_loop(0, 2 * nb, done, 0)
    s_down[...] = down_ring.result()
    down_ring.drain()
    for b in range(nb):
        far_copy(b).wait_send()
        for e, other in ((0, s2), (1, s3), (2, s1)):
            spread(e, other, b).wait()
    for j in range(4):
        pltpu.make_async_copy(stage.at[j], grad_out.at[j], os_.at[j]).wait()
    for cp in keep_all:
        cp.wait()


def run_k2(nd, act, slope, htwo, mid, attn_rows, cot_all, modul, w_out, w_up, w_down):
    nb, _, tl, width = cot_all.shape
    hidden = w_up.shape[1]
    cols = attn_rows.shape[3]
    pc = width // nd
    vm = pl.BlockSpec(memory_space=pltpu.VMEM)
    hb = pl.BlockSpec(memory_space=pl.ANY)
    sds = jax.ShapeDtypeStruct
    v = pltpu.VMEM
    dma = pltpu.SemaphoreType.DMA
    return pl.pallas_call(
        k2_body,
        out_shape=(
            sds((width, hidden), BF),
            sds((4, cols, width), BF),
            sds((nb, tl, width), F32),
            sds((nb, tl, width), F32),
            sds((nb, tl, width), BF),
            sds((4, nb, tl, cols), BF),
            sds((nb, width), F32),
            sds((hidden, pc), F32),
        ),
        in_specs=[hb, hb, hb, hb, hb, hb, vm, hb, hb, hb],
        out_specs=(hb, hb, hb, hb, hb, hb, vm, vm),
        scratch_shapes=[
            v(act.shape, BF),
            v(slope.shape, BF),
            v(htwo.shape, BF),
            v(mid.shape, F32),
            v(attn_rows.shape, BF),
            v(cot_all.shape, BF),
            v(w_out.shape, BF),
            v(w_up.shape, BF),
            v(w_down.shape, BF),
            v((nb, tl, width), F32),
            v((nb, tl, width), F32),
            v((nb, tl, width), BF),
            v((2 * nb, tl, width), BF),
            v((2 * nb, tl, width), BF),
            v((2 * nb, tl, width), BF),
            v((2 * nb, tl, width), BF),
            v((nb, tl, width), BF),
            v((nb, tl, width), BF),
            v((4, nb, tl, cols), BF),
            v((4, 256, width), BF),
            v((hidden, width), BF),
            v((2, hidden // 2, pc), BF),
            v((6, hidden, pc), BF),
            dma,
            dma((16,)),
            dma((16,)),
            dma((4,)),
            dma((6,)),
            dma((4,)),
            dma((3, 4 * nb)),
            dma((8,)),
            dma((8,)),
        ],
        compiler_params=pltpu.CompilerParams(
            collective_id=1, has_side_effects=True, vmem_limit_bytes=VMEM_LIMIT
        ),
        name="feed_forward",
    )(act, slope, htwo, mid, attn_rows, cot_all, modul, w_out, w_up, w_down)


def k3_body(
    fields_h, lse, attn_h, d_heads_h, w_h, normed_h, tok_h, modul, cs_h, sn_h, d_mid_h, base_h, osend,
    g_up, g_out, dsc_two, feats,
    output, grad_tok, s_qkv, s_out, s_up, s_time,
    orecv, dqt, draw, pa, ra, xs, xr, sumh, dhb,
    vu, vo, vq, oa, ob, ox, osum, up_h, up_w, out_h, out_w, qkv_h, qkv_w,
    dpart, tx, dall, qkv, own, d_heads, w, normed_one, tok, cs, sn, d_mid, base,
    ins, ls, ss, rs, gs, gr,
):
    g, s, core, s1, s2, s3 = peers()
    chip = s // 2
    p = ring_place(g)
    nd = dall.shape[0]
    loads = [
        pltpu.make_async_copy(g_up, vu, ls.at[0]),
        pltpu.make_async_copy(g_out, oa, ls.at[1]),
    ]
    pulls = []
    for i, (src, dst) in enumerate(
        (
            (fields_h, qkv), (attn_h, own), (d_heads_h, d_heads), (cs_h, cs), (sn_h, sn),
            (w_h, w), (normed_h, normed_one), (tok_h, tok), (d_mid_h, d_mid), (base_h, base),
        )
    ):
        pulls.append(pltpu.make_async_copy(src, dst, ins.at[i]))
    for cp in pulls[:3]:
        cp.start()
    for cp in loads:
        cp.start()
    for cp in pulls[3:]:
        cp.start()
    greet([(g, s1), (g, s2), (ring_index(p + 1), s), (ring_index(p - 1), s)])
    nb, tl = tok.shape[0], tok.shape[1]
    rows, cols = own.shape[1], own.shape[2]
    heads = cols // HD
    blk = 256
    nk = rows // blk
    pc = D // nd

    def lanes(j, size):
        return pl.ds(pl.multiple_of(j * size, size), size)

    def view_cols(ref, size):
        def view(j, half):
            lo, n = (0, size) if half is None else (half * (size // 2), size // 2)
            return ref.at[lo : lo + n, lanes(j, pc)]

        return view

    def view_rows(ref):
        def view(j, half):
            lo, n = (0, pc) if half is None else (half * (pc // 2), pc // 2)
            return ref.at[pl.ds(pl.multiple_of(j * pc + lo, n), n)]

        return view

    up_ring = Scatter(view_rows(vu), up_h, up_w, gs, gr, 16)
    def view_time(j, half):
        wide = (2 * D + TF) // 2
        ref = dall.at[j]
        return ref if half is None else ref.at[:, half * wide : (half + 1) * wide]

    out_rings = [
        Scatter(view_cols(vo.at[i], vo.shape[1]), out_h.at[i], out_w.at[i], gs, gr, 8 * i)
        for i in range(2)
    ]
    time_ring = Gather(dall.at[g], view_time, gs, gr, 32)
    def view_qkv(side):
        wide = vq.shape[1] // 2

        def view(j, half):
            lo, n = (0, pc) if half is None else (half * (pc // 2), pc // 2)
            return vq.at[
                pl.ds(pl.multiple_of(j * pc + lo, n), n), side * wide : (side + 1) * wide
            ]

        return view

    qkv_rings = [
        Scatter(view_qkv(i), qkv_h.at[i], qkv_w.at[i], gs, gr, 24 + 16 * i) for i in range(2)
    ]

    def qkv_forward(k):
        for ring in qkv_rings:
            ring.forward(k)

    loads[0].wait()
    up_ring.start()
    back = []
    for b in range(nb):
        cp = remote(osend.at[b], orecv.at[b], ss, rs, b, (g, s2))
        cp.start()
        back.append(cp)
    loads[1].wait()
    cross = []
    for i in range(2):
        cp = remote(oa.at[2 * i + 1 - core], ob.at[i], ss, rs, 8 + i, (g, s1))
        cp.start()
        cross.append(cp)
    over = remote(osum, ox, ss, rs, 10, (g, s2))

    def out_pair():
        for i in range(2):
            cross[i].wait_recv()
            vo[i] = (oa[2 * i + core].astype(F32) + ob[i].astype(F32)).astype(BF)
            out_rings[i].start()

    def out_forward(k):
        for ring in out_rings:
            ring.forward(k)

    lane = lax.broadcasted_iota(jnp.int32, (1, cols), 1)

    def near_copy(b, phase):
        i = 2 * b + phase
        return remote(pa.at[i], ra.at[i], ss, rs, 2 + i, (g, s1))

    def far_copy(b):
        return remote(xs.at[b], xr.at[b], ss, rs, 6 + b, (g, s2))

    for cp in pulls[:5]:
        cp.wait()
    out_pair()

    def grads(side):
        wide = vq.shape[1] // 2
        c = slice(side * wide, (side + 1) * wide)

        def one(i, _):
            r = pl.ds(pl.multiple_of(i * 256, 256), 256)
            left = jnp.concatenate(
                [
                    (normed_one[b, :, r].astype(F32) * (1.0 + modul[b : b + 1, r])).astype(BF)
                    for b in range(nb)
                ],
                axis=0,
            )
            vq[r, c] = mm_tn(left, draw[:, :, c].reshape(nb * rows, wide)).astype(BF)
            return 0

        lax.fori_loop(0, D // 256, one, 0)
        qkv_rings[side].start()

    def sequence(b, _):
        for j in range(4):
            dhb[j * tl : (j + 1) * tl] = d_heads[j, b]
        query = qkv[b, 0]
        d_out = dhb[...]
        prod = d_out.astype(F32) * own[b].astype(F32)
        prod = prod.T
        delta = jnp.concatenate(
            [jnp.sum(prod[h * HD : (h + 1) * HD], axis=0, keepdims=True) for h in range(heads)],
            axis=0,
        )
        dqt[...] = jnp.zeros_like(dqt)

        def keys_block(i, _):
            it = b * nk + i
            for when, act in (
                (1, lambda: up_ring.forward(2)),
                (2, lambda: out_forward(2)),
                (3, lambda: up_ring.forward(3)),
                (4, lambda: out_forward(3)),
                (5, lambda: up_ring.forward(4)),
                (6, lambda: out_forward(4)),
            ):

                @pl.when(it == when)
                def _(act=act):
                    act()

            r = pl.ds(pl.multiple_of(i * blk, blk), blk)
            keys, values = qkv[b, 1, r], qkv[b, 2, r]
            dk = jnp.zeros((blk, cols), F32)
            dv = jnp.zeros((blk, cols), F32)
            for h in range(heads):
                mask = lax.rem(lane, 128) // 32 == h
                mask_v = lane // HD == h
                km = jnp.where(mask, keys, jnp.zeros_like(keys))
                vmask = jnp.where(mask_v, values, jnp.zeros_like(values))
                probs = jnp.exp2(mm_nt(km, query) - lse[b, h : h + 1])
                d_probs = mm_nt(vmask, d_out)
                ds = (probs * (d_probs - delta[h : h + 1])).astype(BF)
                dv = jnp.where(mask_v, mm(probs.astype(BF), d_out), dv)
                dk = jnp.where(mask, mm(ds, query), dk)
                dqt[...] += mm_tn(km, ds)
            c, n = cs[r] * math.log(2.0), sn[r] * math.log(2.0)
            da, db = dk[:, :128], dk[:, 128:]
            draw[b, r, 256:512] = jnp.concatenate([da * c + db * n, db * c - da * n], axis=1).astype(BF)
            draw[b, r, 512:768] = dv.astype(BF)
            return 0

        lax.fori_loop(0, nk, keys_block, 0)
        dq = dqt[...].T * 0.125
        da, db = dq[:, :128], dq[:, 128:]
        c, n = cs[...], sn[...]
        draw[b, :, 0:256] = jnp.concatenate([da * c + db * n, db * c - da * n], axis=1).astype(BF)

        @pl.when(b == 0)
        def _():
            for cp in pulls[5:]:
                cp.wait()
            dpart[0, :, :D] = jnp.zeros((nb, D), F32)

        def part(owner):
            r = pl.ds(pl.multiple_of(owner * tl, tl), tl)
            res = mm_nt(draw[b, r], w[...])
            dpart[0, pl.ds(b, 1), :D] += jnp.sum(
                res * normed_one[b, r].astype(F32), axis=0, keepdims=True
            )
            return res

        @pl.when(b == nb - 1)
        def _():
            grads(0)
            grads(1)

        for phase in range(2):
            where = chip if phase else 1 - chip
            pa[2 * b + phase] = part(2 * where + 1 - core).astype(BF)
            near_copy(b, phase).start()
        for phase in range(2):
            where = chip if phase else 1 - chip
            kept = part(2 * where + core)
            near_copy(b, phase).wait_recv()
            kept = kept + ra[2 * b + phase].astype(F32)
            if phase == 0:
                xs[b] = kept.astype(BF)
                far_copy(b).start()
            else:
                sumh[b] = kept
        return 0

    lax.fori_loop(0, nb, sequence, 0)
    dpart[0, :, D:] = dsc_two[...]
    small = [remote(dpart.at[0], dpart.at[1], ss, rs, 11, (g, s1))]
    small[0].start()
    first_out, second_out = out_rings[0].result(), out_rings[1].result()
    osum[...] = jnp.where(chip == 0, second_out, first_out).astype(BF)
    own_out = jnp.where(chip == 0, first_out, second_out)
    over.start()
    qkv_forward(2)
    small[0].wait_recv()
    dall[g, :, : 2 * D] = dpart[0] + dpart[1]
    dall[g, :, 2 * D :] = feats[...]
    time_ring.start()
    for b in range(nb):
        back[b].wait_recv()
        output[b] = (base[b] + orecv[b].astype(F32)).astype(BF)
    s_up[...] = up_ring.result()
    qkv_forward(3)
    time_ring.forward(2)

    def tail(b, _):
        scale = 1.0 + modul[pl.ds(b, 1), :D]
        far_copy(b).wait_recv()
        normed, inverse = moments(tok[b].astype(F32))
        dn = (sumh[b] + xr[b].astype(F32)) * scale
        inner = jnp.mean(dn * normed, axis=-1, keepdims=True)
        grad_tok[b] = (
            d_mid[b]
            + inverse * (dn - jnp.mean(dn, axis=-1, keepdims=True) - normed * inner)
        ).astype(BF)
        return 0

    lax.fori_loop(0, nb - 1, tail, 0)
    qkv_forward(4)
    time_ring.forward(3)
    time_ring.forward(4)
    lax.fori_loop(nb - 1, nb, tail, 0)
    over.wait_recv()
    s_out[...] = own_out + ox[...].astype(F32)
    time_ring.arrive()
    depth = s_time.shape[0]
    lane_t = lax.broadcasted_iota(jnp.int32, (depth, TF), 1)
    row_t = lax.broadcasted_iota(jnp.int32, (depth, TF), 0)
    mine = jnp.zeros((depth, 2 * D), F32)
    theirs = jnp.zeros((depth, 2 * D), F32)
    for d in range(nd):
        for b in range(nb):
            row = dall[d, b : b + 1]
            for which, other in ((0, s), (1, s2)):
                hit = lane_t == row_t + (4 * g + other) * depth
                column = jnp.sum(jnp.where(hit, row[:, 2 * D :], 0.0), axis=1, keepdims=True)
                if which:
                    theirs = theirs + column * row[:, : 2 * D]
                else:
                    mine = mine + column * row[:, : 2 * D]
    tx[0] = theirs
    swap = remote(tx.at[0], tx.at[1], ss, rs, 12, (g, s2))
    swap.start()
    s_qkv[...] = jnp.concatenate([ring.result() for ring in qkv_rings], axis=1)
    swap.wait_recv()
    s_time[...] = mine + tx[1]
    for b in range(nb):
        back[b].wait_send()
        far_copy(b).wait_send()
        for phase in range(2):
            near_copy(b, phase).wait_send()
    for cp in cross + small + [over, swap]:
        cp.wait_send()
    for ring in out_rings + qkv_rings + [up_ring, time_ring]:
        ring.drain()


def run_k3(
    nd, qkv, lse, attn_heads, d_heads, w, normed, tokens, modul, cs, sn, d_mid, base, osend,
    g_up, g_out, dsc_two, feats,
):
    nb, tl, width = tokens.shape
    rows, cols = attn_heads.shape[1], attn_heads.shape[2]
    hidden = g_up.shape[1]
    pc = width // nd
    vm = pl.BlockSpec(memory_space=pltpu.VMEM)
    hb = pl.BlockSpec(memory_space=pl.ANY)
    sds = jax.ShapeDtypeStruct
    v = pltpu.VMEM
    dma = pltpu.SemaphoreType.DMA
    return pl.pallas_call(
        k3_body,
        out_shape=(
            sds((nb, tl, width), BF),
            sds((nb, tl, width), BF),
            sds((pc, 3 * cols), F32),
            sds((cols, pc), F32),
            sds((pc, hidden), F32),
            sds((TF // (4 * nd), 2 * width), F32),
        ),
        in_specs=[hb, vm, hb, hb, hb, hb, hb, vm, hb, hb, hb, hb, hb, hb, hb, vm, vm],
        out_specs=(vm,) * 6,
        scratch_shapes=[
            v((nb, tl, width), BF),
            v((cols, rows), F32),
            v((nb, rows, 3 * cols), BF),
            v((2 * nb, tl, width), BF),
            v((2 * nb, tl, width), BF),
            v((nb, tl, width), BF),
            v((nb, tl, width), BF),
            v((nb, tl, width), F32),
            v((rows, cols), BF),
            v((width, hidden), BF),
            v((2, cols, width), BF),
            v((width, 3 * cols), BF),
            v((4, cols, width), BF),
            v((2, cols, width), BF),
            v((cols, pc), BF),
            v((cols, pc), BF),
            v((2, pc // 2, hidden), BF),
            v((6, pc, hidden), BF),
            v((2, 2, cols // 2, pc), BF),
            v((2, 6, cols, pc), BF),
            v((2, 2, pc // 2, 3 * cols // 2), BF),
            v((2, 6, pc, 3 * cols // 2), BF),
            v((2, nb, 2 * width), F32),
            v((2, TF // (4 * nd), 2 * width), F32),
            v((nd, nb, 2 * width + TF), F32),
            v(qkv.shape, BF),
            v((nb, rows, cols), BF),
            v(d_heads.shape, BF),
            v(w.shape, BF),
            v(normed.shape, BF),
            v(tokens.shape, BF),
            v(cs.shape, F32),
            v(sn.shape, F32),
            v(d_mid.shape, F32),
            v(base.shape, F32),
            dma((10,)),
            dma((2,)),
            dma((13,)),
            dma((13,)),
            dma((48,)),
            dma((48,)),
        ],
        compiler_params=pltpu.CompilerParams(
            collective_id=2, has_side_effects=True, vmem_limit_bytes=VMEM_LIMIT
        ),
        name="attention_backward",
    )(
        qkv, lse, attn_heads, d_heads, w, normed, tokens, modul, cs, sn, d_mid, base, osend,
        g_up, g_out, dsc_two, feats,
    )


def k4_body(*refs):
    count = len(refs) // 2
    for i in range(count):
        if i != 2:
            refs[count + i][...] = refs[i][...]
    w = refs[2][...]
    heads = w.shape[1] // (3 * HD)
    half, size = HD // 2, heads * HD
    pieces = []
    for h in range(heads):
        for part in (0, 1):
            for side in (0, 1):
                at = part * size + side * (size // 2) + h * half
                pieces.append(w[:, at : at + half])
        at = 2 * size + h * HD
        pieces.append(w[:, at : at + HD])
    refs[count + 2][...] = jnp.concatenate(pieces, axis=1)


def run_k4(arrays):
    vm = pl.BlockSpec(memory_space=pltpu.VMEM)
    return pl.pallas_call(
        k4_body,
        out_shape=tuple(jax.ShapeDtypeStruct(a.shape, a.dtype) for a in arrays),
        in_specs=[vm] * len(arrays),
        out_specs=(vm,) * len(arrays),
        compiler_params=pltpu.CompilerParams(vmem_limit_bytes=VMEM_LIMIT),
        name="results",
    )(*arrays)


def order_columns(w):
    rows = w.shape[0]
    heads = w.shape[1] // (3 * HD)
    w = w.reshape(rows, heads, 3, HD)
    turned = w[:, :, 0:2].reshape(rows, heads, 2, 2, HD // 2)
    turned = jnp.transpose(turned, (0, 2, 3, 1, 4)).reshape(rows, 2 * heads * HD)
    return jnp.concatenate([turned, w[:, :, 2].reshape(rows, heads * HD)], axis=1)


def fast_shards(nd, tokens, bins, plan, w_qkv, w_out, w_up, w_down, w_time, cotangent):
    s = lax.axis_index("seq")
    nb, tl, width = tokens.shape
    rows = 4 * tl
    feats = time_features(plan, bins).astype(BF).astype(F32)
    depth = w_time.shape[0]
    table = feats.reshape(nb, nd, 4, depth)
    fs = lax.dynamic_index_in_dim(table, s, axis=2, keepdims=False)[:, :, :, None]
    half = HD // 2
    inverse = jnp.exp(jnp.arange(half, dtype=F32) * (-math.log(10000.0) / half))
    angle = jnp.arange(rows, dtype=F32)[:, None] * inverse[None, :]
    cs = jnp.tile(jnp.cos(angle), (1, 128 // half))
    sn = jnp.tile(jnp.sin(angle), (1, 128 // half))
    (
        modul, full_qkv, full_out, full_up, full_down, normed, qkv, lse, attn_heads, attn_rows,
        cot_all, act, slope, htwo, mid,
    ) = run_k1(
        nd, tokens, w_time, fs, order_columns(w_qkv), w_out, w_up, w_down, cs, sn, cotangent
    )
    grad_up, grad_out, d_mid, base, osend, d_heads, dsc_two, sum_down = run_k2(
        nd, act, slope, htwo, mid, attn_rows, cot_all, modul, full_out, full_up, full_down
    )
    output, grad_tokens, sum_qkv, sum_out, sum_up, grad_time = run_k3(
        nd, qkv, lse, attn_heads, d_heads, full_qkv, normed, tokens, modul, cs, sn, d_mid, base,
        osend, grad_up, grad_out, dsc_two, feats,
    )
    return tuple(
        run_k4((output, grad_tokens, sum_qkv, sum_out, sum_up, sum_down, grad_time))
    )


def solution(mesh):
    nd, ns = mesh.shape["dp"], mesh.shape["seq"]
    fast = nd == 8 and ns == 4
    return jax.shard_map(
        functools.partial(fast_shards, nd) if fast else shards,
        mesh=mesh,
        in_specs=(
            P("dp", "seq", None),
            P("dp"),
            P(),
            P("dp", "seq"),
            P("seq", "dp"),
            P("dp", "seq"),
            P("seq", "dp"),
            P(("dp", "seq"), None),
            P("dp", "seq", None),
        ),
        out_specs=(
            P("dp", "seq", None),
            P("dp", "seq", None),
            P("dp", "seq"),
            P("seq", "dp"),
            P("dp", "seq"),
            P("seq", "dp"),
            P(("dp", "seq"), None),
        ),
        check_vma=False,
    )
```

```python
import functools
import math

import jax
import jax.numpy as jnp
import numpy as np
from jax import lax
from jax.experimental import pallas as pl
from jax.experimental.pallas import tpu as pltpu
from jax.sharding import PartitionSpec as P

D = 1024
HD = 64
TF = 256
LEN = 1024


EPSILON = 1e-05
HIGHEST = lax.Precision.HIGHEST
ROOT_HALF = 0.7071067811865476
DENSITY = 0.3989422804014327


def time_features(plan, bins):
    table = jnp.arange(plan.shape[0], dtype=jnp.int32)
    picked = jnp.where(bins[:, None] == table[None, :], plan[None, :], 0.0)
    sigma = jnp.sum(picked, axis=1)
    level = 0.25 * jnp.log(sigma)
    count = TF // 2
    freqs = jnp.exp(jnp.arange(count, dtype=jnp.float32) * (math.log(1000.0) / count))
    angles = level[:, None] * freqs[None, :]
    return jnp.concatenate([jnp.sin(angles), jnp.cos(angles)], axis=1)


def normalize(field):
    centered = field - jnp.mean(field, axis=-1, keepdims=True)
    spread = jnp.mean(centered * centered, axis=-1, keepdims=True)
    inverse = lax.rsqrt(spread + EPSILON)
    return (centered * inverse, inverse)


def norm_backward(grad_scaled, normed, inverse, scale):
    grad_normed = grad_scaled * scale
    grad_scale = jnp.sum(grad_scaled * normed, axis=1)
    inner = jnp.mean(grad_normed * normed, axis=-1, keepdims=True)
    grad_field = inverse * (
        grad_normed - jnp.mean(grad_normed, axis=-1, keepdims=True) - normed * inner
    )
    return (grad_field, grad_scale)


def rotate(field, cosine, sine):
    half = HD // 2
    first = field[..., :half]
    second = field[..., half:]
    return jnp.concatenate(
        [first * cosine - second * sine, second * cosine + first * sine], axis=-1
    )


def rotary_tables(places):
    half = HD // 2
    inverse = jnp.exp(jnp.arange(half, dtype=jnp.float32) * (-math.log(10000.0) / half))
    angle = places[:, None] * inverse[None, :]
    return (jnp.cos(angle)[:, None, None, :], jnp.sin(angle)[:, None, None, :])


def pack_heads(h_one, qkv_weight, cosine, sine):
    seqs, rows, width = h_one.shape
    raw = jnp.einsum("std,de->ste", h_one, qkv_weight, preferred_element_type=jnp.float32)
    local_heads = qkv_weight.shape[1] // (3 * HD)
    raw = raw.reshape(seqs, rows, local_heads, 3, HD)
    turned = rotate(raw[:, :, :, 0:2], cosine, sine)
    packed = jnp.concatenate([turned, raw[:, :, :, 2:3]], axis=3).astype(jnp.bfloat16)
    return packed.reshape(seqs, rows, local_heads * 3 * HD)


def unpack_grads(grad_packed, cosine, sine):
    seqs, rows, width = grad_packed.shape
    local_heads = width // (3 * HD)
    grad_fields = grad_packed.reshape(seqs, rows, local_heads, 3, HD).astype(jnp.float32)
    unturned = rotate(grad_fields[:, :, :, 0:2], cosine, -sine)
    grad_raw = jnp.concatenate([unturned, grad_fields[:, :, :, 2:3]], axis=3).astype(jnp.bfloat16)
    return grad_raw.reshape(seqs, rows, width)


def gelu_slope(upper):
    return 0.5 * (1.0 + lax.erf(upper * ROOT_HALF)) + upper * DENSITY * jnp.exp(
        -0.5 * upper * upper
    )


def attend_sequence(fields):
    local_heads = fields.shape[1]
    block = min(512, LEN)
    count = LEN // block
    keys = fields[:, :, 1]
    values = fields[:, :, 2]
    query_blocks = fields[:, :, 0].reshape(count, block, local_heads, HD)

    def attend_one_block(query_blk):
        scores = jnp.einsum(
            "qhd,khd->hqk", query_blk, keys, preferred_element_type=jnp.float32
        ) * HD ** (-0.5)
        top = jnp.max(scores, axis=-1, keepdims=True)
        expo = jnp.exp(scores - top)
        totals = jnp.sum(expo, axis=-1, keepdims=True)
        probs = (expo / totals).astype(jnp.bfloat16)
        result = jnp.einsum("hqk,khd->qhd", probs, values, preferred_element_type=jnp.float32)
        return (result.astype(jnp.bfloat16), (top + jnp.log(totals))[:, :, 0])

    results, logsums = lax.map(attend_one_block, query_blocks)
    logsums = jnp.transpose(logsums, (1, 0, 2)).reshape(local_heads, LEN)
    return (results.reshape(LEN, local_heads, HD), logsums)


def attend_all(packed_heads):
    items = packed_heads.shape[0]
    local_heads = packed_heads.shape[2] // (3 * HD)
    fields = packed_heads.reshape(items, LEN, local_heads, 3, HD)
    results, logsums = lax.map(attend_sequence, fields)
    return (results.reshape(items, LEN, local_heads * HD), logsums)


def back_sequence(pieces):
    fields, logsums, grad_heads = pieces
    local_heads = fields.shape[1]
    block = min(512, LEN)
    count = LEN // block
    keys = fields[:, :, 1]
    values = fields[:, :, 2]
    query_blocks = fields[:, :, 0].reshape(count, block, local_heads, HD)
    grad_blocks = grad_heads.reshape(count, block, local_heads, HD)
    sum_blocks = jnp.transpose(logsums.reshape(local_heads, count, block), (1, 0, 2))

    def back_one_block(carry, piece):
        key_acc, value_acc = carry
        query_blk, grad_blk, sum_blk = piece
        scores = jnp.einsum(
            "qhd,khd->hqk", query_blk, keys, preferred_element_type=jnp.float32
        ) * HD ** (-0.5)
        probs = jnp.exp(scores - sum_blk[:, :, None])
        grad_probs = jnp.einsum(
            "qhd,khd->hqk", grad_blk, values, preferred_element_type=jnp.float32
        )
        inner = jnp.sum(probs * grad_probs, axis=-1, keepdims=True)
        grad_scores = (probs * (grad_probs - inner)).astype(jnp.bfloat16)
        grad_query = jnp.einsum(
            "hqk,khd->qhd", grad_scores, keys, preferred_element_type=jnp.float32
        ) * HD ** (-0.5)
        key_acc = key_acc + jnp.einsum(
            "hqk,qhd->khd", grad_scores, query_blk, preferred_element_type=jnp.float32
        ) * HD ** (-0.5)
        value_acc = value_acc + jnp.einsum(
            "hqk,qhd->khd", probs.astype(jnp.bfloat16), grad_blk, preferred_element_type=jnp.float32
        )
        return ((key_acc, value_acc), grad_query)

    empty = jnp.zeros((LEN, local_heads, HD), jnp.float32)
    (grad_keys, grad_values), grad_queries = lax.scan(
        back_one_block, (empty, empty), (query_blocks, grad_blocks, sum_blocks)
    )
    grad_queries = grad_queries.reshape(LEN, local_heads, HD)
    return jnp.stack([grad_queries, grad_keys, grad_values], axis=2).astype(jnp.bfloat16)


def back_all(packed_heads, logsums, grad_heads):
    items = packed_heads.shape[0]
    local_heads = packed_heads.shape[2] // (3 * HD)
    fields = packed_heads.reshape(items, LEN, local_heads, 3, HD)
    grads = grad_heads.reshape(items, LEN, local_heads, HD)
    result = lax.map(back_sequence, (fields, logsums, grads))
    return result.reshape(items, LEN, local_heads * 3 * HD)


def data_layer(
    tokens, cotangent, w_qkv, w_up, w_out, w_down, scale_one, scale_two, norm_one, inverse_one
):
    seqs, local_len, width = tokens.shape
    wide = (
        lax.all_gather(w_qkv, "seq", axis=1, tiled=True),
        lax.all_gather(w_up, "seq", axis=1, tiled=True),
        lax.all_gather(w_out, "seq", axis=0, tiled=True),
        lax.all_gather(w_down, "seq", axis=0, tiled=True),
    )
    full_qkv, full_up, full_out, full_down = (
        lax.all_gather(wide[0], "dp", axis=0, tiled=True),
        lax.all_gather(wide[1], "dp", axis=0, tiled=True),
        lax.all_gather(wide[2], "dp", axis=1, tiled=True),
        lax.all_gather(wide[3], "dp", axis=1, tiled=True),
    )
    field = tokens.astype(jnp.float32)
    h_one = (norm_one * scale_one).astype(jnp.bfloat16)
    places = (lax.axis_index("seq") * local_len + jnp.arange(local_len, dtype=jnp.int32)).astype(
        jnp.float32
    )
    cosine, sine = rotary_tables(places)
    packed = pack_heads(h_one, full_qkv, cosine, sine)
    packed_heads = lax.all_to_all(packed, "seq", split_axis=2, concat_axis=1, tiled=True)
    results, logsums = attend_all(packed_heads)
    back_tokens = lax.all_to_all(results, "seq", split_axis=1, concat_axis=2, tiled=True)
    middle = field + jnp.einsum(
        "std,de->ste", back_tokens, full_out, preferred_element_type=jnp.float32
    )
    norm_two, inverse_two = normalize(middle)
    h_two = (norm_two * scale_two).astype(jnp.bfloat16)
    upper = jnp.einsum("std,df->stf", h_two, full_up, preferred_element_type=jnp.float32)
    active = jax.nn.gelu(upper, approximate=False).astype(jnp.bfloat16)
    output = (
        middle + jnp.einsum("stf,fd->std", active, full_down, preferred_element_type=jnp.float32)
    ).astype(jnp.bfloat16)
    grad_down = jnp.einsum("stf,std->fd", active, cotangent, preferred_element_type=jnp.float32)
    grad_active = jnp.einsum(
        "std,fd->stf", cotangent, full_down, preferred_element_type=jnp.float32
    )
    grad_upper = (grad_active * gelu_slope(upper)).astype(jnp.bfloat16)
    grad_up = jnp.einsum("std,stf->df", h_two, grad_upper, preferred_element_type=jnp.float32)
    grad_htwo = jnp.einsum("stf,df->std", grad_upper, full_up, preferred_element_type=jnp.float32)
    grad_middle, grad_scale_two = norm_backward(grad_htwo, norm_two, inverse_two, scale_two)
    grad_middle = grad_middle + cotangent.astype(jnp.float32)
    grad_branch = grad_middle.astype(jnp.bfloat16)
    grad_out = jnp.einsum(
        "std,ste->de", back_tokens, grad_branch, preferred_element_type=jnp.float32
    )
    grad_attended = jnp.einsum(
        "ste,de->std", grad_branch, full_out, preferred_element_type=jnp.float32
    ).astype(jnp.bfloat16)
    grad_heads = lax.all_to_all(grad_attended, "seq", split_axis=2, concat_axis=1, tiled=True)
    grad_packed_heads = back_all(packed_heads, logsums, grad_heads)
    grad_packed = lax.all_to_all(grad_packed_heads, "seq", split_axis=1, concat_axis=2, tiled=True)
    grad_raw = unpack_grads(grad_packed, cosine, sine)
    grad_qkv = jnp.einsum("std,ste->de", h_one, grad_raw, preferred_element_type=jnp.float32)
    grad_hone = jnp.einsum("ste,de->std", grad_raw, full_qkv, preferred_element_type=jnp.float32)
    grad_field, grad_scale_one = norm_backward(grad_hone, norm_one, inverse_one, scale_one)
    grad_tokens = (grad_middle + grad_field).astype(jnp.bfloat16)
    partial_sums = (
        lax.psum_scatter(
            grad_qkv.astype(jnp.bfloat16), "dp", scatter_dimension=0, tiled=True
        ).astype(jnp.float32),
        lax.psum_scatter(
            grad_up.astype(jnp.bfloat16), "dp", scatter_dimension=0, tiled=True
        ).astype(jnp.float32),
        lax.psum_scatter(
            grad_out.astype(jnp.bfloat16), "dp", scatter_dimension=1, tiled=True
        ).astype(jnp.float32),
        lax.psum_scatter(
            grad_down.astype(jnp.bfloat16), "dp", scatter_dimension=1, tiled=True
        ).astype(jnp.float32),
    )
    sums = (
        lax.psum_scatter(
            partial_sums[0].astype(jnp.bfloat16), "seq", scatter_dimension=1, tiled=True
        ).astype(jnp.float32),
        lax.psum_scatter(
            partial_sums[1].astype(jnp.bfloat16), "seq", scatter_dimension=1, tiled=True
        ).astype(jnp.float32),
        lax.psum_scatter(
            partial_sums[2].astype(jnp.bfloat16), "seq", scatter_dimension=0, tiled=True
        ).astype(jnp.float32),
        lax.psum_scatter(
            partial_sums[3].astype(jnp.bfloat16), "seq", scatter_dimension=0, tiled=True
        ).astype(jnp.float32),
    )
    return (output, grad_tokens, grad_scale_one, grad_scale_two, sums)


def shards(tokens, bins, plan, w_qkv, w_out, w_up, w_down, w_time, cotangent):
    feats = time_features(plan, bins).astype(jnp.bfloat16)
    full_time = lax.all_gather(w_time, ("dp", "seq"), axis=0, tiled=True)
    modul = jnp.dot(feats, full_time, preferred_element_type=jnp.float32)
    scale_one = 1.0 + modul[:, None, :D]
    scale_two = 1.0 + modul[:, None, D:]
    norm_one, inverse_one = normalize(tokens.astype(jnp.float32))
    output, grad_tokens, grad_scale_one, grad_scale_two, sums = data_layer(
        tokens, cotangent, w_qkv, w_up, w_out, w_down, scale_one, scale_two, norm_one, inverse_one
    )
    grad_scales = jnp.concatenate([grad_scale_one, grad_scale_two], axis=1)
    grad_time = jnp.dot(feats.astype(jnp.float32).T, grad_scales, precision=HIGHEST)
    time_sum = lax.psum_scatter(grad_time, ("dp", "seq"), scatter_dimension=0, tiled=True)
    return (output, grad_tokens, sums[0], sums[2], sums[1], sums[3], time_sum)


BF = jnp.bfloat16
F32 = jnp.float32
MESHID = pl.DeviceIdType.MESH
QUERY_SCALE = HD**-0.5 / math.log(2.0)
VMEM_LIMIT = 60 * 1024 * 1024


def mm(a, b):
    return lax.dot_general(a, b, (((1,), (0,)), ((), ())), preferred_element_type=F32)


def mm_nt(a, b):
    return lax.dot_general(a, b, (((1,), (1,)), ((), ())), preferred_element_type=F32)


def mm_tn(a, b):
    return lax.dot_general(a, b, (((0,), (0,)), ((), ())), preferred_element_type=F32)


def peers():
    g = lax.axis_index("dp")
    s = lax.axis_index("seq")
    core = lax.rem(s, 2)
    return g, s, core, s + 1 - 2 * core, lax.rem(s + 2, 4), 3 - s


def remote(src, dst, ss, rs, i, dev):
    return pltpu.make_async_remote_copy(
        src_ref=src,
        dst_ref=dst,
        send_sem=ss.at[i],
        recv_sem=rs.at[i],
        device_id=dev,
        device_id_type=MESHID,
    )


def greet(devices):
    barrier = pltpu.get_barrier_semaphore()
    for dev in devices:
        pl.semaphore_signal(barrier, inc=1, device_id=dev, device_id_type=MESHID)
    pl.semaphore_wait(barrier, len(devices))


def moments(field):
    centered = field - jnp.mean(field, axis=-1, keepdims=True)
    spread = jnp.mean(centered * centered, axis=-1, keepdims=True)
    inverse = lax.rsqrt(spread + EPSILON)
    return centered * inverse, inverse


def ring_place(g):
    z, y = g // 2, lax.rem(g, 2)
    return z + y * (7 - 2 * z)


def ring_index(p):
    p = lax.rem(p + 16, 8)
    return 2 * p + (p // 4) * (15 - 4 * p)


WAYS = (1, -1)


class Gather:
    def __init__(self, own, view, ss, rs, first):
        self.own, self.view, self.ss, self.rs, self.first = own, view, ss, rs, first

    def hop(self, k, way):
        g, s = lax.axis_index("dp"), lax.axis_index("seq")
        p = ring_place(g)
        j = ring_index(p - way * (k - 1))
        half = None if k < 4 else (0 if way > 0 else 1)
        dst = self.view(j, half)
        src = self.own if k == 1 else dst
        i = self.first + 2 * (k - 1) + (way < 0)
        return remote(src, dst, self.ss, self.rs, i, (ring_index(p + way), s))

    def start(self):
        for way in WAYS:
            self.hop(1, way).start()

    def forward(self, k):
        for way in WAYS:
            self.hop(k - 1, way).wait_recv()
            self.hop(k, way).start()

    def arrive(self):
        for way in WAYS:
            self.hop(4, way).wait_recv()

    def drain(self):
        for k in (1, 2, 3, 4):
            for way in WAYS:
                self.hop(k, way).wait_send()


class Scatter:
    def __init__(self, view, halves, wholes, ss, rs, first):
        self.view, self.halves, self.wholes = view, halves, wholes
        self.ss, self.rs, self.first = ss, rs, first

    def hop(self, k, way):
        g, s = lax.axis_index("dp"), lax.axis_index("seq")
        p = ring_place(g)
        side = 0 if way > 0 else 1
        j = ring_index(p + way * (5 - k))
        src = self.view(j, side if k == 1 else None)
        dst = self.halves.at[side] if k == 1 else self.wholes.at[3 * side + k - 2]
        i = self.first + 2 * (k - 1) + side
        return remote(src, dst, self.ss, self.rs, i, (ring_index(p + way), s))

    def start(self):
        for way in WAYS:
            self.hop(1, way).start()

    def forward(self, k):
        p = ring_place(lax.axis_index("dp"))
        for way in WAYS:
            side = 0 if way > 0 else 1
            self.hop(k - 1, way).wait_recv()
            got = self.halves.at[side] if k == 2 else self.wholes.at[3 * side + k - 3]
            mine = self.view(ring_index(p + way * (5 - k)), side if k == 2 else None)
            mine[...] = (mine[...].astype(F32) + got[...].astype(F32)).astype(BF)
            self.hop(k, way).start()

    def result(self):
        for way in WAYS:
            self.hop(4, way).wait_recv()
        mine = self.view(lax.axis_index("dp"), None)
        return mine[...].astype(F32) + (self.wholes[2].astype(F32) + self.wholes[5].astype(F32))

    def drain(self):
        for k in (1, 2, 3, 4):
            for way in WAYS:
                self.hop(k, way).wait_send()


def rows_of(ref, half, size):
    return ref if half is None else ref.at[half * (size // 2) : (half + 1) * (size // 2)]


def ordering(heads):
    half, size = HD // 2, heads * HD
    to = lax.broadcasted_iota(jnp.int32, (1, 3 * size), 1)
    part, at = to // size, lax.rem(to, size)
    side, rest = at // (size // 2), lax.rem(at, size // 2)
    turned = (rest // half) * (3 * HD) + part * HD + side * half + lax.rem(rest, half)
    plain = (at // HD) * (3 * HD) + 2 * HD + lax.rem(at, HD)
    source = jnp.where(part == 2, plain, turned)
    rows = lax.broadcasted_iota(jnp.int32, (3 * size, 3 * size), 0)
    return jnp.where(rows == source, 1.0, 0.0).astype(BF)


def k1_body(
    tok, wt, feats, w_qkv, w_out, w_up, w_down, cs, sn, cot,
    modul, feats_out, wq_out, out_all, up_all, down_all, n_out, qkv_out, lse, attn_heads, attn_rows, cot_all,
    act_out, slope_out, htwo_out, mid_out,
    tokv, wtime, pbuf, vt, cotv, wq, nv, qkv, attn, outv, upv, act, slope, htwo, mids, csv, snv,
    ks, ls, ss, rs, gs, gr, fs_, fr_, os_,
):
    g, s, core, s1, s2, s3 = peers()
    p = ring_place(g)
    nb, tl = tok.shape[0], tok.shape[1]
    rows = 4 * tl
    blk = 256
    nq = rows // blk
    heads = attn.shape[3] // HD
    nr, nc = w_out.shape[0], w_out.shape[1]

    def lanes(j, size):
        return pl.ds(pl.multiple_of(j * size, size), size)

    def view_out(other):
        def view(j, half):
            lo, size = (0, nr) if half is None else (half * (nr // 2), nr // 2)
            return outv.at[pl.ds(pl.multiple_of(other * nr + lo, size), size), lanes(j, nc)]

        return view

    def view_down(j, half):
        size = w_down.shape[0]
        lo, n = (0, size) if half is None else (half * (size // 2), size // 2)
        return down_all.at[lo : lo + n, lanes(j, w_down.shape[1])]

    def view_rows(ref, size):
        def view(j, half):
            lo, n = (0, size) if half is None else (half * (size // 2), size // 2)
            return ref.at[pl.ds(pl.multiple_of(j * size + lo, n), n)]

        return view

    def view_time(j, half):
        return wtime.at[j] if half is None else wtime.at[j, :, half * D : (half + 1) * D]

    def view_qkv(side):
        size = w_qkv.shape[0]

        def view(j, half):
            lo, n = (0, size // 2) if half is None else (half * (size // 4), size // 4)
            at = pl.multiple_of(j * size + side * (size // 2) + lo, n)
            return wq.at[pl.ds(at, n)]

        return view

    here = view_out(s)(g, None)
    time_ring = Gather(wt, view_time, gs, gr, 0)
    part = w_qkv.shape[0] // 2
    qkv_rings = [
        Gather(view_qkv(i)(g, None), view_qkv(i), gs, gr, 8 + 40 * i)
        for i in range(2)
    ]
    up_ring = Gather(w_up, view_rows(upv, w_up.shape[0]), gs, gr, 16)
    down_ring = Gather(w_down, view_down, gs, gr, 24)
    out_ring = Gather(w_out, view_out(s), gs, gr, 32)
    far_ring = Gather(view_out(s2)(g, None), view_out(s2), gs, gr, 40)

    local = [
        pltpu.make_async_copy(tok, tokv.at[:, s], ls.at[0]),
        pltpu.make_async_copy(cot, cotv, ls.at[5]),
        pltpu.make_async_copy(w_up, view_rows(upv, w_up.shape[0])(g, None), ls.at[2]),
        pltpu.make_async_copy(w_down, view_down(g, None), ls.at[3]),
        pltpu.make_async_copy(w_out, here, ls.at[4]),
        pltpu.make_async_copy(cs, csv, ls.at[6]),
        pltpu.make_async_copy(sn, snv, ls.at[7]),
    ]
    greet([(g, s1), (g, s2), (g, s3), (ring_index(p + 1), s), (ring_index(p - 1), s)])
    time_ring.start()
    pair_out = remote(w_out, here, ss, rs, 0, (g, s2))
    pair_out.start()
    far = [remote(tok.at[b], tokv.at[b, s], ss, rs, 1 + b, (g, s2)) for b in range(nb)]
    far[0].start()
    ordered = mm(w_qkv[...], ordering(heads)).astype(BF)
    wq[pl.ds(pl.multiple_of(g * w_qkv.shape[0], w_qkv.shape[0]), w_qkv.shape[0])] = ordered
    for ring in qkv_rings:
        ring.start()
    near = []
    for b in range(nb):
        cp = remote(tok.at[b], tokv.at[b, s], ss, rs, 3 + b, (g, s1))
        cp.start()
        near.append(cp)
    for cp in local:
        cp.start()
    wtime[g] = wt[...]
    pieces = [(0, 0, tl // 4), (0, tl // 4, tl)] + [(b, 0, tl) for b in range(1, nb)]

    def cot_piece(k):
        b, lo, hi = pieces[k]
        return remote(
            cotv.at[b, lo:hi], cot_all.at[b, s, lo:hi], ss, rs, 18 + k, (g, s2)
        )

    local[1].wait()
    cot_far = [cot_piece(k) for k in range(len(pieces))]
    cot_far[0].start()
    for k in (2, 3, 4):
        time_ring.forward(k)
        for ring in qkv_rings:
            ring.forward(k)
    up_ring.start()
    out_ring.start()
    pair_out.wait_recv()
    far_ring.start()
    time_ring.arrive()
    depth = wt.shape[0]
    feats_out[...] = feats[...]
    lane_t = lax.broadcasted_iota(jnp.int32, (depth, TF), 1)
    row_t = lax.broadcasted_iota(jnp.int32, (depth, TF), 0)
    sums = [jnp.zeros((depth, 2 * D), F32) for _ in range(nb)]
    for d in range(wtime.shape[0]):
        hit = lane_t == row_t + (4 * d + s) * depth
        weights = wtime[d].astype(F32)
        for b in range(nb):
            column = jnp.sum(jnp.where(hit, feats[b : b + 1], 0.0), axis=1, keepdims=True)
            sums[b] = sums[b] + weights * column
    pbuf[0] = jnp.concatenate([jnp.sum(v, axis=0, keepdims=True) for v in sums], axis=0)
    small = []
    for e, other in ((1, s1), (2, s2), (3, s3)):
        cp = remote(pbuf.at[0], pbuf.at[e], ss, rs, 4 + e, (g, other))
        cp.start()
        small.append(cp)
    far[1].start()
    cot_far[1].start()
    passed = [
        remote(tokv.at[b, s2], tokv.at[b, s2], ss, rs, 8 + b, (g, s1)) for b in range(nb)
    ]
    cot_near = [remote(cotv.at[b], cot_all.at[b, s], ss, rs, 12 + b, (g, s1)) for b in range(nb)]
    cot_pass = [
        remote(cot_all.at[b, s2], cot_all.at[b, s2], ss, rs, 14 + b, (g, s1)) for b in range(nb)
    ]
    far[0].wait_recv()
    passed[0].start()
    for c in small:
        c.wait_recv()
    modul[...] = (pbuf[0] + pbuf[1]) + (pbuf[2] + pbuf[3])
    for ring in qkv_rings:
        ring.arrive()
    for i in (0, 5, 6):
        local[i].wait()
    keep_w = pltpu.make_async_copy(wq, wq_out, ls.at[8])
    keep_w.start()
    keep_cot = pltpu.make_async_copy(cotv, cot_all.at[:, s], ls.at[9])
    keep_cot.start()

    def attn_copy(kind, it):
        b, q = it // nq, lax.rem(it, nq)
        r = pl.ds(pl.multiple_of(q * blk, blk), blk)
        ref = attn.at[b, s2 if kind == 2 else s, r]
        return remote(ref, ref, fs_.at[kind], fr_.at[kind], it, (g, s2 if kind == 0 else s1))

    lane = lax.broadcasted_iota(jnp.int32, (1, 2 * 128), 1)

    def keep_fields(b):
        return (
            pltpu.make_async_copy(nv.at[b], n_out.at[b], ks.at[0, b]),
            pltpu.make_async_copy(qkv.at[b], qkv_out.at[b], ks.at[1, b]),
        )

    def project(b):
        scale = 1.0 + modul[pl.ds(b, 1), :D]

        def one(i, _):
            r = pl.ds(pl.multiple_of(i * blk, blk), blk)
            normed, _inv = moments(tokv[b, i].astype(F32))
            nv[b, r] = normed.astype(BF)
            raw = mm((normed * scale).astype(BF), wq[...])
            c, n = csv[r], snv[r]
            qa, qb = raw[:, :128] * QUERY_SCALE, raw[:, 128:256] * QUERY_SCALE
            ka, kb = raw[:, 256:384], raw[:, 384:512]
            qkv[b, 0, r] = jnp.concatenate([qa * c - qb * n, qb * c + qa * n], axis=1).astype(BF)
            qkv[b, 1, r] = jnp.concatenate([ka * c - kb * n, kb * c + ka * n], axis=1).astype(BF)
            qkv[b, 2, r] = raw[:, 512:].astype(BF)
            return 0

        lax.fori_loop(0, nq, one, 0)

    def pass_attn(lo, hi):
        def forward(it, _):
            attn_copy(0, it).wait_recv()
            attn_copy(2, it).start()
            return 0

        lax.fori_loop(lo, hi, forward, 0)

    def arrive_attn(lo, hi):
        def forward(it, _):
            attn_copy(1, it).wait_recv()
            attn_copy(2, it).wait_recv()
            return 0

        lax.fori_loop(lo, hi, forward, 0)

    def tokens_of(b):
        near[b].wait_recv()
        passed[b].wait_recv()

    def second_tokens():
        far[1].wait_recv()
        passed[1].start()

    def step(it, _):
        b, q = it // nq, lax.rem(it, nq)
        for i in range(nb):

            @pl.when(it == i * nq)
            def _(i=i):
                tokens_of(i)

        def at(events):
            for when, action in events:

                @pl.when(it == when)
                def _(action=action):
                    action()

        def up_out(k):
            up_ring.forward(k)
            out_ring.forward(k)
            far_ring.forward(k)

        at(((4, lambda: up_out(4)), (4, down_ring.start)))

        @pl.when(q == 0)
        def _():
            project(b)
            vt[...] = qkv[b, 2].T
            for cp in keep_fields(b):
                cp.start()

        at(
            (
                (0, lambda: up_out(2)),
                (2, lambda: up_out(3)),
                (2, second_tokens),
                (6, lambda: pass_attn(0, nq)),
                (7, lambda: down_ring.forward(2)),
            )
        )
        r = pl.ds(pl.multiple_of(q * blk, blk), blk)
        query, keys = qkv[b, 0, r], qkv[b, 1]
        outs, stats = [], []
        for h in range(heads):
            mask = lax.rem(lane, 128) // 32 == h
            scores = mm_nt(keys, jnp.where(mask, query, jnp.zeros_like(query)))
            top = jnp.max(scores, axis=0, keepdims=True)
            expo = jnp.exp2(scores - top)
            total = jnp.sum(expo, axis=0, keepdims=True)
            outs.append(mm(vt[h * HD : (h + 1) * HD], expo.astype(BF)) * (1.0 / total))
            stats.append(top + jnp.log2(total))
        attn[b, s, r] = jnp.concatenate(outs, axis=0).T.astype(BF)
        lse[b, :, r] = jnp.concatenate(stats + [jnp.zeros((8 - heads, blk), F32)], axis=0)
        attn_copy(0, it).start()
        attn_copy(1, it).start()
        return 0

    lax.fori_loop(0, nb * nq, step, 0)
    for cp in cot_far[2:] + cot_near:
        cp.start()
    keep = pltpu.make_async_copy(attn.at[:, s], attn_heads, ls.at[10])
    keep.start()
    out_ring.arrive()
    far_ring.arrive()
    local[4].wait()
    cross = []
    for e, other in ((0, s), (1, s2)):
        ref = outv.at[pl.ds(pl.multiple_of(other * nr, nr), nr)]
        cp = remote(ref, ref, ss, rs, 16 + e, (g, s1))
        cp.start()
        cross.append(cp)
    up_ring.arrive()
    local[2].wait()
    for cp in cross:
        cp.wait_recv()
    arrive_attn(0, nq)
    keep_out = pltpu.make_async_copy(outv, out_all, ls.at[11])
    keep_out.start()
    keep_up = pltpu.make_async_copy(upv, up_all, ls.at[12])
    keep_up.start()

    def keep_block(i):
        return (
            pltpu.make_async_copy(act.at[i], act_out.at[i], os_.at[0, i]),
            pltpu.make_async_copy(slope.at[i], slope_out.at[i], os_.at[1, i]),
            pltpu.make_async_copy(htwo.at[i], htwo_out.at[i], os_.at[2, i]),
        )

    def feed(i, _):
        b, owner = i // 4, lax.rem(i, 4)
        for when, action in (
            (1, lambda: down_ring.forward(3)),
            (3, lambda: pass_attn(nq, 2 * nq)),
            (4, lambda: arrive_attn(nq, 2 * nq)),
            (4, lambda: down_ring.forward(4)),
        ):

            @pl.when(i == when)
            def _(action=action):
                action()

        scale = 1.0 + modul[pl.ds(b, 1), D:]
        r = pl.ds(pl.multiple_of(owner * tl, tl), tl)
        joined = jnp.concatenate([attn[b, j, r] for j in range(4)], axis=1)
        mid = tokv[b, owner].astype(F32) + mm(joined, outv[...])
        normed, _inv = moments(mid)
        h = (normed * scale).astype(BF)
        upper = mm(h, upv[...])
        phi = 0.5 * (1.0 + lax.erf(upper * ROOT_HALF))
        act[i] = (upper * phi).astype(BF)
        slope[i] = (phi + upper * (DENSITY * jnp.exp(-0.5 * upper * upper))).astype(BF)
        htwo[i] = h

        @pl.when(owner == s)
        def _():
            mids[b] = mid

        for cp in keep_block(i):
            cp.start()
        return 0

    lax.fori_loop(0, 4 * nb, feed, 0)
    keep_mid = pltpu.make_async_copy(mids, mid_out, ls.at[13])
    keep_mid.start()
    own_rows = pl.ds(pl.multiple_of(s * tl, tl), tl)
    keep_rows = pltpu.make_async_copy(attn.at[:, :, own_rows], attn_rows, ls.at[14])
    keep_rows.start()
    for b in range(nb):
        for k, piece in enumerate(pieces):
            if piece[0] == b:
                cot_far[k].wait_recv()
        cot_pass[b].start()

    def finish(it, _):
        attn_copy(0, it).wait_send()
        attn_copy(1, it).wait_send()
        attn_copy(2, it).wait_send()
        return 0

    lax.fori_loop(0, nb * nq, finish, 0)

    def kept(i, _):
        for cp in keep_block(i):
            cp.wait()
        return 0

    lax.fori_loop(0, 4 * nb, kept, 0)
    down_ring.arrive()
    for cp in cot_near + cot_pass:
        cp.wait()
    for cp in cot_far + far + near + passed + small + cross + [pair_out]:
        cp.wait_send()
    for ring in [time_ring, up_ring, down_ring, out_ring, far_ring] + qkv_rings:
        ring.drain()
    local[3].wait()
    for cp in (keep_cot, keep, keep_w, keep_out, keep_up, keep_mid, keep_rows):
        cp.wait()
    for b in range(nb):
        for cp in keep_fields(b):
            cp.wait()


def run_k1(nd, tokens, w_time, feats, w_qkv, w_out, w_up, w_down, cs, sn, cot):
    nb, tl, width = tokens.shape
    rows = 4 * tl
    cols = w_qkv.shape[1] // 3
    hidden = w_up.shape[1]
    vm = pl.BlockSpec(memory_space=pltpu.VMEM)
    hb = pl.BlockSpec(memory_space=pl.ANY)
    steps = nb * (rows // 256)
    sds = jax.ShapeDtypeStruct
    dma = pltpu.SemaphoreType.DMA
    v = pltpu.VMEM
    return pl.pallas_call(
        k1_body,
        out_shape=(
            sds((nb, 2 * width), F32),
            sds((nb, TF), F32),
            sds((width, 3 * cols), BF),
            sds((width, width), BF),
            sds((width, hidden), BF),
            sds((hidden, width), BF),
            sds((nb, rows, width), BF),
            sds((nb, 3, rows, cols), BF),
            sds((nb, 8, rows), F32),
            sds((nb, rows, cols), BF),
            sds((nb, 4, tl, cols), BF),
            sds((nb, 4, tl, width), BF),
            sds((4 * nb, tl, hidden), BF),
            sds((4 * nb, tl, hidden), BF),
            sds((4 * nb, tl, width), BF),
            sds((nb, tl, width), F32),
        ),
        in_specs=[hb, vm, vm, vm, vm, vm, vm, hb, hb, hb],
        out_specs=(vm, vm, hb, hb, hb, hb, hb, hb, vm) + (hb,) * 7,
        scratch_shapes=[
            v((nb, 4, tl, width), BF),
            v((nd,) + w_time.shape, BF),
            v((4, nb, 2 * width), F32),
            v((cols, rows), BF),
            v((nb, tl, width), BF),
            v((width, 3 * cols), BF),
            v((nb, rows, width), BF),
            v((nb, 3, rows, cols), BF),
            v((nb, 4, rows, cols), BF),
            v((width, width), BF),
            v((width, hidden), BF),
            v((4 * nb, tl, hidden), BF),
            v((4 * nb, tl, hidden), BF),
            v((4 * nb, tl, width), BF),
            v((nb, tl, width), F32),
            v(cs.shape, F32),
            v(sn.shape, F32),
            dma((2, nb)),
            dma((15,)),
            dma((22,)),
            dma((22,)),
            dma((56,)),
            dma((56,)),
            dma((3, steps)),
            dma((3, steps)),
            dma((3, 4 * nb)),
        ],
        compiler_params=pltpu.CompilerParams(
            collective_id=0, has_side_effects=True, vmem_limit_bytes=VMEM_LIMIT
        ),
        name="attention_forward",
    )(tokens, w_time, feats, w_qkv, w_out, w_up, w_down, cs, sn, cot)


def k2_body(
    act_h, slope_h, htwo_h, mid_h, attn_h, cot_h, modul, w_out_h, w_up_h, w_down_h,
    grad_up, grad_out, d_mid_h, base_h, osend_h, d_heads, dsc, s_down,
    act, dup, htwo, mids, attn, cot, w_out, w_up, w_down, d_mid, base, osend,
    pa, pb_, ra, rb, xs, xr, dat, stage, gdv, down_h, down_w,
    ls, ss, rs, os_, ins, keeps, bs, gs, gr,
):
    g, s, core, s1, s2, s3 = peers()
    p = ring_place(g)
    chip = s // 2
    nb, tl = cot.shape[0], cot.shape[2]

    def pull(jp, which):
        phase, b = jp // nb, lax.rem(jp, nb)
        where = chip + (1 - phase) * (1 - 2 * chip)
        owner = 2 * where + (1 - core if which == 0 else core)
        i = b * 4 + owner
        k = 2 * jp + which
        return (
            pltpu.make_async_copy(cot_h.at[b, owner], cot.at[b, owner], bs.at[0, k]),
            pltpu.make_async_copy(slope_h.at[i], dup.at[i], bs.at[1, k]),
            pltpu.make_async_copy(act_h.at[i], act.at[i], bs.at[2, k]),
        )

    loads = []
    for i, (src, dst) in enumerate(
        (
            (w_down_h, w_down), (w_up_h, w_up),
            (mid_h, mids), (w_out_h, w_out), (htwo_h, htwo), (attn_h, attn),
        )
    ):
        loads.append(pltpu.make_async_copy(src, dst, ins.at[i]))
    first = pull(0, 0)
    loads[0].start()
    for cp in first:
        cp.start()
    loads[1].start()
    for jp in range(2 * nb):
        for which in (0, 1):
            if jp + which:
                for cp in pull(jp, which):
                    cp.start()
    for cp in loads[2:]:
        cp.start()
    greet([(g, s1), (g, s2), (g, s3), (ring_index(p + 1), s), (ring_index(p - 1), s)])
    hidden = act.shape[2]
    pc = s_down.shape[1]

    def view_down(j, half):
        lo, n = (0, hidden) if half is None else (half * (hidden // 2), hidden // 2)
        return gdv.at[lo : lo + n, pl.ds(pl.multiple_of(j * pc, pc), pc)]

    down_ring = Scatter(view_down, down_h, down_w, gs, gr, 0)

    def back_part(b, owner):
        i = b * 4 + owner
        d_act = mm_nt(cot[b, owner], w_down[...])
        d_up = (d_act * dup[i].astype(F32)).astype(BF)
        dup[i] = d_up
        return mm_nt(d_up, w_up[...])

    def back_copy(jp):
        return remote(pa.at[jp], ra.at[jp], ss, rs, jp, (g, s1))

    def out_copy(jp):
        return remote(pb_.at[jp], rb.at[jp], ss, rs, 4 + jp, (g, s1))

    def far_copy(b):
        return remote(xs.at[b], xr.at[b], ss, rs, 8 + b, (g, s2))

    def place(jp):
        phase, b = jp // nb, lax.rem(jp, nb)
        return phase, b, chip + (1 - phase) * (1 - 2 * chip)

    def give(jp, _):
        phase, b, where = place(jp)

        @pl.when(phase == 0)
        def _():
            for cp in pull(jp, 0):
                cp.wait()

        pa[jp] = back_part(b, 2 * where + 1 - core).astype(BF)
        back_copy(jp).start()
        return 0

    def take(jp, _):
        phase, b, where = place(jp)

        @pl.when(phase == 0)
        def _():
            for cp in pull(jp, 1):
                cp.wait()

        dh = back_part(b, 2 * where + core)
        back_copy(jp).wait_recv()
        dh = dh + ra[jp].astype(F32)

        @pl.when(phase == 0)
        def _():
            xs[b] = dh.astype(BF)
            far_copy(b).start()

        @pl.when(phase == 1)
        def _():
            d_mid[b] = dh

        return 0

    def give_out(jp, _):
        _phase, b, where = place(jp)
        pb_[jp] = mm(act[b * 4 + 2 * where + 1 - core], w_down[...]).astype(BF)
        out_copy(jp).start()
        return 0

    def take_out(jp, _):
        phase, b, where = place(jp)
        out = mm(act[b * 4 + 2 * where + core], w_down[...])
        out_copy(jp).wait_recv()
        out = out + rb[jp].astype(F32)

        @pl.when(phase == 0)
        def _():
            osend[b] = out.astype(BF)

        @pl.when(phase == 1)
        def _():
            base[b] = out + mids[b]

        return 0

    def down_grads(i, _):
        r = pl.ds(pl.multiple_of(i * 256, 256), 256)
        left = act[:, :, r].reshape(4 * nb * tl, 256)
        gdv[r] = mm_tn(left, cot[...].reshape(4 * nb * tl, D)).astype(BF)
        return 0

    def up_copy(i):
        r = pl.ds(pl.multiple_of(i * 256, 256), 256)
        return pltpu.make_async_copy(stage.at[i], grad_up.at[r], os_.at[i])

    def up_grads(i, _):
        r = pl.ds(pl.multiple_of(i * 256, 256), 256)
        left = htwo[:, :, r].reshape(4 * nb * tl, 256)
        stage[i] = mm_tn(left, dup[...].reshape(4 * nb * tl, hidden)).astype(BF)
        up_copy(i).start()
        return 0

    def spread(e, other, b):
        return remote(dat.at[other, b], d_heads.at[s, b], ss, rs, 10 + 2 * e + b, (g, other))

    def tail(b, _):
        scale = 1.0 + modul[pl.ds(b, 1), D:]
        far_copy(b).wait_recv()
        dh = d_mid[b] + xr[b].astype(F32)
        normed, inverse = moments(mids[b])
        dsc[pl.ds(b, 1)] = jnp.sum(dh * normed, axis=0, keepdims=True)
        dn = dh * scale
        inner = jnp.mean(dn * normed, axis=-1, keepdims=True)
        dm = cot[b, s].astype(F32) + inverse * (
            dn - jnp.mean(dn, axis=-1, keepdims=True) - normed * inner
        )
        d_mid[b] = dm
        branch = mm_nt(dm.astype(BF), w_out[...]).astype(BF)
        for j in range(4):
            dat[j, b] = branch[:, j * 256 : (j + 1) * 256]
        for e, other in ((0, s2), (1, s3), (2, s1)):
            spread(e, other, b).start()
        return 0

    for cp in loads[:2]:
        cp.wait()
    half = D // 512
    lax.fori_loop(0, nb, give, 0)
    lax.fori_loop(0, nb, take, 0)
    lax.fori_loop(0, nb, give_out, 0)
    lax.fori_loop(0, nb, take_out, 0)
    for jp in range(nb, 2 * nb):
        for which in (0, 1):
            for cp in pull(jp, which):
                cp.wait()
    lax.fori_loop(0, hidden // 256, down_grads, 0)
    down_ring.start()
    for cp in loads[2:]:
        cp.wait()
    lax.fori_loop(nb, 2 * nb, give, 0)
    lax.fori_loop(nb, 2 * nb, take, 0)
    down_ring.forward(2)
    lax.fori_loop(0, nb - 1, tail, 0)
    lax.fori_loop(nb, 2 * nb, give_out, 0)
    lax.fori_loop(nb, 2 * nb, take_out, 0)
    down_ring.forward(3)
    lax.fori_loop(0, half, up_grads, 0)
    lax.fori_loop(nb - 1, nb, tail, 0)
    lax.fori_loop(half, 2 * half, up_grads, 0)
    keep_all = []
    for i, (src, dst) in enumerate(
        ((d_mid, d_mid_h), (base, base_h), (osend, osend_h), (dat.at[s], d_heads.at[s]))
    ):
        cp = pltpu.make_async_copy(src, dst, keeps.at[i])
        cp.start()
        keep_all.append(cp)
    down_ring.forward(4)
    branch = d_mid[...].astype(BF).reshape(nb * tl, D)
    for j in range(4):
        left = jnp.concatenate([attn[b, j] for b in range(nb)], axis=0)
        up_copy(j).wait()
        stage[j] = mm_tn(left, branch).astype(BF)
        pltpu.make_async_copy(stage.at[j], grad_out.at[j], os_.at[j]).start()

    def done(jp, _):
        back_copy(jp).wait_send()
        out_copy(jp).wait_send()
        return 0

    lax.fori_loop(0, 2 * nb, done, 0)
    s_down[...] = down_ring.result()
    down_ring.drain()
    for b in range(nb):
        far_copy(b).wait_send()
        for e, other in ((0, s2), (1, s3), (2, s1)):
            spread(e, other, b).wait()
    for j in range(4):
        pltpu.make_async_copy(stage.at[j], grad_out.at[j], os_.at[j]).wait()
    for cp in keep_all:
        cp.wait()


def run_k2(nd, act, slope, htwo, mid, attn_rows, cot_all, modul, w_out, w_up, w_down):
    nb, _, tl, width = cot_all.shape
    hidden = w_up.shape[1]
    cols = attn_rows.shape[3]
    pc = width // nd
    vm = pl.BlockSpec(memory_space=pltpu.VMEM)
    hb = pl.BlockSpec(memory_space=pl.ANY)
    sds = jax.ShapeDtypeStruct
    v = pltpu.VMEM
    dma = pltpu.SemaphoreType.DMA
    return pl.pallas_call(
        k2_body,
        out_shape=(
            sds((width, hidden), BF),
            sds((4, cols, width), BF),
            sds((nb, tl, width), F32),
            sds((nb, tl, width), F32),
            sds((nb, tl, width), BF),
            sds((4, nb, tl, cols), BF),
            sds((nb, width), F32),
            sds((hidden, pc), F32),
        ),
        in_specs=[hb, hb, hb, hb, hb, hb, vm, hb, hb, hb],
        out_specs=(hb, hb, hb, hb, hb, hb, vm, vm),
        scratch_shapes=[
            v(act.shape, BF),
            v(slope.shape, BF),
            v(htwo.shape, BF),
            v(mid.shape, F32),
            v(attn_rows.shape, BF),
            v(cot_all.shape, BF),
            v(w_out.shape, BF),
            v(w_up.shape, BF),
            v(w_down.shape, BF),
            v((nb, tl, width), F32),
            v((nb, tl, width), F32),
            v((nb, tl, width), BF),
            v((2 * nb, tl, width), BF),
            v((2 * nb, tl, width), BF),
            v((2 * nb, tl, width), BF),
            v((2 * nb, tl, width), BF),
            v((nb, tl, width), BF),
            v((nb, tl, width), BF),
            v((4, nb, tl, cols), BF),
            v((4, 256, width), BF),
            v((hidden, width), BF),
            v((2, hidden // 2, pc), BF),
            v((6, hidden, pc), BF),
            dma,
            dma((16,)),
            dma((16,)),
            dma((4,)),
            dma((6,)),
            dma((4,)),
            dma((3, 4 * nb)),
            dma((8,)),
            dma((8,)),
        ],
        compiler_params=pltpu.CompilerParams(
            collective_id=1, has_side_effects=True, vmem_limit_bytes=VMEM_LIMIT
        ),
        name="feed_forward",
    )(act, slope, htwo, mid, attn_rows, cot_all, modul, w_out, w_up, w_down)


def k3_body(
    fields_h, lse, attn_h, d_heads_h, w_h, normed_h, tok_h, modul, cs_h, sn_h, d_mid_h, base_h, osend,
    g_up, g_out, dsc_h, feats,
    output, grad_tok, s_qkv, s_out, s_up, s_time,
    orecv, dqt, draw, pa, ra, xs, xr, sumh, dhb,
    vu, vo, vq, oa, ob, ox, osum, up_h, up_w, out_h, out_w, qkv_h, qkv_w,
    dpart, tx, dall, qkv, own, d_heads, w, normed_one, tok, cs, sn, d_mid, base, dsc_two,
    ins, ls, ss, rs, gs, gr,
):
    g, s, core, s1, s2, s3 = peers()
    chip = s // 2
    p = ring_place(g)
    nd = dall.shape[0]
    loads = [
        pltpu.make_async_copy(g_up, vu, ls.at[0]),
        pltpu.make_async_copy(g_out, oa, ls.at[1]),
    ]
    pulls = []
    for i, (src, dst) in enumerate(
        (
            (fields_h, qkv), (attn_h, own), (d_heads_h, d_heads), (cs_h, cs), (sn_h, sn),
            (w_h, w), (normed_h, normed_one), (tok_h, tok), (d_mid_h, d_mid), (base_h, base),
            (dsc_h, dsc_two),
        )
    ):
        pulls.append(pltpu.make_async_copy(src, dst, ins.at[i]))
    for cp in pulls[:3]:
        cp.start()
    for cp in loads:
        cp.start()
    for cp in pulls[3:]:
        cp.start()
    others = [(lax.rem(g + d, nd), s) for d in range(1, nd)]
    greet([(g, s1), (g, s2)] + others)
    nb, tl = tok.shape[0], tok.shape[1]
    rows, cols = own.shape[1], own.shape[2]
    heads = cols // HD
    blk = 256
    nk = rows // blk
    pc = D // nd

    def lanes(j, size):
        return pl.ds(pl.multiple_of(j * size, size), size)

    def view_cols(ref, size):
        def view(j, half):
            lo, n = (0, size) if half is None else (half * (size // 2), size // 2)
            return ref.at[lo : lo + n, lanes(j, pc)]

        return view

    def view_rows(ref):
        def view(j, half):
            lo, n = (0, pc) if half is None else (half * (pc // 2), pc // 2)
            return ref.at[pl.ds(pl.multiple_of(j * pc + lo, n), n)]

        return view

    up_ring = Scatter(view_rows(vu), up_h, up_w, gs, gr, 16)
    out_rings = [
        Scatter(view_cols(vo.at[i], vo.shape[1]), out_h.at[i], out_w.at[i], gs, gr, 8 * i)
        for i in range(2)
    ]
    def view_qkv(side):
        wide = vq.shape[1] // 2

        def view(j, half):
            lo, n = (0, pc) if half is None else (half * (pc // 2), pc // 2)
            return vq.at[
                pl.ds(pl.multiple_of(j * pc + lo, n), n), side * wide : (side + 1) * wide
            ]

        return view

    qkv_rings = [
        Scatter(view_qkv(i), qkv_h.at[i], qkv_w.at[i], gs, gr, 24 + 16 * i) for i in range(2)
    ]

    def qkv_forward(k):
        for ring in qkv_rings:
            ring.forward(k)

    loads[0].wait()
    up_ring.start()
    back = []
    for b in range(nb):
        cp = remote(osend.at[b], orecv.at[b], ss, rs, b, (g, s2))
        cp.start()
        back.append(cp)
    loads[1].wait()
    cross = []
    for i in range(2):
        cp = remote(oa.at[2 * i + 1 - core], ob.at[i], ss, rs, 8 + i, (g, s1))
        cp.start()
        cross.append(cp)
    over = remote(osum, ox, ss, rs, 10, (g, s2))

    def out_pair():
        for i in range(2):
            cross[i].wait_recv()
            vo[i] = (oa[2 * i + core].astype(F32) + ob[i].astype(F32)).astype(BF)
            out_rings[i].start()

    def out_forward(k):
        for ring in out_rings:
            ring.forward(k)

    lane = lax.broadcasted_iota(jnp.int32, (1, cols), 1)

    def near_copy(b, phase):
        i = 2 * b + phase
        return remote(pa.at[i], ra.at[i], ss, rs, 2 + i, (g, s1))

    def far_copy(b):
        return remote(xs.at[b], xr.at[b], ss, rs, 6 + b, (g, s2))

    for cp in pulls[:5]:
        cp.wait()
    out_pair()

    def grads(side):
        wide = vq.shape[1] // 2
        c = slice(side * wide, (side + 1) * wide)

        def one(i, _):
            r = pl.ds(pl.multiple_of(i * 256, 256), 256)
            left = jnp.concatenate(
                [
                    (normed_one[b, :, r].astype(F32) * (1.0 + modul[b : b + 1, r])).astype(BF)
                    for b in range(nb)
                ],
                axis=0,
            )
            vq[r, c] = mm_tn(left, draw[:, :, c].reshape(nb * rows, wide)).astype(BF)
            return 0

        lax.fori_loop(0, D // 256, one, 0)
        qkv_rings[side].start()

    def sequence(b, _):
        for j in range(4):
            dhb[j * tl : (j + 1) * tl] = d_heads[j, b]
        query = qkv[b, 0]
        d_out = dhb[...]
        prod = d_out.astype(F32) * own[b].astype(F32)
        prod = prod.T
        delta = jnp.concatenate(
            [jnp.sum(prod[h * HD : (h + 1) * HD], axis=0, keepdims=True) for h in range(heads)],
            axis=0,
        )
        dqt[...] = jnp.zeros_like(dqt)

        def keys_block(i, _):
            it = b * nk + i
            for when, act in (
                (2, lambda: up_ring.forward(2)),
                (3, lambda: out_forward(2)),
                (4, lambda: up_ring.forward(3)),
                (5, lambda: out_forward(3)),
                (6, lambda: up_ring.forward(4)),
                (7, lambda: out_forward(4)),
            ):

                @pl.when(it == when)
                def _(act=act):
                    act()

            r = pl.ds(pl.multiple_of(i * blk, blk), blk)
            keys, values = qkv[b, 1, r], qkv[b, 2, r]
            dk = jnp.zeros((blk, cols), F32)
            dv = jnp.zeros((blk, cols), F32)
            for h in range(heads):
                mask = lax.rem(lane, 128) // 32 == h
                mask_v = lane // HD == h
                km = jnp.where(mask, keys, jnp.zeros_like(keys))
                vmask = jnp.where(mask_v, values, jnp.zeros_like(values))
                probs = jnp.exp2(mm_nt(km, query) - lse[b, h : h + 1])
                d_probs = mm_nt(vmask, d_out)
                ds = (probs * (d_probs - delta[h : h + 1])).astype(BF)
                dv = jnp.where(mask_v, mm(probs.astype(BF), d_out), dv)
                dk = jnp.where(mask, mm(ds, query), dk)
                dqt[...] += mm_tn(km, ds)
            c, n = cs[r] * math.log(2.0), sn[r] * math.log(2.0)
            da, db = dk[:, :128], dk[:, 128:]
            draw[b, r, 256:512] = jnp.concatenate([da * c + db * n, db * c - da * n], axis=1).astype(BF)
            draw[b, r, 512:768] = dv.astype(BF)
            return 0

        lax.fori_loop(0, nk, keys_block, 0)
        dq = dqt[...].T * 0.125
        da, db = dq[:, :128], dq[:, 128:]
        c, n = cs[...], sn[...]
        draw[b, :, 0:256] = jnp.concatenate([da * c + db * n, db * c - da * n], axis=1).astype(BF)

        @pl.when(b == 0)
        def _():
            for cp in pulls[5:]:
                cp.wait()
            dpart[0, :, :D] = jnp.zeros((nb, D), F32)

        def part(owner):
            r = pl.ds(pl.multiple_of(owner * tl, tl), tl)
            res = mm_nt(draw[b, r], w[...])
            dpart[0, pl.ds(b, 1), :D] += jnp.sum(
                res * normed_one[b, r].astype(F32), axis=0, keepdims=True
            )
            return res

        for phase in range(2):
            where = chip if phase else 1 - chip
            pa[2 * b + phase] = part(2 * where + 1 - core).astype(BF)
            near_copy(b, phase).start()
        kept = part(2 * (1 - chip) + core)
        near_copy(b, 0).wait_recv()
        xs[b] = (kept + ra[2 * b].astype(F32)).astype(BF)
        far_copy(b).start()

        @pl.when(b == nb - 1)
        def _():
            grads(0)
            grads(1)

        kept = part(2 * chip + core)
        near_copy(b, 1).wait_recv()
        sumh[b] = kept + ra[2 * b + 1].astype(F32)
        return 0

    lax.fori_loop(0, nb, sequence, 0)
    dpart[0, :, D:] = dsc_two[...]
    small = [remote(dpart.at[0], dpart.at[1], ss, rs, 11, (g, s1))]
    small[0].start()
    first_out, second_out = out_rings[0].result(), out_rings[1].result()
    osum[...] = jnp.where(chip == 0, second_out, first_out).astype(BF)
    own_out = jnp.where(chip == 0, first_out, second_out)
    over.start()
    qkv_forward(2)
    small[0].wait_recv()
    dall[0, :, : 2 * D] = dpart[0] + dpart[1]
    dall[0, :, 2 * D :] = feats[...]
    wide = [remote(dall.at[0], dall.at[d], ss, rs, 12 + d, others[d - 1]) for d in range(1, nd)]
    for cp in wide:
        cp.start()
    for b in range(nb):
        back[b].wait_recv()
        output[b] = (base[b] + orecv[b].astype(F32)).astype(BF)
    s_up[...] = up_ring.result()
    qkv_forward(3)

    def tail(b, _):
        scale = 1.0 + modul[pl.ds(b, 1), :D]
        far_copy(b).wait_recv()
        normed, inverse = moments(tok[b].astype(F32))
        dn = (sumh[b] + xr[b].astype(F32)) * scale
        inner = jnp.mean(dn * normed, axis=-1, keepdims=True)
        grad_tok[b] = (
            d_mid[b]
            + inverse * (dn - jnp.mean(dn, axis=-1, keepdims=True) - normed * inner)
        ).astype(BF)
        return 0

    lax.fori_loop(0, nb - 1, tail, 0)
    qkv_forward(4)
    lax.fori_loop(nb - 1, nb, tail, 0)
    over.wait_recv()
    s_out[...] = own_out + ox[...].astype(F32)
    for cp in wide:
        cp.wait_recv()
    depth = s_time.shape[0]
    lane_t = lax.broadcasted_iota(jnp.int32, (depth, TF), 1)
    row_t = lax.broadcasted_iota(jnp.int32, (depth, TF), 0)
    mine = jnp.zeros((depth, 2 * D), F32)
    theirs = jnp.zeros((depth, 2 * D), F32)
    for d in range(nd):
        for b in range(nb):
            row = dall[d, b : b + 1]
            for which, other in ((0, s), (1, s2)):
                hit = lane_t == row_t + (4 * g + other) * depth
                column = jnp.sum(jnp.where(hit, row[:, 2 * D :], 0.0), axis=1, keepdims=True)
                if which:
                    theirs = theirs + column * row[:, : 2 * D]
                else:
                    mine = mine + column * row[:, : 2 * D]
    tx[0] = theirs
    swap = remote(tx.at[0], tx.at[1], ss, rs, 12, (g, s2))
    swap.start()
    s_qkv[...] = jnp.concatenate([ring.result() for ring in qkv_rings], axis=1)
    swap.wait_recv()
    s_time[...] = mine + tx[1]
    for b in range(nb):
        back[b].wait_send()
        far_copy(b).wait_send()
        for phase in range(2):
            near_copy(b, phase).wait_send()
    for cp in cross + small + wide + [over, swap]:
        cp.wait_send()
    for ring in out_rings + qkv_rings + [up_ring]:
        ring.drain()


def run_k3(
    nd, qkv, lse, attn_heads, d_heads, w, normed, tokens, modul, cs, sn, d_mid, base, osend,
    g_up, g_out, dsc_two, feats,
):
    nb, tl, width = tokens.shape
    rows, cols = attn_heads.shape[1], attn_heads.shape[2]
    hidden = g_up.shape[1]
    pc = width // nd
    vm = pl.BlockSpec(memory_space=pltpu.VMEM)
    hb = pl.BlockSpec(memory_space=pl.ANY)
    sds = jax.ShapeDtypeStruct
    v = pltpu.VMEM
    dma = pltpu.SemaphoreType.DMA
    return pl.pallas_call(
        k3_body,
        out_shape=(
            sds((nb, tl, width), BF),
            sds((nb, tl, width), BF),
            sds((pc, 3 * cols), F32),
            sds((cols, pc), F32),
            sds((pc, hidden), F32),
            sds((TF // (4 * nd), 2 * width), F32),
        ),
        in_specs=[hb, vm, hb, hb, hb, hb, hb, vm, hb, hb, hb, hb, hb, hb, hb, pl.BlockSpec(memory_space=pltpu.HBM), vm],
        out_specs=(vm,) * 6,
        scratch_shapes=[
            v((nb, tl, width), BF),
            v((cols, rows), F32),
            v((nb, rows, 3 * cols), BF),
            v((2 * nb, tl, width), BF),
            v((2 * nb, tl, width), BF),
            v((nb, tl, width), BF),
            v((nb, tl, width), BF),
            v((nb, tl, width), F32),
            v((rows, cols), BF),
            v((width, hidden), BF),
            v((2, cols, width), BF),
            v((width, 3 * cols), BF),
            v((4, cols, width), BF),
            v((2, cols, width), BF),
            v((cols, pc), BF),
            v((cols, pc), BF),
            v((2, pc // 2, hidden), BF),
            v((6, pc, hidden), BF),
            v((2, 2, cols // 2, pc), BF),
            v((2, 6, cols, pc), BF),
            v((2, 2, pc // 2, 3 * cols // 2), BF),
            v((2, 6, pc, 3 * cols // 2), BF),
            v((2, nb, 2 * width), F32),
            v((2, TF // (4 * nd), 2 * width), F32),
            v((nd, nb, 2 * width + TF), F32),
            v(qkv.shape, BF),
            v((nb, rows, cols), BF),
            v(d_heads.shape, BF),
            v(w.shape, BF),
            v(normed.shape, BF),
            v(tokens.shape, BF),
            v(cs.shape, F32),
            v(sn.shape, F32),
            v(d_mid.shape, F32),
            v(base.shape, F32),
            v(dsc_two.shape, F32),
            dma((11,)),
            dma((2,)),
            dma((20,)),
            dma((20,)),
            dma((48,)),
            dma((48,)),
        ],
        compiler_params=pltpu.CompilerParams(
            collective_id=2, has_side_effects=True, vmem_limit_bytes=52 * 1024 * 1024
        ),
        name="attention_backward",
    )(
        qkv, lse, attn_heads, d_heads, w, normed, tokens, modul, cs, sn, d_mid, base, osend,
        g_up, g_out, dsc_two, feats,
    )


def k4_body(*refs):
    *refs, sems = refs
    count = len(refs) // 2
    moves = []
    for i in range(2):
        moves.append(pltpu.make_async_copy(refs[i], refs[count + i], sems.at[i]))
        moves[i].start()
    for i in range(3, count):
        refs[count + i][...] = refs[i][...]
    w = refs[2][...]
    heads = w.shape[1] // (3 * HD)
    half, size = HD // 2, heads * HD
    pieces = []
    for h in range(heads):
        for part in (0, 1):
            for side in (0, 1):
                at = part * size + side * (size // 2) + h * half
                pieces.append(w[:, at : at + half])
        at = 2 * size + h * HD
        pieces.append(w[:, at : at + HD])
    refs[count + 2][...] = jnp.concatenate(pieces, axis=1)
    for cp in moves:
        cp.wait()


def run_k4(arrays):
    vm = pl.BlockSpec(memory_space=pltpu.VMEM)
    hb = pl.BlockSpec(memory_space=pltpu.HBM)
    specs = [hb, hb] + [vm] * (len(arrays) - 2)
    return pl.pallas_call(
        k4_body,
        out_shape=tuple(jax.ShapeDtypeStruct(a.shape, a.dtype) for a in arrays),
        in_specs=specs,
        out_specs=tuple(specs),
        scratch_shapes=[pltpu.SemaphoreType.DMA((2,))],
        compiler_params=pltpu.CompilerParams(vmem_limit_bytes=16 * 1024 * 1024),
        name="results",
    )(*arrays)


def fast_shards(nd, tokens, bins, plan, w_qkv, w_out, w_up, w_down, w_time, cotangent):
    nb, tl, width = tokens.shape
    rows = 4 * tl
    feats = time_features(plan, bins).astype(BF).astype(F32)
    half = HD // 2
    inverse = np.exp(np.arange(half, dtype=np.float32) * np.float32(-math.log(10000.0) / half))
    angle = np.arange(rows, dtype=np.float32)[:, None] * inverse.astype(np.float32)[None, :]
    cs = np.tile(np.cos(angle.astype(np.float64)).astype(np.float32), (1, 128 // half))
    sn = np.tile(np.sin(angle.astype(np.float64)).astype(np.float32), (1, 128 // half))
    (
        modul, feats, full_qkv, full_out, full_up, full_down, normed, qkv, lse, attn_heads, attn_rows,
        cot_all, act, slope, htwo, mid,
    ) = run_k1(
        nd, tokens, w_time, feats, w_qkv, w_out, w_up, w_down, cs, sn, cotangent
    )
    grad_up, grad_out, d_mid, base, osend, d_heads, dsc_two, sum_down = run_k2(
        nd, act, slope, htwo, mid, attn_rows, cot_all, modul, full_out, full_up, full_down
    )
    output, grad_tokens, sum_qkv, sum_out, sum_up, grad_time = run_k3(
        nd, qkv, lse, attn_heads, d_heads, full_qkv, normed, tokens, modul, cs, sn, d_mid, base,
        osend, grad_up, grad_out, dsc_two, feats,
    )
    return tuple(
        run_k4((output, grad_tokens, sum_qkv, sum_out, sum_up, sum_down, grad_time))
    )


def solution(mesh):
    nd, ns = mesh.shape["dp"], mesh.shape["seq"]
    fast = nd == 8 and ns == 4
    return jax.shard_map(
        functools.partial(fast_shards, nd) if fast else shards,
        mesh=mesh,
        in_specs=(
            P("dp", "seq", None),
            P("dp"),
            P(),
            P("dp", "seq"),
            P("seq", "dp"),
            P("dp", "seq"),
            P("seq", "dp"),
            P(("dp", "seq"), None),
            P("dp", "seq", None),
        ),
        out_specs=(
            P("dp", "seq", None),
            P("dp", "seq", None),
            P("dp", "seq"),
            P("seq", "dp"),
            P("dp", "seq"),
            P("seq", "dp"),
            P(("dp", "seq"), None),
        ),
        check_vma=False,
    )
```

```python
import functools
import math

import jax
import jax.numpy as jnp
import numpy as np
from jax import lax
from jax.experimental import pallas as pl
from jax.experimental.pallas import tpu as pltpu
from jax.sharding import PartitionSpec as P

D = 1024
HD = 64
TF = 256
LEN = 1024


EPSILON = 1e-05
HIGHEST = lax.Precision.HIGHEST
ROOT_HALF = 0.7071067811865476
DENSITY = 0.3989422804014327


def time_features(plan, bins):
    table = jnp.arange(plan.shape[0], dtype=jnp.int32)
    picked = jnp.where(bins[:, None] == table[None, :], plan[None, :], 0.0)
    sigma = jnp.sum(picked, axis=1)
    level = 0.25 * jnp.log(sigma)
    count = TF // 2
    freqs = jnp.exp(jnp.arange(count, dtype=jnp.float32) * (math.log(1000.0) / count))
    angles = level[:, None] * freqs[None, :]
    return jnp.concatenate([jnp.sin(angles), jnp.cos(angles)], axis=1)


def normalize(field):
    centered = field - jnp.mean(field, axis=-1, keepdims=True)
    spread = jnp.mean(centered * centered, axis=-1, keepdims=True)
    inverse = lax.rsqrt(spread + EPSILON)
    return (centered * inverse, inverse)


def norm_backward(grad_scaled, normed, inverse, scale):
    grad_normed = grad_scaled * scale
    grad_scale = jnp.sum(grad_scaled * normed, axis=1)
    inner = jnp.mean(grad_normed * normed, axis=-1, keepdims=True)
    grad_field = inverse * (
        grad_normed - jnp.mean(grad_normed, axis=-1, keepdims=True) - normed * inner
    )
    return (grad_field, grad_scale)


def rotate(field, cosine, sine):
    half = HD // 2
    first = field[..., :half]
    second = field[..., half:]
    return jnp.concatenate(
        [first * cosine - second * sine, second * cosine + first * sine], axis=-1
    )


def rotary_tables(places):
    half = HD // 2
    inverse = jnp.exp(jnp.arange(half, dtype=jnp.float32) * (-math.log(10000.0) / half))
    angle = places[:, None] * inverse[None, :]
    return (jnp.cos(angle)[:, None, None, :], jnp.sin(angle)[:, None, None, :])


def pack_heads(h_one, qkv_weight, cosine, sine):
    seqs, rows, width = h_one.shape
    raw = jnp.einsum("std,de->ste", h_one, qkv_weight, preferred_element_type=jnp.float32)
    local_heads = qkv_weight.shape[1] // (3 * HD)
    raw = raw.reshape(seqs, rows, local_heads, 3, HD)
    turned = rotate(raw[:, :, :, 0:2], cosine, sine)
    packed = jnp.concatenate([turned, raw[:, :, :, 2:3]], axis=3).astype(jnp.bfloat16)
    return packed.reshape(seqs, rows, local_heads * 3 * HD)


def unpack_grads(grad_packed, cosine, sine):
    seqs, rows, width = grad_packed.shape
    local_heads = width // (3 * HD)
    grad_fields = grad_packed.reshape(seqs, rows, local_heads, 3, HD).astype(jnp.float32)
    unturned = rotate(grad_fields[:, :, :, 0:2], cosine, -sine)
    grad_raw = jnp.concatenate([unturned, grad_fields[:, :, :, 2:3]], axis=3).astype(jnp.bfloat16)
    return grad_raw.reshape(seqs, rows, width)


def gelu_slope(upper):
    return 0.5 * (1.0 + lax.erf(upper * ROOT_HALF)) + upper * DENSITY * jnp.exp(
        -0.5 * upper * upper
    )


def attend_sequence(fields):
    local_heads = fields.shape[1]
    block = min(512, LEN)
    count = LEN // block
    keys = fields[:, :, 1]
    values = fields[:, :, 2]
    query_blocks = fields[:, :, 0].reshape(count, block, local_heads, HD)

    def attend_one_block(query_blk):
        scores = jnp.einsum(
            "qhd,khd->hqk", query_blk, keys, preferred_element_type=jnp.float32
        ) * HD ** (-0.5)
        top = jnp.max(scores, axis=-1, keepdims=True)
        expo = jnp.exp(scores - top)
        totals = jnp.sum(expo, axis=-1, keepdims=True)
        probs = (expo / totals).astype(jnp.bfloat16)
        result = jnp.einsum("hqk,khd->qhd", probs, values, preferred_element_type=jnp.float32)
        return (result.astype(jnp.bfloat16), (top + jnp.log(totals))[:, :, 0])

    results, logsums = lax.map(attend_one_block, query_blocks)
    logsums = jnp.transpose(logsums, (1, 0, 2)).reshape(local_heads, LEN)
    return (results.reshape(LEN, local_heads, HD), logsums)


def attend_all(packed_heads):
    items = packed_heads.shape[0]
    local_heads = packed_heads.shape[2] // (3 * HD)
    fields = packed_heads.reshape(items, LEN, local_heads, 3, HD)
    results, logsums = lax.map(attend_sequence, fields)
    return (results.reshape(items, LEN, local_heads * HD), logsums)


def back_sequence(pieces):
    fields, logsums, grad_heads = pieces
    local_heads = fields.shape[1]
    block = min(512, LEN)
    count = LEN // block
    keys = fields[:, :, 1]
    values = fields[:, :, 2]
    query_blocks = fields[:, :, 0].reshape(count, block, local_heads, HD)
    grad_blocks = grad_heads.reshape(count, block, local_heads, HD)
    sum_blocks = jnp.transpose(logsums.reshape(local_heads, count, block), (1, 0, 2))

    def back_one_block(carry, piece):
        key_acc, value_acc = carry
        query_blk, grad_blk, sum_blk = piece
        scores = jnp.einsum(
            "qhd,khd->hqk", query_blk, keys, preferred_element_type=jnp.float32
        ) * HD ** (-0.5)
        probs = jnp.exp(scores - sum_blk[:, :, None])
        grad_probs = jnp.einsum(
            "qhd,khd->hqk", grad_blk, values, preferred_element_type=jnp.float32
        )
        inner = jnp.sum(probs * grad_probs, axis=-1, keepdims=True)
        grad_scores = (probs * (grad_probs - inner)).astype(jnp.bfloat16)
        grad_query = jnp.einsum(
            "hqk,khd->qhd", grad_scores, keys, preferred_element_type=jnp.float32
        ) * HD ** (-0.5)
        key_acc = key_acc + jnp.einsum(
            "hqk,qhd->khd", grad_scores, query_blk, preferred_element_type=jnp.float32
        ) * HD ** (-0.5)
        value_acc = value_acc + jnp.einsum(
            "hqk,qhd->khd", probs.astype(jnp.bfloat16), grad_blk, preferred_element_type=jnp.float32
        )
        return ((key_acc, value_acc), grad_query)

    empty = jnp.zeros((LEN, local_heads, HD), jnp.float32)
    (grad_keys, grad_values), grad_queries = lax.scan(
        back_one_block, (empty, empty), (query_blocks, grad_blocks, sum_blocks)
    )
    grad_queries = grad_queries.reshape(LEN, local_heads, HD)
    return jnp.stack([grad_queries, grad_keys, grad_values], axis=2).astype(jnp.bfloat16)


def back_all(packed_heads, logsums, grad_heads):
    items = packed_heads.shape[0]
    local_heads = packed_heads.shape[2] // (3 * HD)
    fields = packed_heads.reshape(items, LEN, local_heads, 3, HD)
    grads = grad_heads.reshape(items, LEN, local_heads, HD)
    result = lax.map(back_sequence, (fields, logsums, grads))
    return result.reshape(items, LEN, local_heads * 3 * HD)


def data_layer(
    tokens, cotangent, w_qkv, w_up, w_out, w_down, scale_one, scale_two, norm_one, inverse_one
):
    seqs, local_len, width = tokens.shape
    wide = (
        lax.all_gather(w_qkv, "seq", axis=1, tiled=True),
        lax.all_gather(w_up, "seq", axis=1, tiled=True),
        lax.all_gather(w_out, "seq", axis=0, tiled=True),
        lax.all_gather(w_down, "seq", axis=0, tiled=True),
    )
    full_qkv, full_up, full_out, full_down = (
        lax.all_gather(wide[0], "dp", axis=0, tiled=True),
        lax.all_gather(wide[1], "dp", axis=0, tiled=True),
        lax.all_gather(wide[2], "dp", axis=1, tiled=True),
        lax.all_gather(wide[3], "dp", axis=1, tiled=True),
    )
    field = tokens.astype(jnp.float32)
    h_one = (norm_one * scale_one).astype(jnp.bfloat16)
    places = (lax.axis_index("seq") * local_len + jnp.arange(local_len, dtype=jnp.int32)).astype(
        jnp.float32
    )
    cosine, sine = rotary_tables(places)
    packed = pack_heads(h_one, full_qkv, cosine, sine)
    packed_heads = lax.all_to_all(packed, "seq", split_axis=2, concat_axis=1, tiled=True)
    results, logsums = attend_all(packed_heads)
    back_tokens = lax.all_to_all(results, "seq", split_axis=1, concat_axis=2, tiled=True)
    middle = field + jnp.einsum(
        "std,de->ste", back_tokens, full_out, preferred_element_type=jnp.float32
    )
    norm_two, inverse_two = normalize(middle)
    h_two = (norm_two * scale_two).astype(jnp.bfloat16)
    upper = jnp.einsum("std,df->stf", h_two, full_up, preferred_element_type=jnp.float32)
    active = jax.nn.gelu(upper, approximate=False).astype(jnp.bfloat16)
    output = (
        middle + jnp.einsum("stf,fd->std", active, full_down, preferred_element_type=jnp.float32)
    ).astype(jnp.bfloat16)
    grad_down = jnp.einsum("stf,std->fd", active, cotangent, preferred_element_type=jnp.float32)
    grad_active = jnp.einsum(
        "std,fd->stf", cotangent, full_down, preferred_element_type=jnp.float32
    )
    grad_upper = (grad_active * gelu_slope(upper)).astype(jnp.bfloat16)
    grad_up = jnp.einsum("std,stf->df", h_two, grad_upper, preferred_element_type=jnp.float32)
    grad_htwo = jnp.einsum("stf,df->std", grad_upper, full_up, preferred_element_type=jnp.float32)
    grad_middle, grad_scale_two = norm_backward(grad_htwo, norm_two, inverse_two, scale_two)
    grad_middle = grad_middle + cotangent.astype(jnp.float32)
    grad_branch = grad_middle.astype(jnp.bfloat16)
    grad_out = jnp.einsum(
        "std,ste->de", back_tokens, grad_branch, preferred_element_type=jnp.float32
    )
    grad_attended = jnp.einsum(
        "ste,de->std", grad_branch, full_out, preferred_element_type=jnp.float32
    ).astype(jnp.bfloat16)
    grad_heads = lax.all_to_all(grad_attended, "seq", split_axis=2, concat_axis=1, tiled=True)
    grad_packed_heads = back_all(packed_heads, logsums, grad_heads)
    grad_packed = lax.all_to_all(grad_packed_heads, "seq", split_axis=1, concat_axis=2, tiled=True)
    grad_raw = unpack_grads(grad_packed, cosine, sine)
    grad_qkv = jnp.einsum("std,ste->de", h_one, grad_raw, preferred_element_type=jnp.float32)
    grad_hone = jnp.einsum("ste,de->std", grad_raw, full_qkv, preferred_element_type=jnp.float32)
    grad_field, grad_scale_one = norm_backward(grad_hone, norm_one, inverse_one, scale_one)
    grad_tokens = (grad_middle + grad_field).astype(jnp.bfloat16)
    partial_sums = (
        lax.psum_scatter(
            grad_qkv.astype(jnp.bfloat16), "dp", scatter_dimension=0, tiled=True
        ).astype(jnp.float32),
        lax.psum_scatter(
            grad_up.astype(jnp.bfloat16), "dp", scatter_dimension=0, tiled=True
        ).astype(jnp.float32),
        lax.psum_scatter(
            grad_out.astype(jnp.bfloat16), "dp", scatter_dimension=1, tiled=True
        ).astype(jnp.float32),
        lax.psum_scatter(
            grad_down.astype(jnp.bfloat16), "dp", scatter_dimension=1, tiled=True
        ).astype(jnp.float32),
    )
    sums = (
        lax.psum_scatter(
            partial_sums[0].astype(jnp.bfloat16), "seq", scatter_dimension=1, tiled=True
        ).astype(jnp.float32),
        lax.psum_scatter(
            partial_sums[1].astype(jnp.bfloat16), "seq", scatter_dimension=1, tiled=True
        ).astype(jnp.float32),
        lax.psum_scatter(
            partial_sums[2].astype(jnp.bfloat16), "seq", scatter_dimension=0, tiled=True
        ).astype(jnp.float32),
        lax.psum_scatter(
            partial_sums[3].astype(jnp.bfloat16), "seq", scatter_dimension=0, tiled=True
        ).astype(jnp.float32),
    )
    return (output, grad_tokens, grad_scale_one, grad_scale_two, sums)


def shards(tokens, bins, plan, w_qkv, w_out, w_up, w_down, w_time, cotangent):
    feats = time_features(plan, bins).astype(jnp.bfloat16)
    full_time = lax.all_gather(w_time, ("dp", "seq"), axis=0, tiled=True)
    modul = jnp.dot(feats, full_time, preferred_element_type=jnp.float32)
    scale_one = 1.0 + modul[:, None, :D]
    scale_two = 1.0 + modul[:, None, D:]
    norm_one, inverse_one = normalize(tokens.astype(jnp.float32))
    output, grad_tokens, grad_scale_one, grad_scale_two, sums = data_layer(
        tokens, cotangent, w_qkv, w_up, w_out, w_down, scale_one, scale_two, norm_one, inverse_one
    )
    grad_scales = jnp.concatenate([grad_scale_one, grad_scale_two], axis=1)
    grad_time = jnp.dot(feats.astype(jnp.float32).T, grad_scales, precision=HIGHEST)
    time_sum = lax.psum_scatter(grad_time, ("dp", "seq"), scatter_dimension=0, tiled=True)
    return (output, grad_tokens, sums[0], sums[2], sums[1], sums[3], time_sum)


BF = jnp.bfloat16
F32 = jnp.float32
MESHID = pl.DeviceIdType.MESH
QUERY_SCALE = HD**-0.5 / math.log(2.0)
VMEM_LIMIT = 60 * 1024 * 1024


def mm(a, b):
    return lax.dot_general(a, b, (((1,), (0,)), ((), ())), preferred_element_type=F32)


def mm_nt(a, b):
    return lax.dot_general(a, b, (((1,), (1,)), ((), ())), preferred_element_type=F32)


def mm_tn(a, b):
    return lax.dot_general(a, b, (((0,), (0,)), ((), ())), preferred_element_type=F32)


def peers():
    g = lax.axis_index("dp")
    s = lax.axis_index("seq")
    core = lax.rem(s, 2)
    return g, s, core, s + 1 - 2 * core, lax.rem(s + 2, 4), 3 - s


def remote(src, dst, ss, rs, i, dev):
    return pltpu.make_async_remote_copy(
        src_ref=src,
        dst_ref=dst,
        send_sem=ss.at[i],
        recv_sem=rs.at[i],
        device_id=dev,
        device_id_type=MESHID,
    )


def greet(devices):
    barrier = pltpu.get_barrier_semaphore()
    for dev in devices:
        pl.semaphore_signal(barrier, inc=1, device_id=dev, device_id_type=MESHID)
    pl.semaphore_wait(barrier, len(devices))


def moments(field):
    centered = field - jnp.mean(field, axis=-1, keepdims=True)
    spread = jnp.mean(centered * centered, axis=-1, keepdims=True)
    inverse = lax.rsqrt(spread + EPSILON)
    return centered * inverse, inverse


def ring_place(g):
    z, y = g // 2, lax.rem(g, 2)
    return z + y * (7 - 2 * z)


def ring_index(p):
    p = lax.rem(p + 16, 8)
    return 2 * p + (p // 4) * (15 - 4 * p)


WAYS = (1, -1)


class Gather:
    def __init__(self, own, view, ss, rs, first):
        self.own, self.view, self.ss, self.rs, self.first = own, view, ss, rs, first

    def hop(self, k, way):
        g, s = lax.axis_index("dp"), lax.axis_index("seq")
        p = ring_place(g)
        j = ring_index(p - way * (k - 1))
        half = None if k < 4 else (0 if way > 0 else 1)
        dst = self.view(j, half)
        src = self.own if k == 1 else dst
        i = self.first + 2 * (k - 1) + (way < 0)
        return remote(src, dst, self.ss, self.rs, i, (ring_index(p + way), s))

    def start(self):
        for way in WAYS:
            self.hop(1, way).start()

    def forward(self, k):
        for way in WAYS:
            self.hop(k - 1, way).wait_recv()
            self.hop(k, way).start()

    def arrive(self):
        for way in WAYS:
            self.hop(4, way).wait_recv()

    def drain(self):
        for k in (1, 2, 3, 4):
            for way in WAYS:
                self.hop(k, way).wait_send()


class Scatter:
    def __init__(self, view, halves, wholes, ss, rs, first):
        self.view, self.halves, self.wholes = view, halves, wholes
        self.ss, self.rs, self.first = ss, rs, first

    def hop(self, k, way):
        g, s = lax.axis_index("dp"), lax.axis_index("seq")
        p = ring_place(g)
        side = 0 if way > 0 else 1
        j = ring_index(p + way * (5 - k))
        src = self.view(j, side if k == 1 else None)
        dst = self.halves.at[side] if k == 1 else self.wholes.at[3 * side + k - 2]
        i = self.first + 2 * (k - 1) + side
        return remote(src, dst, self.ss, self.rs, i, (ring_index(p + way), s))

    def start(self):
        for way in WAYS:
            self.hop(1, way).start()

    def forward(self, k):
        p = ring_place(lax.axis_index("dp"))
        for way in WAYS:
            side = 0 if way > 0 else 1
            self.hop(k - 1, way).wait_recv()
            got = self.halves.at[side] if k == 2 else self.wholes.at[3 * side + k - 3]
            mine = self.view(ring_index(p + way * (5 - k)), side if k == 2 else None)
            mine[...] = (mine[...].astype(F32) + got[...].astype(F32)).astype(BF)
            self.hop(k, way).start()

    def result(self):
        for way in WAYS:
            self.hop(4, way).wait_recv()
        mine = self.view(lax.axis_index("dp"), None)
        return mine[...].astype(F32) + (self.wholes[2].astype(F32) + self.wholes[5].astype(F32))

    def drain(self):
        for k in (1, 2, 3, 4):
            for way in WAYS:
                self.hop(k, way).wait_send()


def rows_of(ref, half, size):
    return ref if half is None else ref.at[half * (size // 2) : (half + 1) * (size // 2)]


def ordering(heads):
    half, size = HD // 2, heads * HD
    to = lax.broadcasted_iota(jnp.int32, (1, 3 * size), 1)
    part, at = to // size, lax.rem(to, size)
    side, rest = at // (size // 2), lax.rem(at, size // 2)
    turned = (rest // half) * (3 * HD) + part * HD + side * half + lax.rem(rest, half)
    plain = (at // HD) * (3 * HD) + 2 * HD + lax.rem(at, HD)
    source = jnp.where(part == 2, plain, turned)
    rows = lax.broadcasted_iota(jnp.int32, (3 * size, 3 * size), 0)
    return jnp.where(rows == source, 1.0, 0.0).astype(BF)


def k1_body(
    tok, wt, feats, w_qkv, w_out, w_up, w_down, cs, sn, cot,
    modul, feats_out, wq_out, out_all, up_all, down_all, n_out, qkv_out, lse, attn_heads, attn_rows, cot_all,
    act_out, slope_out, htwo_out, mid_out,
    tokv, wtime, pbuf, vt, cotv, wq, nv, qkv, attn, outv, upv, act, slope, htwo, mids, csv, snv,
    ks, ls, ss, rs, gs, gr, fs_, fr_, os_,
):
    g, s, core, s1, s2, s3 = peers()
    p = ring_place(g)
    nb, tl = tok.shape[0], tok.shape[1]
    rows = 4 * tl
    blk = 256
    nq = rows // blk
    heads = attn.shape[3] // HD
    nr, nc = w_out.shape[0], w_out.shape[1]

    def lanes(j, size):
        return pl.ds(pl.multiple_of(j * size, size), size)

    def view_out(other):
        def view(j, half):
            lo, size = (0, nr) if half is None else (half * (nr // 2), nr // 2)
            return outv.at[pl.ds(pl.multiple_of(other * nr + lo, size), size), lanes(j, nc)]

        return view

    def view_down(j, half):
        size = w_down.shape[0]
        lo, n = (0, size) if half is None else (half * (size // 2), size // 2)
        return down_all.at[lo : lo + n, lanes(j, w_down.shape[1])]

    def view_rows(ref, size):
        def view(j, half):
            lo, n = (0, size) if half is None else (half * (size // 2), size // 2)
            return ref.at[pl.ds(pl.multiple_of(j * size + lo, n), n)]

        return view

    def view_time(j, half):
        return wtime.at[j] if half is None else wtime.at[j, :, half * D : (half + 1) * D]

    def view_qkv(side):
        size = w_qkv.shape[0]

        def view(j, half):
            lo, n = (0, size // 2) if half is None else (half * (size // 4), size // 4)
            at = pl.multiple_of(j * size + side * (size // 2) + lo, n)
            return wq.at[pl.ds(at, n)]

        return view

    here = view_out(s)(g, None)
    time_ring = Gather(wt, view_time, gs, gr, 0)
    part = w_qkv.shape[0] // 2
    qkv_rings = [
        Gather(view_qkv(i)(g, None), view_qkv(i), gs, gr, 8 + 40 * i)
        for i in range(2)
    ]
    up_ring = Gather(w_up, view_rows(upv, w_up.shape[0]), gs, gr, 16)
    down_ring = Gather(w_down, view_down, gs, gr, 24)
    out_ring = Gather(w_out, view_out(s), gs, gr, 32)
    far_ring = Gather(view_out(s2)(g, None), view_out(s2), gs, gr, 40)

    local = [
        pltpu.make_async_copy(tok, tokv.at[:, s], ls.at[0]),
        pltpu.make_async_copy(cot, cotv, ls.at[5]),
        pltpu.make_async_copy(w_up, view_rows(upv, w_up.shape[0])(g, None), ls.at[2]),
        pltpu.make_async_copy(w_down, view_down(g, None), ls.at[3]),
        pltpu.make_async_copy(w_out, here, ls.at[4]),
        pltpu.make_async_copy(cs, csv, ls.at[6]),
        pltpu.make_async_copy(sn, snv, ls.at[7]),
    ]
    greet([(g, s1), (g, s2), (g, s3), (ring_index(p + 1), s), (ring_index(p - 1), s)])
    time_ring.start()
    pair_out = remote(w_out, here, ss, rs, 0, (g, s2))
    pair_out.start()
    far = [remote(tok.at[b], tokv.at[b, s], ss, rs, 1 + b, (g, s2)) for b in range(nb)]
    far[0].start()
    ordered = mm(w_qkv[...], ordering(heads)).astype(BF)
    wq[pl.ds(pl.multiple_of(g * w_qkv.shape[0], w_qkv.shape[0]), w_qkv.shape[0])] = ordered
    for ring in qkv_rings:
        ring.start()
    near = []
    for b in range(nb):
        cp = remote(tok.at[b], tokv.at[b, s], ss, rs, 3 + b, (g, s1))
        cp.start()
        near.append(cp)
    for cp in local:
        cp.start()
    wtime[g] = wt[...]
    pieces = [(0, 0, tl // 4), (0, tl // 4, tl)] + [(b, 0, tl) for b in range(1, nb)]

    def cot_piece(k):
        b, lo, hi = pieces[k]
        return remote(
            cotv.at[b, lo:hi], cot_all.at[b, s, lo:hi], ss, rs, 18 + k, (g, s2)
        )

    local[1].wait()
    cot_far = [cot_piece(k) for k in range(len(pieces))]
    cot_far[0].start()
    for k in (2, 3, 4):
        time_ring.forward(k)
        for ring in qkv_rings:
            ring.forward(k)
    up_ring.start()
    out_ring.start()
    pair_out.wait_recv()
    far_ring.start()
    time_ring.arrive()
    depth = wt.shape[0]
    feats_out[...] = feats[...]
    lane_t = lax.broadcasted_iota(jnp.int32, (depth, TF), 1)
    row_t = lax.broadcasted_iota(jnp.int32, (depth, TF), 0)
    sums = [jnp.zeros((depth, 2 * D), F32) for _ in range(nb)]
    for d in range(wtime.shape[0]):
        hit = lane_t == row_t + (4 * d + s) * depth
        weights = wtime[d].astype(F32)
        for b in range(nb):
            column = jnp.sum(jnp.where(hit, feats[b : b + 1], 0.0), axis=1, keepdims=True)
            sums[b] = sums[b] + weights * column
    pbuf[0] = jnp.concatenate([jnp.sum(v, axis=0, keepdims=True) for v in sums], axis=0)
    small = []
    for e, other in ((1, s1), (2, s2), (3, s3)):
        cp = remote(pbuf.at[0], pbuf.at[e], ss, rs, 4 + e, (g, other))
        cp.start()
        small.append(cp)
    far[1].start()
    cot_far[1].start()
    passed = [
        remote(tokv.at[b, s2], tokv.at[b, s2], ss, rs, 8 + b, (g, s1)) for b in range(nb)
    ]
    cot_near = [remote(cotv.at[b], cot_all.at[b, s], ss, rs, 12 + b, (g, s1)) for b in range(nb)]
    cot_pass = [
        remote(cot_all.at[b, s2], cot_all.at[b, s2], ss, rs, 14 + b, (g, s1)) for b in range(nb)
    ]
    far[0].wait_recv()
    passed[0].start()
    for c in small:
        c.wait_recv()
    modul[...] = (pbuf[0] + pbuf[1]) + (pbuf[2] + pbuf[3])
    for ring in qkv_rings:
        ring.arrive()
    for i in (0, 5, 6):
        local[i].wait()
    keep_w = pltpu.make_async_copy(wq, wq_out, ls.at[8])
    keep_w.start()
    keep_cot = pltpu.make_async_copy(cotv, cot_all.at[:, s], ls.at[9])
    keep_cot.start()

    def attn_copy(kind, it):
        b, q = it // nq, lax.rem(it, nq)
        r = pl.ds(pl.multiple_of(q * blk, blk), blk)
        ref = attn.at[b, s2 if kind == 2 else s, r]
        return remote(ref, ref, fs_.at[kind], fr_.at[kind], it, (g, s2 if kind == 0 else s1))

    lane = lax.broadcasted_iota(jnp.int32, (1, 2 * 128), 1)

    def keep_fields(b):
        return (
            pltpu.make_async_copy(nv.at[b], n_out.at[b], ks.at[0, b]),
            pltpu.make_async_copy(qkv.at[b], qkv_out.at[b], ks.at[1, b]),
        )

    def project(b):
        scale = 1.0 + modul[pl.ds(b, 1), :D]

        def one(i, _):
            r = pl.ds(pl.multiple_of(i * blk, blk), blk)
            normed, _inv = moments(tokv[b, i].astype(F32))
            nv[b, r] = normed.astype(BF)
            raw = mm((normed * scale).astype(BF), wq[...])
            c, n = csv[r], snv[r]
            qa, qb = raw[:, :128] * QUERY_SCALE, raw[:, 128:256] * QUERY_SCALE
            ka, kb = raw[:, 256:384], raw[:, 384:512]
            qkv[b, 0, r] = jnp.concatenate([qa * c - qb * n, qb * c + qa * n], axis=1).astype(BF)
            qkv[b, 1, r] = jnp.concatenate([ka * c - kb * n, kb * c + ka * n], axis=1).astype(BF)
            qkv[b, 2, r] = raw[:, 512:].astype(BF)
            return 0

        lax.fori_loop(0, nq, one, 0)

    def pass_attn(lo, hi):
        def forward(it, _):
            attn_copy(0, it).wait_recv()
            attn_copy(2, it).start()
            return 0

        lax.fori_loop(lo, hi, forward, 0)

    def arrive_attn(lo, hi):
        def forward(it, _):
            attn_copy(1, it).wait_recv()
            attn_copy(2, it).wait_recv()
            return 0

        lax.fori_loop(lo, hi, forward, 0)

    def tokens_of(b):
        near[b].wait_recv()
        passed[b].wait_recv()

    def second_tokens():
        far[1].wait_recv()
        passed[1].start()

    def step(it, _):
        b, q = it // nq, lax.rem(it, nq)
        for i in range(nb):

            @pl.when(it == i * nq)
            def _(i=i):
                tokens_of(i)

        def at(events):
            for when, action in events:

                @pl.when(it == when)
                def _(action=action):
                    action()

        def up_out(k):
            up_ring.forward(k)
            out_ring.forward(k)
            far_ring.forward(k)

        at(((4, lambda: up_out(4)), (4, down_ring.start)))

        @pl.when(q == 0)
        def _():
            project(b)
            vt[...] = qkv[b, 2].T
            for cp in keep_fields(b):
                cp.start()

        at(
            (
                (0, lambda: up_out(2)),
                (2, lambda: up_out(3)),
                (2, second_tokens),
                (6, lambda: pass_attn(0, nq)),
                (7, lambda: down_ring.forward(2)),
            )
        )
        r = pl.ds(pl.multiple_of(q * blk, blk), blk)
        query, keys = qkv[b, 0, r], qkv[b, 1]
        outs, stats = [], []
        masked = jnp.concatenate(
            [
                jnp.where(lax.rem(lane, 128) // 32 == h, query, jnp.zeros_like(query))
                for h in range(heads)
            ],
            axis=0,
        )
        both = mm_nt(keys, masked)
        tops = jnp.max(both, axis=0, keepdims=True)
        expo = jnp.exp2(both - tops)
        totals = jnp.sum(expo, axis=0, keepdims=True)
        expo = expo.astype(BF)
        shares = 1.0 / totals
        for h in range(heads):
            c = slice(h * blk, (h + 1) * blk)
            outs.append(mm(vt[h * HD : (h + 1) * HD], expo[:, c]) * shares[:, c])
            stats.append(tops[:, c] + jnp.log2(totals[:, c]))
        attn[b, s, r] = jnp.concatenate(outs, axis=0).T.astype(BF)
        lse[b, :, r] = jnp.concatenate(stats + [jnp.zeros((8 - heads, blk), F32)], axis=0)
        attn_copy(0, it).start()
        attn_copy(1, it).start()
        return 0

    lax.fori_loop(0, nb * nq, step, 0)
    for cp in cot_far[2:] + cot_near:
        cp.start()
    keep = pltpu.make_async_copy(attn.at[:, s], attn_heads, ls.at[10])
    keep.start()
    out_ring.arrive()
    far_ring.arrive()
    local[4].wait()
    cross = []
    for e, other in ((0, s), (1, s2)):
        ref = outv.at[pl.ds(pl.multiple_of(other * nr, nr), nr)]
        cp = remote(ref, ref, ss, rs, 16 + e, (g, s1))
        cp.start()
        cross.append(cp)
    up_ring.arrive()
    local[2].wait()
    for cp in cross:
        cp.wait_recv()
    arrive_attn(0, nq)
    keep_out = pltpu.make_async_copy(outv, out_all, ls.at[11])
    keep_out.start()
    keep_up = pltpu.make_async_copy(upv, up_all, ls.at[12])
    keep_up.start()

    def keep_block(i):
        return (
            pltpu.make_async_copy(act.at[i], act_out.at[i], os_.at[0, i]),
            pltpu.make_async_copy(slope.at[i], slope_out.at[i], os_.at[1, i]),
            pltpu.make_async_copy(htwo.at[i], htwo_out.at[i], os_.at[2, i]),
        )

    def feed(i, _):
        b, owner = i // 4, lax.rem(i, 4)
        for when, action in (
            (1, lambda: down_ring.forward(3)),
            (3, lambda: pass_attn(nq, 2 * nq)),
            (4, lambda: arrive_attn(nq, 2 * nq)),
            (4, lambda: down_ring.forward(4)),
        ):

            @pl.when(i == when)
            def _(action=action):
                action()

        scale = 1.0 + modul[pl.ds(b, 1), D:]
        r = pl.ds(pl.multiple_of(owner * tl, tl), tl)
        joined = jnp.concatenate([attn[b, j, r] for j in range(4)], axis=1)
        mid = tokv[b, owner].astype(F32) + mm(joined, outv[...])
        normed, _inv = moments(mid)
        h = (normed * scale).astype(BF)
        upper = mm(h, upv[...])
        phi = 0.5 * (1.0 + lax.erf(upper * ROOT_HALF))
        act[i] = (upper * phi).astype(BF)
        slope[i] = (phi + upper * (DENSITY * jnp.exp(-0.5 * upper * upper))).astype(BF)
        htwo[i] = h

        @pl.when(owner == s)
        def _():
            mids[b] = mid

        for cp in keep_block(i):
            cp.start()
        return 0

    lax.fori_loop(0, 4 * nb, feed, 0)
    keep_mid = pltpu.make_async_copy(mids, mid_out, ls.at[13])
    keep_mid.start()
    own_rows = pl.ds(pl.multiple_of(s * tl, tl), tl)
    keep_rows = pltpu.make_async_copy(attn.at[:, :, own_rows], attn_rows, ls.at[14])
    keep_rows.start()
    for b in range(nb):
        for k, piece in enumerate(pieces):
            if piece[0] == b:
                cot_far[k].wait_recv()
        cot_pass[b].start()

    def finish(it, _):
        attn_copy(0, it).wait_send()
        attn_copy(1, it).wait_send()
        attn_copy(2, it).wait_send()
        return 0

    lax.fori_loop(0, nb * nq, finish, 0)

    def kept(i, _):
        for cp in keep_block(i):
            cp.wait()
        return 0

    lax.fori_loop(0, 4 * nb, kept, 0)
    down_ring.arrive()
    for cp in cot_near + cot_pass:
        cp.wait()
    for cp in cot_far + far + near + passed + small + cross + [pair_out]:
        cp.wait_send()
    for ring in [time_ring, up_ring, down_ring, out_ring, far_ring] + qkv_rings:
        ring.drain()
    local[3].wait()
    for cp in (keep_cot, keep, keep_w, keep_out, keep_up, keep_mid, keep_rows):
        cp.wait()
    for b in range(nb):
        for cp in keep_fields(b):
            cp.wait()


def run_k1(nd, tokens, w_time, feats, w_qkv, w_out, w_up, w_down, cs, sn, cot):
    nb, tl, width = tokens.shape
    rows = 4 * tl
    cols = w_qkv.shape[1] // 3
    hidden = w_up.shape[1]
    vm = pl.BlockSpec(memory_space=pltpu.VMEM)
    hb = pl.BlockSpec(memory_space=pl.ANY)
    steps = nb * (rows // 256)
    sds = jax.ShapeDtypeStruct
    dma = pltpu.SemaphoreType.DMA
    v = pltpu.VMEM
    return pl.pallas_call(
        k1_body,
        out_shape=(
            sds((nb, 2 * width), F32),
            sds((nb, TF), F32),
            sds((width, 3 * cols), BF),
            sds((width, width), BF),
            sds((width, hidden), BF),
            sds((hidden, width), BF),
            sds((nb, rows, width), BF),
            sds((nb, 3, rows, cols), BF),
            sds((nb, 8, rows), F32),
            sds((nb, rows, cols), BF),
            sds((nb, 4, tl, cols), BF),
            sds((nb, 4, tl, width), BF),
            sds((4 * nb, tl, hidden), BF),
            sds((4 * nb, tl, hidden), BF),
            sds((4 * nb, tl, width), BF),
            sds((nb, tl, width), F32),
        ),
        in_specs=[hb, vm, vm, vm, vm, vm, vm, hb, hb, hb],
        out_specs=(vm, vm, hb, hb, hb, hb, hb, hb, vm) + (hb,) * 7,
        scratch_shapes=[
            v((nb, 4, tl, width), BF),
            v((nd,) + w_time.shape, BF),
            v((4, nb, 2 * width), F32),
            v((cols, rows), BF),
            v((nb, tl, width), BF),
            v((width, 3 * cols), BF),
            v((nb, rows, width), BF),
            v((nb, 3, rows, cols), BF),
            v((nb, 4, rows, cols), BF),
            v((width, width), BF),
            v((width, hidden), BF),
            v((4 * nb, tl, hidden), BF),
            v((4 * nb, tl, hidden), BF),
            v((4 * nb, tl, width), BF),
            v((nb, tl, width), F32),
            v(cs.shape, F32),
            v(sn.shape, F32),
            dma((2, nb)),
            dma((15,)),
            dma((22,)),
            dma((22,)),
            dma((56,)),
            dma((56,)),
            dma((3, steps)),
            dma((3, steps)),
            dma((3, 4 * nb)),
        ],
        compiler_params=pltpu.CompilerParams(
            collective_id=0, has_side_effects=True, vmem_limit_bytes=VMEM_LIMIT
        ),
        name="attention_forward",
    )(tokens, w_time, feats, w_qkv, w_out, w_up, w_down, cs, sn, cot)


def k2_body(
    act_h, slope_h, htwo_h, mid_h, attn_h, cot_h, modul, w_out_h, w_up_h, w_down_h,
    grad_up, grad_out, d_mid_h, base_h, osend_h, d_heads, dsc, s_down,
    act, dup, htwo, mids, attn, cot, w_out, w_up, w_down, d_mid, base, osend,
    pa, pb_, ra, rb, xs, xr, dat, stage, gdv, down_h, down_w,
    ls, ss, rs, os_, ins, keeps, bs, gs, gr,
):
    g, s, core, s1, s2, s3 = peers()
    p = ring_place(g)
    chip = s // 2
    nb, tl = cot.shape[0], cot.shape[2]

    def pull(jp, which):
        phase, b = jp // nb, lax.rem(jp, nb)
        where = chip + (1 - phase) * (1 - 2 * chip)
        owner = 2 * where + (1 - core if which == 0 else core)
        i = b * 4 + owner
        k = 2 * jp + which
        return (
            pltpu.make_async_copy(cot_h.at[b, owner], cot.at[b, owner], bs.at[0, k]),
            pltpu.make_async_copy(slope_h.at[i], dup.at[i], bs.at[1, k]),
            pltpu.make_async_copy(act_h.at[i], act.at[i], bs.at[2, k]),
        )

    loads = []
    for i, (src, dst) in enumerate(
        (
            (w_down_h, w_down), (w_up_h, w_up),
            (mid_h, mids), (w_out_h, w_out), (htwo_h, htwo), (attn_h, attn),
        )
    ):
        loads.append(pltpu.make_async_copy(src, dst, ins.at[i]))
    first = pull(0, 0)
    loads[0].start()
    for cp in first:
        cp.start()
    loads[1].start()
    for jp in range(2 * nb):
        for which in (0, 1):
            if jp + which:
                for cp in pull(jp, which):
                    cp.start()
    for cp in loads[2:]:
        cp.start()
    greet([(g, s1), (g, s2), (g, s3), (ring_index(p + 1), s), (ring_index(p - 1), s)])
    hidden = act.shape[2]
    pc = s_down.shape[1]

    def view_down(j, half):
        lo, n = (0, hidden) if half is None else (half * (hidden // 2), hidden // 2)
        return gdv.at[lo : lo + n, pl.ds(pl.multiple_of(j * pc, pc), pc)]

    down_ring = Scatter(view_down, down_h, down_w, gs, gr, 0)

    def back_part(b, owner):
        i = b * 4 + owner
        d_act = mm_nt(cot[b, owner], w_down[...])
        d_up = (d_act * dup[i].astype(F32)).astype(BF)
        dup[i] = d_up
        return mm_nt(d_up, w_up[...])

    def back_copy(jp):
        return remote(pa.at[jp], ra.at[jp], ss, rs, jp, (g, s1))

    def out_copy(jp):
        return remote(pb_.at[jp], rb.at[jp], ss, rs, 4 + jp, (g, s1))

    def far_copy(b):
        return remote(xs.at[b], xr.at[b], ss, rs, 8 + b, (g, s2))

    def place(jp):
        phase, b = jp // nb, lax.rem(jp, nb)
        return phase, b, chip + (1 - phase) * (1 - 2 * chip)

    def give(jp, _):
        phase, b, where = place(jp)

        @pl.when(phase == 0)
        def _():
            for cp in pull(jp, 0):
                cp.wait()

        pa[jp] = back_part(b, 2 * where + 1 - core).astype(BF)
        back_copy(jp).start()
        return 0

    def take(jp, _):
        phase, b, where = place(jp)

        @pl.when(phase == 0)
        def _():
            for cp in pull(jp, 1):
                cp.wait()

        dh = back_part(b, 2 * where + core)
        back_copy(jp).wait_recv()
        dh = dh + ra[jp].astype(F32)

        @pl.when(phase == 0)
        def _():
            xs[b] = dh.astype(BF)
            far_copy(b).start()

        @pl.when(phase == 1)
        def _():
            d_mid[b] = dh

        return 0

    def give_out(jp, _):
        _phase, b, where = place(jp)
        pb_[jp] = mm(act[b * 4 + 2 * where + 1 - core], w_down[...]).astype(BF)
        out_copy(jp).start()
        return 0

    def take_out(jp, _):
        phase, b, where = place(jp)
        out = mm(act[b * 4 + 2 * where + core], w_down[...])
        out_copy(jp).wait_recv()
        out = out + rb[jp].astype(F32)

        @pl.when(phase == 0)
        def _():
            osend[b] = out.astype(BF)

        @pl.when(phase == 1)
        def _():
            base[b] = out + mids[b]

        return 0

    def down_grads(i, _):
        r = pl.ds(pl.multiple_of(i * 256, 256), 256)
        left = act[:, :, r].reshape(4 * nb * tl, 256)
        gdv[r] = mm_tn(left, cot[...].reshape(4 * nb * tl, D)).astype(BF)
        return 0

    def up_copy(i):
        r = pl.ds(pl.multiple_of(i * 256, 256), 256)
        return pltpu.make_async_copy(stage.at[i], grad_up.at[r], os_.at[i])

    def up_grads(i, _):
        r = pl.ds(pl.multiple_of(i * 256, 256), 256)
        left = htwo[:, :, r].reshape(4 * nb * tl, 256)
        stage[i] = mm_tn(left, dup[...].reshape(4 * nb * tl, hidden)).astype(BF)
        up_copy(i).start()
        return 0

    def spread(e, other, b):
        return remote(dat.at[other, b], d_heads.at[s, b], ss, rs, 10 + 2 * e + b, (g, other))

    def tail(b, _):
        scale = 1.0 + modul[pl.ds(b, 1), D:]
        far_copy(b).wait_recv()
        dh = d_mid[b] + xr[b].astype(F32)
        normed, inverse = moments(mids[b])
        dsc[pl.ds(b, 1)] = jnp.sum(dh * normed, axis=0, keepdims=True)
        dn = dh * scale
        inner = jnp.mean(dn * normed, axis=-1, keepdims=True)
        dm = cot[b, s].astype(F32) + inverse * (
            dn - jnp.mean(dn, axis=-1, keepdims=True) - normed * inner
        )
        d_mid[b] = dm
        branch = mm_nt(dm.astype(BF), w_out[...]).astype(BF)
        for j in range(4):
            dat[j, b] = branch[:, j * 256 : (j + 1) * 256]
        for e, other in ((0, s2), (1, s3), (2, s1)):
            spread(e, other, b).start()
        return 0

    for cp in loads[:2]:
        cp.wait()
    half = D // 512
    lax.fori_loop(0, nb, give, 0)
    lax.fori_loop(0, nb, take, 0)
    lax.fori_loop(0, nb, give_out, 0)
    lax.fori_loop(0, nb, take_out, 0)
    for jp in range(nb, 2 * nb):
        for which in (0, 1):
            for cp in pull(jp, which):
                cp.wait()
    lax.fori_loop(0, hidden // 256, down_grads, 0)
    down_ring.start()
    for cp in loads[2:]:
        cp.wait()
    lax.fori_loop(nb, 2 * nb, give, 0)
    lax.fori_loop(nb, 2 * nb, take, 0)
    down_ring.forward(2)
    lax.fori_loop(0, nb - 1, tail, 0)
    lax.fori_loop(nb, 2 * nb, give_out, 0)
    lax.fori_loop(nb, 2 * nb, take_out, 0)
    down_ring.forward(3)
    lax.fori_loop(0, half, up_grads, 0)
    lax.fori_loop(nb - 1, nb, tail, 0)
    lax.fori_loop(half, 2 * half, up_grads, 0)
    keep_all = []
    for i, (src, dst) in enumerate(
        ((d_mid, d_mid_h), (base, base_h), (osend, osend_h), (dat.at[s], d_heads.at[s]))
    ):
        cp = pltpu.make_async_copy(src, dst, keeps.at[i])
        cp.start()
        keep_all.append(cp)
    down_ring.forward(4)
    branch = d_mid[...].astype(BF).reshape(nb * tl, D)
    for j in range(4):
        left = jnp.concatenate([attn[b, j] for b in range(nb)], axis=0)
        up_copy(j).wait()
        stage[j] = mm_tn(left, branch).astype(BF)
        pltpu.make_async_copy(stage.at[j], grad_out.at[j], os_.at[j]).start()

    def done(jp, _):
        back_copy(jp).wait_send()
        out_copy(jp).wait_send()
        return 0

    lax.fori_loop(0, 2 * nb, done, 0)
    s_down[...] = down_ring.result()
    down_ring.drain()
    for b in range(nb):
        far_copy(b).wait_send()
        for e, other in ((0, s2), (1, s3), (2, s1)):
            spread(e, other, b).wait()
    for j in range(4):
        pltpu.make_async_copy(stage.at[j], grad_out.at[j], os_.at[j]).wait()
    for cp in keep_all:
        cp.wait()


def run_k2(nd, act, slope, htwo, mid, attn_rows, cot_all, modul, w_out, w_up, w_down):
    nb, _, tl, width = cot_all.shape
    hidden = w_up.shape[1]
    cols = attn_rows.shape[3]
    pc = width // nd
    vm = pl.BlockSpec(memory_space=pltpu.VMEM)
    hb = pl.BlockSpec(memory_space=pl.ANY)
    sds = jax.ShapeDtypeStruct
    v = pltpu.VMEM
    dma = pltpu.SemaphoreType.DMA
    return pl.pallas_call(
        k2_body,
        out_shape=(
            sds((width, hidden), BF),
            sds((4, cols, width), BF),
            sds((nb, tl, width), F32),
            sds((nb, tl, width), F32),
            sds((nb, tl, width), BF),
            sds((4, nb, tl, cols), BF),
            sds((nb, width), F32),
            sds((hidden, pc), F32),
        ),
        in_specs=[hb, hb, hb, hb, hb, hb, vm, hb, hb, hb],
        out_specs=(hb, hb, hb, hb, hb, hb, vm, vm),
        scratch_shapes=[
            v(act.shape, BF),
            v(slope.shape, BF),
            v(htwo.shape, BF),
            v(mid.shape, F32),
            v(attn_rows.shape, BF),
            v(cot_all.shape, BF),
            v(w_out.shape, BF),
            v(w_up.shape, BF),
            v(w_down.shape, BF),
            v((nb, tl, width), F32),
            v((nb, tl, width), F32),
            v((nb, tl, width), BF),
            v((2 * nb, tl, width), BF),
            v((2 * nb, tl, width), BF),
            v((2 * nb, tl, width), BF),
            v((2 * nb, tl, width), BF),
            v((nb, tl, width), BF),
            v((nb, tl, width), BF),
            v((4, nb, tl, cols), BF),
            v((4, 256, width), BF),
            v((hidden, width), BF),
            v((2, hidden // 2, pc), BF),
            v((6, hidden, pc), BF),
            dma,
            dma((16,)),
            dma((16,)),
            dma((4,)),
            dma((6,)),
            dma((4,)),
            dma((3, 4 * nb)),
            dma((8,)),
            dma((8,)),
        ],
        compiler_params=pltpu.CompilerParams(
            collective_id=1, has_side_effects=True, vmem_limit_bytes=VMEM_LIMIT
        ),
        name="feed_forward",
    )(act, slope, htwo, mid, attn_rows, cot_all, modul, w_out, w_up, w_down)


def k3_body(
    fields_h, lse, attn_h, d_heads_h, w_h, normed_h, tok_h, modul, cs_h, sn_h, d_mid_h, base_h, osend,
    g_up, g_out, dsc_h, feats,
    output, grad_tok, s_qkv, s_out, s_up, s_time,
    orecv, dqt, draw, pa, ra, xs, xr, sumh, dhb,
    vu, vo, vq, oa, ob, ox, osum, up_h, up_w, out_h, out_w, qkv_h, qkv_w,
    dpart, tx, dall, qkv, own, d_heads, w, normed_one, tok, cs, sn, d_mid, base, dsc_two,
    ins, ls, ss, rs, gs, gr,
):
    g, s, core, s1, s2, s3 = peers()
    chip = s // 2
    p = ring_place(g)
    nd = dall.shape[0]
    loads = [
        pltpu.make_async_copy(g_up, vu, ls.at[0]),
        pltpu.make_async_copy(g_out, oa, ls.at[1]),
    ]
    pulls = []
    for i, (src, dst) in enumerate(
        (
            (fields_h, qkv), (attn_h, own), (d_heads_h, d_heads), (cs_h, cs), (sn_h, sn),
            (w_h, w), (normed_h, normed_one), (tok_h, tok), (d_mid_h, d_mid), (base_h, base),
            (dsc_h, dsc_two),
        )
    ):
        pulls.append(pltpu.make_async_copy(src, dst, ins.at[i]))
    for cp in pulls[:3]:
        cp.start()
    for cp in loads:
        cp.start()
    for cp in pulls[3:]:
        cp.start()
    others = [(lax.rem(g + d, nd), s) for d in range(1, nd)]
    greet([(g, s1), (g, s2)] + others)
    nb, tl = tok.shape[0], tok.shape[1]
    rows, cols = own.shape[1], own.shape[2]
    heads = cols // HD
    blk = 256
    nk = rows // blk
    pc = D // nd

    def lanes(j, size):
        return pl.ds(pl.multiple_of(j * size, size), size)

    def view_cols(ref, size):
        def view(j, half):
            lo, n = (0, size) if half is None else (half * (size // 2), size // 2)
            return ref.at[lo : lo + n, lanes(j, pc)]

        return view

    def view_rows(ref):
        def view(j, half):
            lo, n = (0, pc) if half is None else (half * (pc // 2), pc // 2)
            return ref.at[pl.ds(pl.multiple_of(j * pc + lo, n), n)]

        return view

    up_ring = Scatter(view_rows(vu), up_h, up_w, gs, gr, 16)
    out_rings = [
        Scatter(view_cols(vo.at[i], vo.shape[1]), out_h.at[i], out_w.at[i], gs, gr, 8 * i)
        for i in range(2)
    ]
    def view_qkv(side):
        wide = vq.shape[1] // 2

        def view(j, half):
            lo, n = (0, pc) if half is None else (half * (pc // 2), pc // 2)
            return vq.at[
                pl.ds(pl.multiple_of(j * pc + lo, n), n), side * wide : (side + 1) * wide
            ]

        return view

    qkv_rings = [
        Scatter(view_qkv(i), qkv_h.at[i], qkv_w.at[i], gs, gr, 24 + 16 * i) for i in range(2)
    ]

    def qkv_forward(k):
        for ring in qkv_rings:
            ring.forward(k)

    loads[0].wait()
    up_ring.start()
    back = []
    for b in range(nb):
        cp = remote(osend.at[b], orecv.at[b], ss, rs, b, (g, s2))
        cp.start()
        back.append(cp)
    loads[1].wait()
    cross = []
    for i in range(2):
        cp = remote(oa.at[2 * i + 1 - core], ob.at[i], ss, rs, 8 + i, (g, s1))
        cp.start()
        cross.append(cp)
    over = remote(osum, ox, ss, rs, 10, (g, s2))

    def out_pair():
        for i in range(2):
            cross[i].wait_recv()
            vo[i] = (oa[2 * i + core].astype(F32) + ob[i].astype(F32)).astype(BF)
            out_rings[i].start()

    def out_forward(k):
        for ring in out_rings:
            ring.forward(k)

    lane = lax.broadcasted_iota(jnp.int32, (1, cols), 1)

    def near_copy(b, phase):
        i = 2 * b + phase
        return remote(pa.at[i], ra.at[i], ss, rs, 2 + i, (g, s1))

    def far_copy(b):
        return remote(xs.at[b], xr.at[b], ss, rs, 6 + b, (g, s2))

    for cp in pulls[:5]:
        cp.wait()
    out_pair()

    def grads(side):
        wide = vq.shape[1] // 2
        c = slice(side * wide, (side + 1) * wide)

        def one(i, _):
            r = pl.ds(pl.multiple_of(i * 256, 256), 256)
            left = jnp.concatenate(
                [
                    (normed_one[b, :, r].astype(F32) * (1.0 + modul[b : b + 1, r])).astype(BF)
                    for b in range(nb)
                ],
                axis=0,
            )
            vq[r, c] = mm_tn(left, draw[:, :, c].reshape(nb * rows, wide)).astype(BF)
            return 0

        lax.fori_loop(0, D // 256, one, 0)
        qkv_rings[side].start()

    def sequence(b, _):
        for j in range(4):
            dhb[j * tl : (j + 1) * tl] = d_heads[j, b]
        query = qkv[b, 0]
        d_out = dhb[...]
        prod = d_out.astype(F32) * own[b].astype(F32)
        prod = prod.T
        delta = jnp.concatenate(
            [jnp.sum(prod[h * HD : (h + 1) * HD], axis=0, keepdims=True) for h in range(heads)],
            axis=0,
        )
        dqt[...] = jnp.zeros_like(dqt)

        def keys_block(i, _):
            it = b * nk + i
            for when, act in (
                (2, lambda: up_ring.forward(2)),
                (3, lambda: out_forward(2)),
                (4, lambda: up_ring.forward(3)),
                (5, lambda: out_forward(3)),
                (6, lambda: up_ring.forward(4)),
                (7, lambda: out_forward(4)),
            ):

                @pl.when(it == when)
                def _(act=act):
                    act()

            r = pl.ds(pl.multiple_of(i * blk, blk), blk)
            keys, values = qkv[b, 1, r], qkv[b, 2, r]
            dk = jnp.zeros((blk, cols), F32)
            dv = jnp.zeros((blk, cols), F32)
            for h in range(heads):
                mask = lax.rem(lane, 128) // 32 == h
                mask_v = lane // HD == h
                km = jnp.where(mask, keys, jnp.zeros_like(keys))
                vmask = jnp.where(mask_v, values, jnp.zeros_like(values))
                probs = jnp.exp2(mm_nt(km, query) - lse[b, h : h + 1])
                d_probs = mm_nt(vmask, d_out)
                ds = (probs * (d_probs - delta[h : h + 1])).astype(BF)
                dv = jnp.where(mask_v, mm(probs.astype(BF), d_out), dv)
                dk = jnp.where(mask, mm(ds, query), dk)
                dqt[...] += mm_tn(km, ds)
            c, n = cs[r] * math.log(2.0), sn[r] * math.log(2.0)
            da, db = dk[:, :128], dk[:, 128:]
            draw[b, r, 256:512] = jnp.concatenate([da * c + db * n, db * c - da * n], axis=1).astype(BF)
            draw[b, r, 512:768] = dv.astype(BF)
            return 0

        lax.fori_loop(0, nk, keys_block, 0)
        dq = dqt[...].T * 0.125
        da, db = dq[:, :128], dq[:, 128:]
        c, n = cs[...], sn[...]
        draw[b, :, 0:256] = jnp.concatenate([da * c + db * n, db * c - da * n], axis=1).astype(BF)

        @pl.when(b == 0)
        def _():
            for cp in pulls[5:]:
                cp.wait()
            dpart[0, :, :D] = jnp.zeros((nb, D), F32)

        def part(owner):
            r = pl.ds(pl.multiple_of(owner * tl, tl), tl)
            res = mm_nt(draw[b, r], w[...])
            dpart[0, pl.ds(b, 1), :D] += jnp.sum(
                res * normed_one[b, r].astype(F32), axis=0, keepdims=True
            )
            return res

        for phase in range(2):
            where = chip if phase else 1 - chip
            pa[2 * b + phase] = part(2 * where + 1 - core).astype(BF)
            near_copy(b, phase).start()
        kept = part(2 * (1 - chip) + core)
        near_copy(b, 0).wait_recv()
        xs[b] = (kept + ra[2 * b].astype(F32)).astype(BF)
        far_copy(b).start()

        @pl.when(b == nb - 1)
        def _():
            grads(0)
            grads(1)

        kept = part(2 * chip + core)
        near_copy(b, 1).wait_recv()
        sumh[b] = kept + ra[2 * b + 1].astype(F32)
        return 0

    lax.fori_loop(0, nb, sequence, 0)
    dpart[0, :, D:] = dsc_two[...]
    small = [remote(dpart.at[0], dpart.at[1], ss, rs, 11, (g, s1))]
    small[0].start()
    first_out, second_out = out_rings[0].result(), out_rings[1].result()
    osum[...] = jnp.where(chip == 0, second_out, first_out).astype(BF)
    own_out = jnp.where(chip == 0, first_out, second_out)
    over.start()
    qkv_forward(2)
    small[0].wait_recv()
    dall[0, :, : 2 * D] = dpart[0] + dpart[1]
    dall[0, :, 2 * D :] = feats[...]
    wide = [remote(dall.at[0], dall.at[d], ss, rs, 12 + d, others[d - 1]) for d in range(1, nd)]
    for cp in wide:
        cp.start()
    for b in range(nb):
        back[b].wait_recv()
        output[b] = (base[b] + orecv[b].astype(F32)).astype(BF)
    s_up[...] = up_ring.result()
    qkv_forward(3)

    def tail(b, _):
        scale = 1.0 + modul[pl.ds(b, 1), :D]
        far_copy(b).wait_recv()
        normed, inverse = moments(tok[b].astype(F32))
        dn = (sumh[b] + xr[b].astype(F32)) * scale
        inner = jnp.mean(dn * normed, axis=-1, keepdims=True)
        grad_tok[b] = (
            d_mid[b]
            + inverse * (dn - jnp.mean(dn, axis=-1, keepdims=True) - normed * inner)
        ).astype(BF)
        return 0

    lax.fori_loop(0, nb - 1, tail, 0)
    qkv_forward(4)
    lax.fori_loop(nb - 1, nb, tail, 0)
    over.wait_recv()
    s_out[...] = own_out + ox[...].astype(F32)
    for cp in wide:
        cp.wait_recv()
    depth = s_time.shape[0]
    lane_t = lax.broadcasted_iota(jnp.int32, (depth, TF), 1)
    row_t = lax.broadcasted_iota(jnp.int32, (depth, TF), 0)
    mine = jnp.zeros((depth, 2 * D), F32)
    theirs = jnp.zeros((depth, 2 * D), F32)
    for d in range(nd):
        for b in range(nb):
            row = dall[d, b : b + 1]
            for which, other in ((0, s), (1, s2)):
                hit = lane_t == row_t + (4 * g + other) * depth
                column = jnp.sum(jnp.where(hit, row[:, 2 * D :], 0.0), axis=1, keepdims=True)
                if which:
                    theirs = theirs + column * row[:, : 2 * D]
                else:
                    mine = mine + column * row[:, : 2 * D]
    tx[0] = theirs
    swap = remote(tx.at[0], tx.at[1], ss, rs, 12, (g, s2))
    swap.start()
    s_qkv[...] = jnp.concatenate([ring.result() for ring in qkv_rings], axis=1)
    swap.wait_recv()
    s_time[...] = mine + tx[1]
    for b in range(nb):
        back[b].wait_send()
        far_copy(b).wait_send()
        for phase in range(2):
            near_copy(b, phase).wait_send()
    for cp in cross + small + wide + [over, swap]:
        cp.wait_send()
    for ring in out_rings + qkv_rings + [up_ring]:
        ring.drain()


def run_k3(
    nd, qkv, lse, attn_heads, d_heads, w, normed, tokens, modul, cs, sn, d_mid, base, osend,
    g_up, g_out, dsc_two, feats,
):
    nb, tl, width = tokens.shape
    rows, cols = attn_heads.shape[1], attn_heads.shape[2]
    hidden = g_up.shape[1]
    pc = width // nd
    vm = pl.BlockSpec(memory_space=pltpu.VMEM)
    hb = pl.BlockSpec(memory_space=pl.ANY)
    sds = jax.ShapeDtypeStruct
    v = pltpu.VMEM
    dma = pltpu.SemaphoreType.DMA
    return pl.pallas_call(
        k3_body,
        out_shape=(
            sds((nb, tl, width), BF),
            sds((nb, tl, width), BF),
            sds((pc, 3 * cols), F32),
            sds((cols, pc), F32),
            sds((pc, hidden), F32),
            sds((TF // (4 * nd), 2 * width), F32),
        ),
        in_specs=[hb, vm, hb, hb, hb, hb, hb, vm, hb, hb, hb, hb, hb, hb, hb, pl.BlockSpec(memory_space=pltpu.HBM), vm],
        out_specs=(vm,) * 6,
        scratch_shapes=[
            v((nb, tl, width), BF),
            v((cols, rows), F32),
            v((nb, rows, 3 * cols), BF),
            v((2 * nb, tl, width), BF),
            v((2 * nb, tl, width), BF),
            v((nb, tl, width), BF),
            v((nb, tl, width), BF),
            v((nb, tl, width), F32),
            v((rows, cols), BF),
            v((width, hidden), BF),
            v((2, cols, width), BF),
            v((width, 3 * cols), BF),
            v((4, cols, width), BF),
            v((2, cols, width), BF),
            v((cols, pc), BF),
            v((cols, pc), BF),
            v((2, pc // 2, hidden), BF),
            v((6, pc, hidden), BF),
            v((2, 2, cols // 2, pc), BF),
            v((2, 6, cols, pc), BF),
            v((2, 2, pc // 2, 3 * cols // 2), BF),
            v((2, 6, pc, 3 * cols // 2), BF),
            v((2, nb, 2 * width), F32),
            v((2, TF // (4 * nd), 2 * width), F32),
            v((nd, nb, 2 * width + TF), F32),
            v(qkv.shape, BF),
            v((nb, rows, cols), BF),
            v(d_heads.shape, BF),
            v(w.shape, BF),
            v(normed.shape, BF),
            v(tokens.shape, BF),
            v(cs.shape, F32),
            v(sn.shape, F32),
            v(d_mid.shape, F32),
            v(base.shape, F32),
            v(dsc_two.shape, F32),
            dma((11,)),
            dma((2,)),
            dma((20,)),
            dma((20,)),
            dma((48,)),
            dma((48,)),
        ],
        compiler_params=pltpu.CompilerParams(
            collective_id=2, has_side_effects=True, vmem_limit_bytes=52 * 1024 * 1024
        ),
        name="attention_backward",
    )(
        qkv, lse, attn_heads, d_heads, w, normed, tokens, modul, cs, sn, d_mid, base, osend,
        g_up, g_out, dsc_two, feats,
    )


def k4_body(*refs):
    *refs, sems = refs
    count = len(refs) // 2
    moves = []
    for i in range(2):
        moves.append(pltpu.make_async_copy(refs[i], refs[count + i], sems.at[i]))
        moves[i].start()
    for i in range(3, count):
        refs[count + i][...] = refs[i][...]
    w = refs[2][...]
    heads = w.shape[1] // (3 * HD)
    half, size = HD // 2, heads * HD
    pieces = []
    for h in range(heads):
        for part in (0, 1):
            for side in (0, 1):
                at = part * size + side * (size // 2) + h * half
                pieces.append(w[:, at : at + half])
        at = 2 * size + h * HD
        pieces.append(w[:, at : at + HD])
    refs[count + 2][...] = jnp.concatenate(pieces, axis=1)
    for cp in moves:
        cp.wait()


def run_k4(arrays):
    vm = pl.BlockSpec(memory_space=pltpu.VMEM)
    hb = pl.BlockSpec(memory_space=pltpu.HBM)
    specs = [hb, hb] + [vm] * (len(arrays) - 2)
    return pl.pallas_call(
        k4_body,
        out_shape=tuple(jax.ShapeDtypeStruct(a.shape, a.dtype) for a in arrays),
        in_specs=specs,
        out_specs=tuple(specs),
        scratch_shapes=[pltpu.SemaphoreType.DMA((2,))],
        compiler_params=pltpu.CompilerParams(vmem_limit_bytes=16 * 1024 * 1024),
        name="results",
    )(*arrays)


def fast_shards(nd, tokens, bins, plan, w_qkv, w_out, w_up, w_down, w_time, cotangent):
    nb, tl, width = tokens.shape
    rows = 4 * tl
    feats = time_features(plan, bins).astype(BF).astype(F32)
    half = HD // 2
    inverse = np.exp(np.arange(half, dtype=np.float32) * np.float32(-math.log(10000.0) / half))
    angle = np.arange(rows, dtype=np.float32)[:, None] * inverse.astype(np.float32)[None, :]
    cs = np.tile(np.cos(angle.astype(np.float64)).astype(np.float32), (1, 128 // half))
    sn = np.tile(np.sin(angle.astype(np.float64)).astype(np.float32), (1, 128 // half))
    (
        modul, feats, full_qkv, full_out, full_up, full_down, normed, qkv, lse, attn_heads, attn_rows,
        cot_all, act, slope, htwo, mid,
    ) = run_k1(
        nd, tokens, w_time, feats, w_qkv, w_out, w_up, w_down, cs, sn, cotangent
    )
    grad_up, grad_out, d_mid, base, osend, d_heads, dsc_two, sum_down = run_k2(
        nd, act, slope, htwo, mid, attn_rows, cot_all, modul, full_out, full_up, full_down
    )
    output, grad_tokens, sum_qkv, sum_out, sum_up, grad_time = run_k3(
        nd, qkv, lse, attn_heads, d_heads, full_qkv, normed, tokens, modul, cs, sn, d_mid, base,
        osend, grad_up, grad_out, dsc_two, feats,
    )
    return tuple(
        run_k4((output, grad_tokens, sum_qkv, sum_out, sum_up, sum_down, grad_time))
    )


def solution(mesh):
    nd, ns = mesh.shape["dp"], mesh.shape["seq"]
    fast = nd == 8 and ns == 4
    return jax.shard_map(
        functools.partial(fast_shards, nd) if fast else shards,
        mesh=mesh,
        in_specs=(
            P("dp", "seq", None),
            P("dp"),
            P(),
            P("dp", "seq"),
            P("seq", "dp"),
            P("dp", "seq"),
            P("seq", "dp"),
            P(("dp", "seq"), None),
            P("dp", "seq", None),
        ),
        out_specs=(
            P("dp", "seq", None),
            P("dp", "seq", None),
            P("dp", "seq"),
            P("seq", "dp"),
            P("dp", "seq"),
            P("seq", "dp"),
            P(("dp", "seq"), None),
        ),
        check_vma=False,
    )
```

```python
import functools
import math

import jax
import jax.numpy as jnp
import numpy as np
from jax import lax
from jax.experimental import pallas as pl
from jax.experimental.pallas import tpu as pltpu
from jax.sharding import PartitionSpec as P

D = 1024
HD = 64
TF = 256
LEN = 1024


EPSILON = 1e-05
HIGHEST = lax.Precision.HIGHEST
ROOT_HALF = 0.7071067811865476
DENSITY = 0.3989422804014327


def time_features(plan, bins):
    table = jnp.arange(plan.shape[0], dtype=jnp.int32)
    picked = jnp.where(bins[:, None] == table[None, :], plan[None, :], 0.0)
    sigma = jnp.sum(picked, axis=1)
    level = 0.25 * jnp.log(sigma)
    count = TF // 2
    freqs = jnp.exp(jnp.arange(count, dtype=jnp.float32) * (math.log(1000.0) / count))
    angles = level[:, None] * freqs[None, :]
    return jnp.concatenate([jnp.sin(angles), jnp.cos(angles)], axis=1)


def normalize(field):
    centered = field - jnp.mean(field, axis=-1, keepdims=True)
    spread = jnp.mean(centered * centered, axis=-1, keepdims=True)
    inverse = lax.rsqrt(spread + EPSILON)
    return (centered * inverse, inverse)


def norm_backward(grad_scaled, normed, inverse, scale):
    grad_normed = grad_scaled * scale
    grad_scale = jnp.sum(grad_scaled * normed, axis=1)
    inner = jnp.mean(grad_normed * normed, axis=-1, keepdims=True)
    grad_field = inverse * (
        grad_normed - jnp.mean(grad_normed, axis=-1, keepdims=True) - normed * inner
    )
    return (grad_field, grad_scale)


def rotate(field, cosine, sine):
    half = HD // 2
    first = field[..., :half]
    second = field[..., half:]
    return jnp.concatenate(
        [first * cosine - second * sine, second * cosine + first * sine], axis=-1
    )


def rotary_tables(places):
    half = HD // 2
    inverse = jnp.exp(jnp.arange(half, dtype=jnp.float32) * (-math.log(10000.0) / half))
    angle = places[:, None] * inverse[None, :]
    return (jnp.cos(angle)[:, None, None, :], jnp.sin(angle)[:, None, None, :])


def pack_heads(h_one, qkv_weight, cosine, sine):
    seqs, rows, width = h_one.shape
    raw = jnp.einsum("std,de->ste", h_one, qkv_weight, preferred_element_type=jnp.float32)
    local_heads = qkv_weight.shape[1] // (3 * HD)
    raw = raw.reshape(seqs, rows, local_heads, 3, HD)
    turned = rotate(raw[:, :, :, 0:2], cosine, sine)
    packed = jnp.concatenate([turned, raw[:, :, :, 2:3]], axis=3).astype(jnp.bfloat16)
    return packed.reshape(seqs, rows, local_heads * 3 * HD)


def unpack_grads(grad_packed, cosine, sine):
    seqs, rows, width = grad_packed.shape
    local_heads = width // (3 * HD)
    grad_fields = grad_packed.reshape(seqs, rows, local_heads, 3, HD).astype(jnp.float32)
    unturned = rotate(grad_fields[:, :, :, 0:2], cosine, -sine)
    grad_raw = jnp.concatenate([unturned, grad_fields[:, :, :, 2:3]], axis=3).astype(jnp.bfloat16)
    return grad_raw.reshape(seqs, rows, width)


def gelu_slope(upper):
    return 0.5 * (1.0 + lax.erf(upper * ROOT_HALF)) + upper * DENSITY * jnp.exp(
        -0.5 * upper * upper
    )


def attend_sequence(fields):
    local_heads = fields.shape[1]
    block = min(512, LEN)
    count = LEN // block
    keys = fields[:, :, 1]
    values = fields[:, :, 2]
    query_blocks = fields[:, :, 0].reshape(count, block, local_heads, HD)

    def attend_one_block(query_blk):
        scores = jnp.einsum(
            "qhd,khd->hqk", query_blk, keys, preferred_element_type=jnp.float32
        ) * HD ** (-0.5)
        top = jnp.max(scores, axis=-1, keepdims=True)
        expo = jnp.exp(scores - top)
        totals = jnp.sum(expo, axis=-1, keepdims=True)
        probs = (expo / totals).astype(jnp.bfloat16)
        result = jnp.einsum("hqk,khd->qhd", probs, values, preferred_element_type=jnp.float32)
        return (result.astype(jnp.bfloat16), (top + jnp.log(totals))[:, :, 0])

    results, logsums = lax.map(attend_one_block, query_blocks)
    logsums = jnp.transpose(logsums, (1, 0, 2)).reshape(local_heads, LEN)
    return (results.reshape(LEN, local_heads, HD), logsums)


def attend_all(packed_heads):
    items = packed_heads.shape[0]
    local_heads = packed_heads.shape[2] // (3 * HD)
    fields = packed_heads.reshape(items, LEN, local_heads, 3, HD)
    results, logsums = lax.map(attend_sequence, fields)
    return (results.reshape(items, LEN, local_heads * HD), logsums)


def back_sequence(pieces):
    fields, logsums, grad_heads = pieces
    local_heads = fields.shape[1]
    block = min(512, LEN)
    count = LEN // block
    keys = fields[:, :, 1]
    values = fields[:, :, 2]
    query_blocks = fields[:, :, 0].reshape(count, block, local_heads, HD)
    grad_blocks = grad_heads.reshape(count, block, local_heads, HD)
    sum_blocks = jnp.transpose(logsums.reshape(local_heads, count, block), (1, 0, 2))

    def back_one_block(carry, piece):
        key_acc, value_acc = carry
        query_blk, grad_blk, sum_blk = piece
        scores = jnp.einsum(
            "qhd,khd->hqk", query_blk, keys, preferred_element_type=jnp.float32
        ) * HD ** (-0.5)
        probs = jnp.exp(scores - sum_blk[:, :, None])
        grad_probs = jnp.einsum(
            "qhd,khd->hqk", grad_blk, values, preferred_element_type=jnp.float32
        )
        inner = jnp.sum(probs * grad_probs, axis=-1, keepdims=True)
        grad_scores = (probs * (grad_probs - inner)).astype(jnp.bfloat16)
        grad_query = jnp.einsum(
            "hqk,khd->qhd", grad_scores, keys, preferred_element_type=jnp.float32
        ) * HD ** (-0.5)
        key_acc = key_acc + jnp.einsum(
            "hqk,qhd->khd", grad_scores, query_blk, preferred_element_type=jnp.float32
        ) * HD ** (-0.5)
        value_acc = value_acc + jnp.einsum(
            "hqk,qhd->khd", probs.astype(jnp.bfloat16), grad_blk, preferred_element_type=jnp.float32
        )
        return ((key_acc, value_acc), grad_query)

    empty = jnp.zeros((LEN, local_heads, HD), jnp.float32)
    (grad_keys, grad_values), grad_queries = lax.scan(
        back_one_block, (empty, empty), (query_blocks, grad_blocks, sum_blocks)
    )
    grad_queries = grad_queries.reshape(LEN, local_heads, HD)
    return jnp.stack([grad_queries, grad_keys, grad_values], axis=2).astype(jnp.bfloat16)


def back_all(packed_heads, logsums, grad_heads):
    items = packed_heads.shape[0]
    local_heads = packed_heads.shape[2] // (3 * HD)
    fields = packed_heads.reshape(items, LEN, local_heads, 3, HD)
    grads = grad_heads.reshape(items, LEN, local_heads, HD)
    result = lax.map(back_sequence, (fields, logsums, grads))
    return result.reshape(items, LEN, local_heads * 3 * HD)


def data_layer(
    tokens, cotangent, w_qkv, w_up, w_out, w_down, scale_one, scale_two, norm_one, inverse_one
):
    seqs, local_len, width = tokens.shape
    wide = (
        lax.all_gather(w_qkv, "seq", axis=1, tiled=True),
        lax.all_gather(w_up, "seq", axis=1, tiled=True),
        lax.all_gather(w_out, "seq", axis=0, tiled=True),
        lax.all_gather(w_down, "seq", axis=0, tiled=True),
    )
    full_qkv, full_up, full_out, full_down = (
        lax.all_gather(wide[0], "dp", axis=0, tiled=True),
        lax.all_gather(wide[1], "dp", axis=0, tiled=True),
        lax.all_gather(wide[2], "dp", axis=1, tiled=True),
        lax.all_gather(wide[3], "dp", axis=1, tiled=True),
    )
    field = tokens.astype(jnp.float32)
    h_one = (norm_one * scale_one).astype(jnp.bfloat16)
    places = (lax.axis_index("seq") * local_len + jnp.arange(local_len, dtype=jnp.int32)).astype(
        jnp.float32
    )
    cosine, sine = rotary_tables(places)
    packed = pack_heads(h_one, full_qkv, cosine, sine)
    packed_heads = lax.all_to_all(packed, "seq", split_axis=2, concat_axis=1, tiled=True)
    results, logsums = attend_all(packed_heads)
    back_tokens = lax.all_to_all(results, "seq", split_axis=1, concat_axis=2, tiled=True)
    middle = field + jnp.einsum(
        "std,de->ste", back_tokens, full_out, preferred_element_type=jnp.float32
    )
    norm_two, inverse_two = normalize(middle)
    h_two = (norm_two * scale_two).astype(jnp.bfloat16)
    upper = jnp.einsum("std,df->stf", h_two, full_up, preferred_element_type=jnp.float32)
    active = jax.nn.gelu(upper, approximate=False).astype(jnp.bfloat16)
    output = (
        middle + jnp.einsum("stf,fd->std", active, full_down, preferred_element_type=jnp.float32)
    ).astype(jnp.bfloat16)
    grad_down = jnp.einsum("stf,std->fd", active, cotangent, preferred_element_type=jnp.float32)
    grad_active = jnp.einsum(
        "std,fd->stf", cotangent, full_down, preferred_element_type=jnp.float32
    )
    grad_upper = (grad_active * gelu_slope(upper)).astype(jnp.bfloat16)
    grad_up = jnp.einsum("std,stf->df", h_two, grad_upper, preferred_element_type=jnp.float32)
    grad_htwo = jnp.einsum("stf,df->std", grad_upper, full_up, preferred_element_type=jnp.float32)
    grad_middle, grad_scale_two = norm_backward(grad_htwo, norm_two, inverse_two, scale_two)
    grad_middle = grad_middle + cotangent.astype(jnp.float32)
    grad_branch = grad_middle.astype(jnp.bfloat16)
    grad_out = jnp.einsum(
        "std,ste->de", back_tokens, grad_branch, preferred_element_type=jnp.float32
    )
    grad_attended = jnp.einsum(
        "ste,de->std", grad_branch, full_out, preferred_element_type=jnp.float32
    ).astype(jnp.bfloat16)
    grad_heads = lax.all_to_all(grad_attended, "seq", split_axis=2, concat_axis=1, tiled=True)
    grad_packed_heads = back_all(packed_heads, logsums, grad_heads)
    grad_packed = lax.all_to_all(grad_packed_heads, "seq", split_axis=1, concat_axis=2, tiled=True)
    grad_raw = unpack_grads(grad_packed, cosine, sine)
    grad_qkv = jnp.einsum("std,ste->de", h_one, grad_raw, preferred_element_type=jnp.float32)
    grad_hone = jnp.einsum("ste,de->std", grad_raw, full_qkv, preferred_element_type=jnp.float32)
    grad_field, grad_scale_one = norm_backward(grad_hone, norm_one, inverse_one, scale_one)
    grad_tokens = (grad_middle + grad_field).astype(jnp.bfloat16)
    partial_sums = (
        lax.psum_scatter(
            grad_qkv.astype(jnp.bfloat16), "dp", scatter_dimension=0, tiled=True
        ).astype(jnp.float32),
        lax.psum_scatter(
            grad_up.astype(jnp.bfloat16), "dp", scatter_dimension=0, tiled=True
        ).astype(jnp.float32),
        lax.psum_scatter(
            grad_out.astype(jnp.bfloat16), "dp", scatter_dimension=1, tiled=True
        ).astype(jnp.float32),
        lax.psum_scatter(
            grad_down.astype(jnp.bfloat16), "dp", scatter_dimension=1, tiled=True
        ).astype(jnp.float32),
    )
    sums = (
        lax.psum_scatter(
            partial_sums[0].astype(jnp.bfloat16), "seq", scatter_dimension=1, tiled=True
        ).astype(jnp.float32),
        lax.psum_scatter(
            partial_sums[1].astype(jnp.bfloat16), "seq", scatter_dimension=1, tiled=True
        ).astype(jnp.float32),
        lax.psum_scatter(
            partial_sums[2].astype(jnp.bfloat16), "seq", scatter_dimension=0, tiled=True
        ).astype(jnp.float32),
        lax.psum_scatter(
            partial_sums[3].astype(jnp.bfloat16), "seq", scatter_dimension=0, tiled=True
        ).astype(jnp.float32),
    )
    return (output, grad_tokens, grad_scale_one, grad_scale_two, sums)


def shards(tokens, bins, plan, w_qkv, w_out, w_up, w_down, w_time, cotangent):
    feats = time_features(plan, bins).astype(jnp.bfloat16)
    full_time = lax.all_gather(w_time, ("dp", "seq"), axis=0, tiled=True)
    modul = jnp.dot(feats, full_time, preferred_element_type=jnp.float32)
    scale_one = 1.0 + modul[:, None, :D]
    scale_two = 1.0 + modul[:, None, D:]
    norm_one, inverse_one = normalize(tokens.astype(jnp.float32))
    output, grad_tokens, grad_scale_one, grad_scale_two, sums = data_layer(
        tokens, cotangent, w_qkv, w_up, w_out, w_down, scale_one, scale_two, norm_one, inverse_one
    )
    grad_scales = jnp.concatenate([grad_scale_one, grad_scale_two], axis=1)
    grad_time = jnp.dot(feats.astype(jnp.float32).T, grad_scales, precision=HIGHEST)
    time_sum = lax.psum_scatter(grad_time, ("dp", "seq"), scatter_dimension=0, tiled=True)
    return (output, grad_tokens, sums[0], sums[2], sums[1], sums[3], time_sum)


BF = jnp.bfloat16
F32 = jnp.float32
MESHID = pl.DeviceIdType.MESH
QUERY_SCALE = HD**-0.5 / math.log(2.0)
VMEM_LIMIT = 60 * 1024 * 1024


def mm(a, b):
    return lax.dot_general(a, b, (((1,), (0,)), ((), ())), preferred_element_type=F32)


def mm_nt(a, b):
    return lax.dot_general(a, b, (((1,), (1,)), ((), ())), preferred_element_type=F32)


def mm_tn(a, b):
    return lax.dot_general(a, b, (((0,), (0,)), ((), ())), preferred_element_type=F32)


def peers():
    g = lax.axis_index("dp")
    s = lax.axis_index("seq")
    core = lax.rem(s, 2)
    return g, s, core, s + 1 - 2 * core, lax.rem(s + 2, 4), 3 - s


def remote(src, dst, ss, rs, i, dev):
    return pltpu.make_async_remote_copy(
        src_ref=src,
        dst_ref=dst,
        send_sem=ss.at[i],
        recv_sem=rs.at[i],
        device_id=dev,
        device_id_type=MESHID,
    )


def greet(devices):
    barrier = pltpu.get_barrier_semaphore()
    for dev in devices:
        pl.semaphore_signal(barrier, inc=1, device_id=dev, device_id_type=MESHID)
    pl.semaphore_wait(barrier, len(devices))


def moments(field):
    centered = field - jnp.mean(field, axis=-1, keepdims=True)
    spread = jnp.mean(centered * centered, axis=-1, keepdims=True)
    inverse = lax.rsqrt(spread + EPSILON)
    return centered * inverse, inverse


def ring_place(g):
    z, y = g // 2, lax.rem(g, 2)
    return z + y * (7 - 2 * z)


def ring_index(p):
    p = lax.rem(p + 16, 8)
    return 2 * p + (p // 4) * (15 - 4 * p)


WAYS = (1, -1)


class Gather:
    def __init__(self, own, view, ss, rs, first):
        self.own, self.view, self.ss, self.rs, self.first = own, view, ss, rs, first

    def hop(self, k, way):
        g, s = lax.axis_index("dp"), lax.axis_index("seq")
        p = ring_place(g)
        j = ring_index(p - way * (k - 1))
        half = None if k < 4 else (0 if way > 0 else 1)
        dst = self.view(j, half)
        src = self.own if k == 1 else dst
        i = self.first + 2 * (k - 1) + (way < 0)
        return remote(src, dst, self.ss, self.rs, i, (ring_index(p + way), s))

    def start(self):
        for way in WAYS:
            self.hop(1, way).start()

    def forward(self, k):
        for way in WAYS:
            self.hop(k - 1, way).wait_recv()
            self.hop(k, way).start()

    def arrive(self):
        for way in WAYS:
            self.hop(4, way).wait_recv()

    def drain(self):
        for k in (1, 2, 3, 4):
            for way in WAYS:
                self.hop(k, way).wait_send()


class Scatter:
    def __init__(self, view, halves, wholes, ss, rs, first):
        self.view, self.halves, self.wholes = view, halves, wholes
        self.ss, self.rs, self.first = ss, rs, first

    def hop(self, k, way):
        g, s = lax.axis_index("dp"), lax.axis_index("seq")
        p = ring_place(g)
        side = 0 if way > 0 else 1
        j = ring_index(p + way * (5 - k))
        src = self.view(j, side if k == 1 else None)
        dst = self.halves.at[side] if k == 1 else self.wholes.at[3 * side + k - 2]
        i = self.first + 2 * (k - 1) + side
        return remote(src, dst, self.ss, self.rs, i, (ring_index(p + way), s))

    def start(self):
        for way in WAYS:
            self.hop(1, way).start()

    def forward(self, k):
        p = ring_place(lax.axis_index("dp"))
        for way in WAYS:
            side = 0 if way > 0 else 1
            self.hop(k - 1, way).wait_recv()
            got = self.halves.at[side] if k == 2 else self.wholes.at[3 * side + k - 3]
            mine = self.view(ring_index(p + way * (5 - k)), side if k == 2 else None)
            mine[...] = (mine[...].astype(F32) + got[...].astype(F32)).astype(BF)
            self.hop(k, way).start()

    def result(self):
        for way in WAYS:
            self.hop(4, way).wait_recv()
        mine = self.view(lax.axis_index("dp"), None)
        return mine[...].astype(F32) + (self.wholes[2].astype(F32) + self.wholes[5].astype(F32))

    def drain(self):
        for k in (1, 2, 3, 4):
            for way in WAYS:
                self.hop(k, way).wait_send()


def rows_of(ref, half, size):
    return ref if half is None else ref.at[half * (size // 2) : (half + 1) * (size // 2)]


def ordering(heads):
    half, size = HD // 2, heads * HD
    to = lax.broadcasted_iota(jnp.int32, (1, 3 * size), 1)
    part, at = to // size, lax.rem(to, size)
    side, rest = at // (size // 2), lax.rem(at, size // 2)
    turned = (rest // half) * (3 * HD) + part * HD + side * half + lax.rem(rest, half)
    plain = (at // HD) * (3 * HD) + 2 * HD + lax.rem(at, HD)
    source = jnp.where(part == 2, plain, turned)
    rows = lax.broadcasted_iota(jnp.int32, (3 * size, 3 * size), 0)
    return jnp.where(rows == source, 1.0, 0.0).astype(BF)


def k1_body(
    tok, wt, feats, w_qkv, w_out, w_up, w_down, cs, sn, cot,
    modul, feats_out, wq_out, out_all, up_all, down_all, n_out, qkv_out, lse, attn_heads, attn_rows, cot_all,
    act_out, slope_out, htwo_out, mid_out,
    tokv, wtime, pbuf, vt, cotv, wq, nv, qkv, attn, outv, upv, act, slope, htwo, mids, csv, snv,
    ks, ls, ss, rs, gs, gr, fs_, fr_, os_,
):
    g, s, core, s1, s2, s3 = peers()
    p = ring_place(g)
    nb, tl = tok.shape[0], tok.shape[1]
    rows = 4 * tl
    blk = 256
    nq = rows // blk
    heads = attn.shape[3] // HD
    nr, nc = w_out.shape[0], w_out.shape[1]

    def lanes(j, size):
        return pl.ds(pl.multiple_of(j * size, size), size)

    def view_out(other):
        def view(j, half):
            lo, size = (0, nr) if half is None else (half * (nr // 2), nr // 2)
            return outv.at[pl.ds(pl.multiple_of(other * nr + lo, size), size), lanes(j, nc)]

        return view

    def view_down(j, half):
        size = w_down.shape[0]
        lo, n = (0, size) if half is None else (half * (size // 2), size // 2)
        return down_all.at[lo : lo + n, lanes(j, w_down.shape[1])]

    def view_rows(ref, size):
        def view(j, half):
            lo, n = (0, size) if half is None else (half * (size // 2), size // 2)
            return ref.at[pl.ds(pl.multiple_of(j * size + lo, n), n)]

        return view

    def view_time(j, half):
        return wtime.at[j] if half is None else wtime.at[j, :, half * D : (half + 1) * D]

    def view_qkv(side):
        size = w_qkv.shape[0]

        def view(j, half):
            lo, n = (0, size // 2) if half is None else (half * (size // 4), size // 4)
            at = pl.multiple_of(j * size + side * (size // 2) + lo, n)
            return wq.at[pl.ds(at, n)]

        return view

    here = view_out(s)(g, None)
    time_ring = Gather(wt, view_time, gs, gr, 0)
    part = w_qkv.shape[0] // 2
    qkv_rings = [
        Gather(view_qkv(i)(g, None), view_qkv(i), gs, gr, 8 + 40 * i)
        for i in range(2)
    ]
    up_ring = Gather(w_up, view_rows(upv, w_up.shape[0]), gs, gr, 16)
    down_ring = Gather(w_down, view_down, gs, gr, 24)
    out_ring = Gather(w_out, view_out(s), gs, gr, 32)
    far_ring = Gather(view_out(s2)(g, None), view_out(s2), gs, gr, 40)

    local = [
        pltpu.make_async_copy(tok, tokv.at[:, s], ls.at[0]),
        pltpu.make_async_copy(cot, cotv, ls.at[5]),
        pltpu.make_async_copy(w_up, view_rows(upv, w_up.shape[0])(g, None), ls.at[2]),
        pltpu.make_async_copy(w_down, view_down(g, None), ls.at[3]),
        pltpu.make_async_copy(w_out, here, ls.at[4]),
        pltpu.make_async_copy(cs, csv, ls.at[6]),
        pltpu.make_async_copy(sn, snv, ls.at[7]),
    ]
    greet([(g, s1), (g, s2), (g, s3), (ring_index(p + 1), s), (ring_index(p - 1), s)])
    time_ring.start()
    pair_out = remote(w_out, here, ss, rs, 0, (g, s2))
    pair_out.start()
    far = [remote(tok.at[b], tokv.at[b, s], ss, rs, 1 + b, (g, s2)) for b in range(nb)]
    far[0].start()
    ordered = mm(w_qkv[...], ordering(heads)).astype(BF)
    wq[pl.ds(pl.multiple_of(g * w_qkv.shape[0], w_qkv.shape[0]), w_qkv.shape[0])] = ordered
    for ring in qkv_rings:
        ring.start()
    near = []
    for b in range(nb):
        cp = remote(tok.at[b], tokv.at[b, s], ss, rs, 3 + b, (g, s1))
        cp.start()
        near.append(cp)
    for cp in local:
        cp.start()
    wtime[g] = wt[...]
    pieces = [(0, 0, tl // 4), (0, tl // 4, tl)] + [(b, 0, tl) for b in range(1, nb)]

    def cot_piece(k):
        b, lo, hi = pieces[k]
        return remote(
            cotv.at[b, lo:hi], cot_all.at[b, s, lo:hi], ss, rs, 18 + k, (g, s2)
        )

    local[1].wait()
    cot_far = [cot_piece(k) for k in range(len(pieces))]
    cot_far[0].start()
    for k in (2, 3, 4):
        time_ring.forward(k)
        for ring in qkv_rings:
            ring.forward(k)
    up_ring.start()
    out_ring.start()
    pair_out.wait_recv()
    far_ring.start()
    time_ring.arrive()
    depth = wt.shape[0]
    feats_out[...] = feats[...]
    lane_t = lax.broadcasted_iota(jnp.int32, (depth, TF), 1)
    row_t = lax.broadcasted_iota(jnp.int32, (depth, TF), 0)
    sums = [jnp.zeros((depth, 2 * D), F32) for _ in range(nb)]
    for d in range(wtime.shape[0]):
        hit = lane_t == row_t + (4 * d + s) * depth
        weights = wtime[d].astype(F32)
        for b in range(nb):
            column = jnp.sum(jnp.where(hit, feats[b : b + 1], 0.0), axis=1, keepdims=True)
            sums[b] = sums[b] + weights * column
    pbuf[0] = jnp.concatenate([jnp.sum(v, axis=0, keepdims=True) for v in sums], axis=0)
    small = []
    for e, other in ((1, s1), (2, s2), (3, s3)):
        cp = remote(pbuf.at[0], pbuf.at[e], ss, rs, 4 + e, (g, other))
        cp.start()
        small.append(cp)
    far[1].start()
    cot_far[1].start()
    passed = [
        remote(tokv.at[b, s2], tokv.at[b, s2], ss, rs, 8 + b, (g, s1)) for b in range(nb)
    ]
    cot_near = [remote(cotv.at[b], cot_all.at[b, s], ss, rs, 12 + b, (g, s1)) for b in range(nb)]
    cot_pass = [
        remote(cot_all.at[b, s2], cot_all.at[b, s2], ss, rs, 14 + b, (g, s1)) for b in range(nb)
    ]
    far[0].wait_recv()
    passed[0].start()
    for c in small:
        c.wait_recv()
    modul[...] = (pbuf[0] + pbuf[1]) + (pbuf[2] + pbuf[3])
    for ring in qkv_rings:
        ring.arrive()
    for i in (0, 5, 6):
        local[i].wait()
    keep_w = pltpu.make_async_copy(wq, wq_out, ls.at[8])
    keep_w.start()
    keep_cot = pltpu.make_async_copy(cotv, cot_all.at[:, s], ls.at[9])
    keep_cot.start()

    def attn_copy(kind, it):
        b, q = it // nq, lax.rem(it, nq)
        r = pl.ds(pl.multiple_of(q * blk, blk), blk)
        ref = attn.at[b, s2 if kind == 2 else s, r]
        return remote(ref, ref, fs_.at[kind], fr_.at[kind], it, (g, s2 if kind == 0 else s1))

    lane = lax.broadcasted_iota(jnp.int32, (1, 2 * 128), 1)

    def keep_fields(b):
        return (
            pltpu.make_async_copy(nv.at[b], n_out.at[b], ks.at[0, b]),
            pltpu.make_async_copy(qkv.at[b], qkv_out.at[b], ks.at[1, b]),
        )

    def project(b):
        scale = 1.0 + modul[pl.ds(b, 1), :D]

        def one(i, _):
            r = pl.ds(pl.multiple_of(i * blk, blk), blk)
            normed, _inv = moments(tokv[b, i].astype(F32))
            nv[b, r] = normed.astype(BF)
            raw = mm((normed * scale).astype(BF), wq[...])
            c, n = csv[r], snv[r]
            qa, qb = raw[:, :128] * QUERY_SCALE, raw[:, 128:256] * QUERY_SCALE
            ka, kb = raw[:, 256:384], raw[:, 384:512]
            qkv[b, 0, r] = jnp.concatenate([qa * c - qb * n, qb * c + qa * n], axis=1).astype(BF)
            qkv[b, 1, r] = jnp.concatenate([ka * c - kb * n, kb * c + ka * n], axis=1).astype(BF)
            qkv[b, 2, r] = raw[:, 512:].astype(BF)
            return 0

        lax.fori_loop(0, nq, one, 0)

    def pass_attn(lo, hi):
        def forward(it, _):
            attn_copy(0, it).wait_recv()
            attn_copy(2, it).start()
            return 0

        lax.fori_loop(lo, hi, forward, 0)

    def arrive_attn(lo, hi):
        def forward(it, _):
            attn_copy(1, it).wait_recv()
            attn_copy(2, it).wait_recv()
            return 0

        lax.fori_loop(lo, hi, forward, 0)

    def tokens_of(b):
        near[b].wait_recv()
        passed[b].wait_recv()

    def second_tokens():
        far[1].wait_recv()
        passed[1].start()

    def step(it, _):
        b, q = it // nq, lax.rem(it, nq)
        for i in range(nb):

            @pl.when(it == i * nq)
            def _(i=i):
                tokens_of(i)

        def at(events):
            for when, action in events:

                @pl.when(it == when)
                def _(action=action):
                    action()

        def up_out(k):
            up_ring.forward(k)
            out_ring.forward(k)
            far_ring.forward(k)

        at(((4, lambda: up_out(4)), (4, down_ring.start)))

        @pl.when(q == 0)
        def _():
            project(b)
            vt[...] = qkv[b, 2].T
            for cp in keep_fields(b):
                cp.start()

        at(
            (
                (0, lambda: up_out(2)),
                (2, lambda: up_out(3)),
                (2, second_tokens),
                (6, lambda: pass_attn(0, nq)),
                (7, lambda: down_ring.forward(2)),
            )
        )
        r = pl.ds(pl.multiple_of(q * blk, blk), blk)
        query, keys = qkv[b, 0, r], qkv[b, 1]
        outs, stats = [], []
        masked = jnp.concatenate(
            [
                jnp.where(lax.rem(lane, 128) // 32 == h, query, jnp.zeros_like(query))
                for h in range(heads)
            ],
            axis=0,
        )
        both = mm_nt(keys, masked)
        tops = jnp.max(both, axis=0, keepdims=True)
        expo = jnp.exp2(both - tops)
        totals = jnp.sum(expo, axis=0, keepdims=True)
        expo = expo.astype(BF)
        shares = 1.0 / totals
        for h in range(heads):
            c = slice(h * blk, (h + 1) * blk)
            outs.append(mm(vt[h * HD : (h + 1) * HD], expo[:, c]) * shares[:, c])
            stats.append(tops[:, c] + jnp.log2(totals[:, c]))
        attn[b, s, r] = jnp.concatenate(outs, axis=0).T.astype(BF)
        lse[b, :, r] = jnp.concatenate(stats + [jnp.zeros((8 - heads, blk), F32)], axis=0)
        attn_copy(0, it).start()
        attn_copy(1, it).start()
        return 0

    lax.fori_loop(0, nb * nq, step, 0)
    for cp in cot_far[2:] + cot_near:
        cp.start()
    keep = pltpu.make_async_copy(attn.at[:, s], attn_heads, ls.at[10])
    keep.start()
    out_ring.arrive()
    far_ring.arrive()
    local[4].wait()
    cross = []
    for e, other in ((0, s), (1, s2)):
        ref = outv.at[pl.ds(pl.multiple_of(other * nr, nr), nr)]
        cp = remote(ref, ref, ss, rs, 16 + e, (g, s1))
        cp.start()
        cross.append(cp)
    up_ring.arrive()
    local[2].wait()
    for cp in cross:
        cp.wait_recv()
    arrive_attn(0, nq)
    keep_out = pltpu.make_async_copy(outv, out_all, ls.at[11])
    keep_out.start()
    keep_up = pltpu.make_async_copy(upv, up_all, ls.at[12])
    keep_up.start()

    def keep_block(i):
        return (
            pltpu.make_async_copy(act.at[i], act_out.at[i], os_.at[0, i]),
            pltpu.make_async_copy(slope.at[i], slope_out.at[i], os_.at[1, i]),
            pltpu.make_async_copy(htwo.at[i], htwo_out.at[i], os_.at[2, i]),
        )

    def feed(i, _):
        b, owner = i // 4, lax.rem(i, 4)
        for when, action in (
            (1, lambda: down_ring.forward(3)),
            (3, lambda: pass_attn(nq, 2 * nq)),
            (4, lambda: arrive_attn(nq, 2 * nq)),
            (4, lambda: down_ring.forward(4)),
        ):

            @pl.when(i == when)
            def _(action=action):
                action()

        scale = 1.0 + modul[pl.ds(b, 1), D:]
        r = pl.ds(pl.multiple_of(owner * tl, tl), tl)
        joined = jnp.concatenate([attn[b, j, r] for j in range(4)], axis=1)
        mid = tokv[b, owner].astype(F32) + mm(joined, outv[...])
        normed, _inv = moments(mid)
        h = (normed * scale).astype(BF)
        upper = mm(h, upv[...])
        phi = 0.5 * (1.0 + lax.erf(upper * ROOT_HALF))
        act[i] = (upper * phi).astype(BF)
        slope[i] = (phi + upper * (DENSITY * jnp.exp(-0.5 * upper * upper))).astype(BF)
        htwo[i] = h

        @pl.when(owner == s)
        def _():
            mids[b] = mid

        for cp in keep_block(i):
            cp.start()
        return 0

    lax.fori_loop(0, 4 * nb, feed, 0)
    keep_mid = pltpu.make_async_copy(mids, mid_out, ls.at[13])
    keep_mid.start()
    own_rows = pl.ds(pl.multiple_of(s * tl, tl), tl)
    keep_rows = pltpu.make_async_copy(attn.at[:, :, own_rows], attn_rows, ls.at[14])
    keep_rows.start()
    for b in range(nb):
        for k, piece in enumerate(pieces):
            if piece[0] == b:
                cot_far[k].wait_recv()
        cot_pass[b].start()

    def finish(it, _):
        attn_copy(0, it).wait_send()
        attn_copy(1, it).wait_send()
        attn_copy(2, it).wait_send()
        return 0

    lax.fori_loop(0, nb * nq, finish, 0)

    def kept(i, _):
        for cp in keep_block(i):
            cp.wait()
        return 0

    lax.fori_loop(0, 4 * nb, kept, 0)
    down_ring.arrive()
    for cp in cot_near + cot_pass:
        cp.wait()
    for cp in cot_far + far + near + passed + small + cross + [pair_out]:
        cp.wait_send()
    for ring in [time_ring, up_ring, down_ring, out_ring, far_ring] + qkv_rings:
        ring.drain()
    local[3].wait()
    for cp in (keep_cot, keep, keep_w, keep_out, keep_up, keep_mid, keep_rows):
        cp.wait()
    for b in range(nb):
        for cp in keep_fields(b):
            cp.wait()


def run_k1(nd, tokens, w_time, feats, w_qkv, w_out, w_up, w_down, cs, sn, cot):
    nb, tl, width = tokens.shape
    rows = 4 * tl
    cols = w_qkv.shape[1] // 3
    hidden = w_up.shape[1]
    vm = pl.BlockSpec(memory_space=pltpu.VMEM)
    hb = pl.BlockSpec(memory_space=pl.ANY)
    steps = nb * (rows // 256)
    sds = jax.ShapeDtypeStruct
    dma = pltpu.SemaphoreType.DMA
    v = pltpu.VMEM
    return pl.pallas_call(
        k1_body,
        out_shape=(
            sds((nb, 2 * width), F32),
            sds((nb, TF), F32),
            sds((width, 3 * cols), BF),
            sds((width, width), BF),
            sds((width, hidden), BF),
            sds((hidden, width), BF),
            sds((nb, rows, width), BF),
            sds((nb, 3, rows, cols), BF),
            sds((nb, 8, rows), F32),
            sds((nb, rows, cols), BF),
            sds((nb, 4, tl, cols), BF),
            sds((nb, 4, tl, width), BF),
            sds((4 * nb, tl, hidden), BF),
            sds((4 * nb, tl, hidden), BF),
            sds((4 * nb, tl, width), BF),
            sds((nb, tl, width), F32),
        ),
        in_specs=[hb, vm, vm, vm, vm, vm, vm, hb, hb, hb],
        out_specs=(vm, vm, hb, hb, hb, hb, hb, hb, vm) + (hb,) * 7,
        scratch_shapes=[
            v((nb, 4, tl, width), BF),
            v((nd,) + w_time.shape, BF),
            v((4, nb, 2 * width), F32),
            v((cols, rows), BF),
            v((nb, tl, width), BF),
            v((width, 3 * cols), BF),
            v((nb, rows, width), BF),
            v((nb, 3, rows, cols), BF),
            v((nb, 4, rows, cols), BF),
            v((width, width), BF),
            v((width, hidden), BF),
            v((4 * nb, tl, hidden), BF),
            v((4 * nb, tl, hidden), BF),
            v((4 * nb, tl, width), BF),
            v((nb, tl, width), F32),
            v(cs.shape, F32),
            v(sn.shape, F32),
            dma((2, nb)),
            dma((15,)),
            dma((22,)),
            dma((22,)),
            dma((56,)),
            dma((56,)),
            dma((3, steps)),
            dma((3, steps)),
            dma((3, 4 * nb)),
        ],
        compiler_params=pltpu.CompilerParams(
            collective_id=0, has_side_effects=True, vmem_limit_bytes=VMEM_LIMIT
        ),
        name="attention_forward",
    )(tokens, w_time, feats, w_qkv, w_out, w_up, w_down, cs, sn, cot)


def k2_body(
    act_h, slope_h, htwo_h, mid_h, attn_h, cot_h, modul, w_out_h, w_up_h, w_down_h,
    grad_up, grad_out, d_mid_h, base_h, osend_h, d_heads, dsc, s_down,
    act, dup, htwo, mids, attn, cot, w_out, w_up, w_down, d_mid, base, osend,
    pa, pb_, ra, rb, xs, xr, dat, stage, gdv, down_h, down_w,
    ls, ss, rs, os_, ins, keeps, bs, gs, gr,
):
    g, s, core, s1, s2, s3 = peers()
    p = ring_place(g)
    chip = s // 2
    nb, tl = cot.shape[0], cot.shape[2]

    def pull(jp, which):
        phase, b = jp // nb, lax.rem(jp, nb)
        where = chip + (1 - phase) * (1 - 2 * chip)
        owner = 2 * where + (1 - core if which == 0 else core)
        i = b * 4 + owner
        k = 2 * jp + which
        return (
            pltpu.make_async_copy(cot_h.at[b, owner], cot.at[b, owner], bs.at[0, k]),
            pltpu.make_async_copy(slope_h.at[i], dup.at[i], bs.at[1, k]),
            pltpu.make_async_copy(act_h.at[i], act.at[i], bs.at[2, k]),
        )

    loads = []
    for i, (src, dst) in enumerate(
        (
            (w_down_h, w_down), (w_up_h, w_up),
            (mid_h, mids), (w_out_h, w_out), (htwo_h, htwo), (attn_h, attn),
        )
    ):
        loads.append(pltpu.make_async_copy(src, dst, ins.at[i]))
    first = pull(0, 0)
    loads[0].start()
    for cp in first:
        cp.start()
    loads[1].start()
    greet([(g, s1), (g, s2), (g, s3), (ring_index(p + 1), s), (ring_index(p - 1), s)])
    hidden = act.shape[2]
    pc = s_down.shape[1]

    def view_down(j, half):
        lo, n = (0, hidden) if half is None else (half * (hidden // 2), hidden // 2)
        return gdv.at[lo : lo + n, pl.ds(pl.multiple_of(j * pc, pc), pc)]

    down_ring = Scatter(view_down, down_h, down_w, gs, gr, 0)

    def back_part(b, owner):
        i = b * 4 + owner
        d_act = mm_nt(cot[b, owner], w_down[...])
        d_up = (d_act * dup[i].astype(F32)).astype(BF)
        dup[i] = d_up
        return mm_nt(d_up, w_up[...])

    def back_copy(jp):
        return remote(pa.at[jp], ra.at[jp], ss, rs, jp, (g, s1))

    def out_copy(jp):
        return remote(pb_.at[jp], rb.at[jp], ss, rs, 4 + jp, (g, s1))

    def far_copy(b):
        return remote(xs.at[b], xr.at[b], ss, rs, 8 + b, (g, s2))

    def place(jp):
        phase, b = jp // nb, lax.rem(jp, nb)
        return phase, b, chip + (1 - phase) * (1 - 2 * chip)

    def give(jp, _):
        phase, b, where = place(jp)

        @pl.when(phase == 0)
        def _():
            for cp in pull(jp, 0):
                cp.wait()

        pa[jp] = back_part(b, 2 * where + 1 - core).astype(BF)
        back_copy(jp).start()
        return 0

    def take(jp, _):
        phase, b, where = place(jp)

        @pl.when(phase == 0)
        def _():
            for cp in pull(jp, 1):
                cp.wait()

        dh = back_part(b, 2 * where + core)
        back_copy(jp).wait_recv()
        dh = dh + ra[jp].astype(F32)

        @pl.when(phase == 0)
        def _():
            xs[b] = dh.astype(BF)
            far_copy(b).start()

        @pl.when(phase == 1)
        def _():
            d_mid[b] = dh

        return 0

    def give_out(jp, _):
        _phase, b, where = place(jp)
        pb_[jp] = mm(act[b * 4 + 2 * where + 1 - core], w_down[...]).astype(BF)
        out_copy(jp).start()
        return 0

    def take_out(jp, _):
        phase, b, where = place(jp)
        out = mm(act[b * 4 + 2 * where + core], w_down[...])
        out_copy(jp).wait_recv()
        out = out + rb[jp].astype(F32)

        @pl.when(phase == 0)
        def _():
            osend[b] = out.astype(BF)

        @pl.when(phase == 1)
        def _():
            base[b] = out + mids[b]

        return 0

    def down_grads(i, _):
        r = pl.ds(pl.multiple_of(i * 256, 256), 256)
        left = act[:, :, r].reshape(4 * nb * tl, 256)
        gdv[r] = mm_tn(left, cot[...].reshape(4 * nb * tl, D)).astype(BF)
        return 0

    def up_copy(i):
        r = pl.ds(pl.multiple_of(i * 256, 256), 256)
        return pltpu.make_async_copy(stage.at[i], grad_up.at[r], os_.at[i])

    def up_grads(i, _):
        r = pl.ds(pl.multiple_of(i * 256, 256), 256)
        left = htwo[:, :, r].reshape(4 * nb * tl, 256)
        stage[i] = mm_tn(left, dup[...].reshape(4 * nb * tl, hidden)).astype(BF)
        up_copy(i).start()
        return 0

    def spread(e, other, b):
        return remote(dat.at[other, b], d_heads.at[s, b], ss, rs, 10 + 2 * e + b, (g, other))

    def tail(b, _):
        scale = 1.0 + modul[pl.ds(b, 1), D:]
        far_copy(b).wait_recv()
        dh = d_mid[b] + xr[b].astype(F32)
        normed, inverse = moments(mids[b])
        dsc[pl.ds(b, 1)] = jnp.sum(dh * normed, axis=0, keepdims=True)
        dn = dh * scale
        inner = jnp.mean(dn * normed, axis=-1, keepdims=True)
        dm = cot[b, s].astype(F32) + inverse * (
            dn - jnp.mean(dn, axis=-1, keepdims=True) - normed * inner
        )
        d_mid[b] = dm
        branch = mm_nt(dm.astype(BF), w_out[...]).astype(BF)
        for j in range(4):
            dat[j, b] = branch[:, j * 256 : (j + 1) * 256]
        for e, other in ((0, s2), (1, s3), (2, s1)):
            spread(e, other, b).start()
        return 0

    for which in (0, 1):
        for jp in range(nb):
            if jp + which:
                for cp in pull(jp, which):
                    cp.start()
    for cp in loads[:2]:
        cp.wait()
    half = D // 512
    lax.fori_loop(0, nb, give, 0)
    for jp in range(nb, 2 * nb):
        for which in (0, 1):
            for cp in pull(jp, which):
                cp.start()
    for cp in loads[2:]:
        cp.start()
    lax.fori_loop(0, nb, take, 0)
    lax.fori_loop(0, nb, give_out, 0)
    lax.fori_loop(0, nb, take_out, 0)
    for jp in range(nb, 2 * nb):
        for which in (0, 1):
            for cp in pull(jp, which):
                cp.wait()
    lax.fori_loop(0, hidden // 256, down_grads, 0)
    down_ring.start()
    for cp in loads[2:]:
        cp.wait()
    lax.fori_loop(nb, 2 * nb, give, 0)
    lax.fori_loop(nb, 2 * nb, take, 0)
    down_ring.forward(2)
    lax.fori_loop(0, nb - 1, tail, 0)
    lax.fori_loop(nb, 2 * nb, give_out, 0)
    lax.fori_loop(nb, 2 * nb, take_out, 0)
    down_ring.forward(3)
    lax.fori_loop(0, half, up_grads, 0)
    lax.fori_loop(nb - 1, nb, tail, 0)
    lax.fori_loop(half, 2 * half, up_grads, 0)
    keep_all = []
    for i, (src, dst) in enumerate(
        ((d_mid, d_mid_h), (base, base_h), (osend, osend_h), (dat.at[s], d_heads.at[s]))
    ):
        cp = pltpu.make_async_copy(src, dst, keeps.at[i])
        cp.start()
        keep_all.append(cp)
    down_ring.forward(4)
    branch = d_mid[...].astype(BF).reshape(nb * tl, D)
    for j in range(4):
        left = jnp.concatenate([attn[b, j] for b in range(nb)], axis=0)
        up_copy(j).wait()
        stage[j] = mm_tn(left, branch).astype(BF)
        pltpu.make_async_copy(stage.at[j], grad_out.at[j], os_.at[j]).start()

    def done(jp, _):
        back_copy(jp).wait_send()
        out_copy(jp).wait_send()
        return 0

    lax.fori_loop(0, 2 * nb, done, 0)
    s_down[...] = down_ring.result()
    down_ring.drain()
    for b in range(nb):
        far_copy(b).wait_send()
        for e, other in ((0, s2), (1, s3), (2, s1)):
            spread(e, other, b).wait()
    for j in range(4):
        pltpu.make_async_copy(stage.at[j], grad_out.at[j], os_.at[j]).wait()
    for cp in keep_all:
        cp.wait()


def run_k2(nd, act, slope, htwo, mid, attn_rows, cot_all, modul, w_out, w_up, w_down):
    nb, _, tl, width = cot_all.shape
    hidden = w_up.shape[1]
    cols = attn_rows.shape[3]
    pc = width // nd
    vm = pl.BlockSpec(memory_space=pltpu.VMEM)
    hb = pl.BlockSpec(memory_space=pl.ANY)
    sds = jax.ShapeDtypeStruct
    v = pltpu.VMEM
    dma = pltpu.SemaphoreType.DMA
    return pl.pallas_call(
        k2_body,
        out_shape=(
            sds((width, hidden), BF),
            sds((4, cols, width), BF),
            sds((nb, tl, width), F32),
            sds((nb, tl, width), F32),
            sds((nb, tl, width), BF),
            sds((4, nb, tl, cols), BF),
            sds((nb, width), F32),
            sds((hidden, pc), F32),
        ),
        in_specs=[hb, hb, hb, hb, hb, hb, vm, hb, hb, hb],
        out_specs=(hb, hb, hb, hb, hb, hb, vm, vm),
        scratch_shapes=[
            v(act.shape, BF),
            v(slope.shape, BF),
            v(htwo.shape, BF),
            v(mid.shape, F32),
            v(attn_rows.shape, BF),
            v(cot_all.shape, BF),
            v(w_out.shape, BF),
            v(w_up.shape, BF),
            v(w_down.shape, BF),
            v((nb, tl, width), F32),
            v((nb, tl, width), F32),
            v((nb, tl, width), BF),
            v((2 * nb, tl, width), BF),
            v((2 * nb, tl, width), BF),
            v((2 * nb, tl, width), BF),
            v((2 * nb, tl, width), BF),
            v((nb, tl, width), BF),
            v((nb, tl, width), BF),
            v((4, nb, tl, cols), BF),
            v((4, 256, width), BF),
            v((hidden, width), BF),
            v((2, hidden // 2, pc), BF),
            v((6, hidden, pc), BF),
            dma,
            dma((16,)),
            dma((16,)),
            dma((4,)),
            dma((6,)),
            dma((4,)),
            dma((3, 4 * nb)),
            dma((8,)),
            dma((8,)),
        ],
        compiler_params=pltpu.CompilerParams(
            collective_id=1, has_side_effects=True, vmem_limit_bytes=VMEM_LIMIT
        ),
        name="feed_forward",
    )(act, slope, htwo, mid, attn_rows, cot_all, modul, w_out, w_up, w_down)


def k3_body(
    fields_h, lse, attn_h, d_heads_h, w_h, normed_h, tok_h, modul, cs_h, sn_h, d_mid_h, base_h, osend,
    g_up, g_out, dsc_h, feats,
    output, grad_tok, s_qkv, s_out, s_up, s_time,
    orecv, dqt, draw, pa, ra, xs, xr, sumh, dhb,
    vu, vo, vq, oa, ob, ox, osum, up_h, up_w, out_h, out_w, qkv_h, qkv_w,
    dpart, tx, dall, qkv, own, d_heads, w, normed_one, tok, cs, sn, d_mid, base, dsc_two,
    ins, ls, ss, rs, gs, gr,
):
    g, s, core, s1, s2, s3 = peers()
    chip = s // 2
    p = ring_place(g)
    nd = dall.shape[0]
    loads = [
        pltpu.make_async_copy(g_up, vu, ls.at[0]),
        pltpu.make_async_copy(g_out, oa, ls.at[1]),
    ]
    pulls = []
    for i, (src, dst) in enumerate(
        (
            (fields_h, qkv), (attn_h, own), (d_heads_h, d_heads), (cs_h, cs), (sn_h, sn),
            (w_h, w), (normed_h, normed_one), (tok_h, tok), (d_mid_h, d_mid), (base_h, base),
            (dsc_h, dsc_two),
        )
    ):
        pulls.append(pltpu.make_async_copy(src, dst, ins.at[i]))
    for cp in pulls[:3]:
        cp.start()
    for cp in loads:
        cp.start()
    for cp in pulls[3:]:
        cp.start()
    others = [(lax.rem(g + d, nd), s) for d in range(1, nd)]
    greet([(g, s1), (g, s2)] + others)
    nb, tl = tok.shape[0], tok.shape[1]
    rows, cols = own.shape[1], own.shape[2]
    heads = cols // HD
    blk = 256
    nk = rows // blk
    pc = D // nd

    def lanes(j, size):
        return pl.ds(pl.multiple_of(j * size, size), size)

    def view_cols(ref, size):
        def view(j, half):
            lo, n = (0, size) if half is None else (half * (size // 2), size // 2)
            return ref.at[lo : lo + n, lanes(j, pc)]

        return view

    def view_rows(ref):
        def view(j, half):
            lo, n = (0, pc) if half is None else (half * (pc // 2), pc // 2)
            return ref.at[pl.ds(pl.multiple_of(j * pc + lo, n), n)]

        return view

    up_ring = Scatter(view_rows(vu), up_h, up_w, gs, gr, 16)
    out_rings = [
        Scatter(view_cols(vo.at[i], vo.shape[1]), out_h.at[i], out_w.at[i], gs, gr, 8 * i)
        for i in range(2)
    ]
    def view_qkv(side):
        wide = vq.shape[1] // 2

        def view(j, half):
            lo, n = (0, pc) if half is None else (half * (pc // 2), pc // 2)
            return vq.at[
                pl.ds(pl.multiple_of(j * pc + lo, n), n), side * wide : (side + 1) * wide
            ]

        return view

    qkv_rings = [
        Scatter(view_qkv(i), qkv_h.at[i], qkv_w.at[i], gs, gr, 24 + 16 * i) for i in range(2)
    ]

    def qkv_forward(k):
        for ring in qkv_rings:
            ring.forward(k)

    loads[0].wait()
    up_ring.start()
    back = []
    for b in range(nb):
        cp = remote(osend.at[b], orecv.at[b], ss, rs, b, (g, s2))
        cp.start()
        back.append(cp)
    loads[1].wait()
    cross = []
    for i in range(2):
        cp = remote(oa.at[2 * i + 1 - core], ob.at[i], ss, rs, 8 + i, (g, s1))
        cp.start()
        cross.append(cp)
    over = remote(osum, ox, ss, rs, 10, (g, s2))

    def out_pair():
        for i in range(2):
            cross[i].wait_recv()
            vo[i] = (oa[2 * i + core].astype(F32) + ob[i].astype(F32)).astype(BF)
            out_rings[i].start()

    def out_forward(k):
        for ring in out_rings:
            ring.forward(k)

    lane = lax.broadcasted_iota(jnp.int32, (1, cols), 1)

    def near_copy(b, phase):
        i = 2 * b + phase
        return remote(pa.at[i], ra.at[i], ss, rs, 2 + i, (g, s1))

    def far_copy(b):
        return remote(xs.at[b], xr.at[b], ss, rs, 6 + b, (g, s2))

    for cp in pulls[:5]:
        cp.wait()
    out_pair()

    def grads(side):
        wide = vq.shape[1] // 2
        c = slice(side * wide, (side + 1) * wide)

        def one(i, _):
            r = pl.ds(pl.multiple_of(i * 256, 256), 256)
            left = jnp.concatenate(
                [
                    (normed_one[b, :, r].astype(F32) * (1.0 + modul[b : b + 1, r])).astype(BF)
                    for b in range(nb)
                ],
                axis=0,
            )
            vq[r, c] = mm_tn(left, draw[:, :, c].reshape(nb * rows, wide)).astype(BF)
            return 0

        lax.fori_loop(0, D // 256, one, 0)
        qkv_rings[side].start()

    def sequence(b, _):
        for j in range(4):
            dhb[j * tl : (j + 1) * tl] = d_heads[j, b]
        query = qkv[b, 0]
        d_out = dhb[...]
        prod = d_out.astype(F32) * own[b].astype(F32)
        prod = prod.T
        delta = jnp.concatenate(
            [jnp.sum(prod[h * HD : (h + 1) * HD], axis=0, keepdims=True) for h in range(heads)],
            axis=0,
        )
        dqt[...] = jnp.zeros_like(dqt)

        def keys_block(i, _):
            it = b * nk + i
            for when, act in (
                (2, lambda: up_ring.forward(2)),
                (3, lambda: out_forward(2)),
                (4, lambda: up_ring.forward(3)),
                (5, lambda: out_forward(3)),
                (6, lambda: up_ring.forward(4)),
                (7, lambda: out_forward(4)),
            ):

                @pl.when(it == when)
                def _(act=act):
                    act()

            r = pl.ds(pl.multiple_of(i * blk, blk), blk)
            keys, values = qkv[b, 1, r], qkv[b, 2, r]
            dk = jnp.zeros((blk, cols), F32)
            dv = jnp.zeros((blk, cols), F32)
            for h in range(heads):
                mask = lax.rem(lane, 128) // 32 == h
                mask_v = lane // HD == h
                km = jnp.where(mask, keys, jnp.zeros_like(keys))
                vmask = jnp.where(mask_v, values, jnp.zeros_like(values))
                probs = jnp.exp2(mm_nt(km, query) - lse[b, h : h + 1])
                d_probs = mm_nt(vmask, d_out)
                ds = (probs * (d_probs - delta[h : h + 1])).astype(BF)
                dv = jnp.where(mask_v, mm(probs.astype(BF), d_out), dv)
                dk = jnp.where(mask, mm(ds, query), dk)
                dqt[...] += mm_tn(km, ds)
            c, n = cs[r] * math.log(2.0), sn[r] * math.log(2.0)
            da, db = dk[:, :128], dk[:, 128:]
            draw[b, r, 256:512] = jnp.concatenate([da * c + db * n, db * c - da * n], axis=1).astype(BF)
            draw[b, r, 512:768] = dv.astype(BF)
            return 0

        lax.fori_loop(0, nk, keys_block, 0)
        dq = dqt[...].T * 0.125
        da, db = dq[:, :128], dq[:, 128:]
        c, n = cs[...], sn[...]
        draw[b, :, 0:256] = jnp.concatenate([da * c + db * n, db * c - da * n], axis=1).astype(BF)

        @pl.when(b == 0)
        def _():
            for cp in pulls[5:]:
                cp.wait()
            dpart[0, :, :D] = jnp.zeros((nb, D), F32)

        def part(owner):
            r = pl.ds(pl.multiple_of(owner * tl, tl), tl)
            res = mm_nt(draw[b, r], w[...])
            dpart[0, pl.ds(b, 1), :D] += jnp.sum(
                res * normed_one[b, r].astype(F32), axis=0, keepdims=True
            )
            return res

        for phase in range(2):
            where = chip if phase else 1 - chip
            pa[2 * b + phase] = part(2 * where + 1 - core).astype(BF)
            near_copy(b, phase).start()
        kept = part(2 * (1 - chip) + core)
        near_copy(b, 0).wait_recv()
        xs[b] = (kept + ra[2 * b].astype(F32)).astype(BF)
        far_copy(b).start()

        @pl.when(b == nb - 1)
        def _():
            grads(0)
            grads(1)

        kept = part(2 * chip + core)
        near_copy(b, 1).wait_recv()
        sumh[b] = kept + ra[2 * b + 1].astype(F32)
        return 0

    lax.fori_loop(0, nb, sequence, 0)
    dpart[0, :, D:] = dsc_two[...]
    small = [remote(dpart.at[0], dpart.at[1], ss, rs, 11, (g, s1))]
    small[0].start()
    first_out, second_out = out_rings[0].result(), out_rings[1].result()
    osum[...] = jnp.where(chip == 0, second_out, first_out).astype(BF)
    own_out = jnp.where(chip == 0, first_out, second_out)
    over.start()
    qkv_forward(2)
    small[0].wait_recv()
    dall[0, :, : 2 * D] = dpart[0] + dpart[1]
    dall[0, :, 2 * D :] = feats[...]
    wide = [remote(dall.at[0], dall.at[d], ss, rs, 12 + d, others[d - 1]) for d in range(1, nd)]
    for cp in wide:
        cp.start()
    for b in range(nb):
        back[b].wait_recv()
        output[b] = (base[b] + orecv[b].astype(F32)).astype(BF)
    s_up[...] = up_ring.result()
    qkv_forward(3)

    def tail(b, _):
        scale = 1.0 + modul[pl.ds(b, 1), :D]
        far_copy(b).wait_recv()
        normed, inverse = moments(tok[b].astype(F32))
        dn = (sumh[b] + xr[b].astype(F32)) * scale
        inner = jnp.mean(dn * normed, axis=-1, keepdims=True)
        grad_tok[b] = (
            d_mid[b]
            + inverse * (dn - jnp.mean(dn, axis=-1, keepdims=True) - normed * inner)
        ).astype(BF)
        return 0

    lax.fori_loop(0, nb - 1, tail, 0)
    qkv_forward(4)
    lax.fori_loop(nb - 1, nb, tail, 0)
    over.wait_recv()
    s_out[...] = own_out + ox[...].astype(F32)
    for cp in wide:
        cp.wait_recv()
    depth = s_time.shape[0]
    lane_t = lax.broadcasted_iota(jnp.int32, (depth, TF), 1)
    row_t = lax.broadcasted_iota(jnp.int32, (depth, TF), 0)
    mine = jnp.zeros((depth, 2 * D), F32)
    theirs = jnp.zeros((depth, 2 * D), F32)
    for d in range(nd):
        for b in range(nb):
            row = dall[d, b : b + 1]
            for which, other in ((0, s), (1, s2)):
                hit = lane_t == row_t + (4 * g + other) * depth
                column = jnp.sum(jnp.where(hit, row[:, 2 * D :], 0.0), axis=1, keepdims=True)
                if which:
                    theirs = theirs + column * row[:, : 2 * D]
                else:
                    mine = mine + column * row[:, : 2 * D]
    tx[0] = theirs
    swap = remote(tx.at[0], tx.at[1], ss, rs, 12, (g, s2))
    swap.start()
    s_qkv[...] = jnp.concatenate([ring.result() for ring in qkv_rings], axis=1)
    swap.wait_recv()
    s_time[...] = mine + tx[1]
    for b in range(nb):
        back[b].wait_send()
        far_copy(b).wait_send()
        for phase in range(2):
            near_copy(b, phase).wait_send()
    for cp in cross + small + wide + [over, swap]:
        cp.wait_send()
    for ring in out_rings + qkv_rings + [up_ring]:
        ring.drain()


def run_k3(
    nd, qkv, lse, attn_heads, d_heads, w, normed, tokens, modul, cs, sn, d_mid, base, osend,
    g_up, g_out, dsc_two, feats,
):
    nb, tl, width = tokens.shape
    rows, cols = attn_heads.shape[1], attn_heads.shape[2]
    hidden = g_up.shape[1]
    pc = width // nd
    vm = pl.BlockSpec(memory_space=pltpu.VMEM)
    hb = pl.BlockSpec(memory_space=pl.ANY)
    sds = jax.ShapeDtypeStruct
    v = pltpu.VMEM
    dma = pltpu.SemaphoreType.DMA
    return pl.pallas_call(
        k3_body,
        out_shape=(
            sds((nb, tl, width), BF),
            sds((nb, tl, width), BF),
            sds((pc, 3 * cols), F32),
            sds((cols, pc), F32),
            sds((pc, hidden), F32),
            sds((TF // (4 * nd), 2 * width), F32),
        ),
        in_specs=[hb, vm, hb, hb, hb, hb, hb, vm, hb, hb, hb, hb, hb, hb, hb, pl.BlockSpec(memory_space=pltpu.HBM), vm],
        out_specs=(vm,) * 6,
        scratch_shapes=[
            v((nb, tl, width), BF),
            v((cols, rows), F32),
            v((nb, rows, 3 * cols), BF),
            v((2 * nb, tl, width), BF),
            v((2 * nb, tl, width), BF),
            v((nb, tl, width), BF),
            v((nb, tl, width), BF),
            v((nb, tl, width), F32),
            v((rows, cols), BF),
            v((width, hidden), BF),
            v((2, cols, width), BF),
            v((width, 3 * cols), BF),
            v((4, cols, width), BF),
            v((2, cols, width), BF),
            v((cols, pc), BF),
            v((cols, pc), BF),
            v((2, pc // 2, hidden), BF),
            v((6, pc, hidden), BF),
            v((2, 2, cols // 2, pc), BF),
            v((2, 6, cols, pc), BF),
            v((2, 2, pc // 2, 3 * cols // 2), BF),
            v((2, 6, pc, 3 * cols // 2), BF),
            v((2, nb, 2 * width), F32),
            v((2, TF // (4 * nd), 2 * width), F32),
            v((nd, nb, 2 * width + TF), F32),
            v(qkv.shape, BF),
            v((nb, rows, cols), BF),
            v(d_heads.shape, BF),
            v(w.shape, BF),
            v(normed.shape, BF),
            v(tokens.shape, BF),
            v(cs.shape, F32),
            v(sn.shape, F32),
            v(d_mid.shape, F32),
            v(base.shape, F32),
            v(dsc_two.shape, F32),
            dma((11,)),
            dma((2,)),
            dma((20,)),
            dma((20,)),
            dma((48,)),
            dma((48,)),
        ],
        compiler_params=pltpu.CompilerParams(
            collective_id=2, has_side_effects=True, vmem_limit_bytes=52 * 1024 * 1024
        ),
        name="attention_backward",
    )(
        qkv, lse, attn_heads, d_heads, w, normed, tokens, modul, cs, sn, d_mid, base, osend,
        g_up, g_out, dsc_two, feats,
    )


def k4_body(*refs):
    *refs, sems = refs
    count = len(refs) // 2
    moves = []
    for i in range(2):
        moves.append(pltpu.make_async_copy(refs[i], refs[count + i], sems.at[i]))
        moves[i].start()
    for i in range(3, count):
        refs[count + i][...] = refs[i][...]
    w = refs[2][...]
    heads = w.shape[1] // (3 * HD)
    half, size = HD // 2, heads * HD
    pieces = []
    for h in range(heads):
        for part in (0, 1):
            for side in (0, 1):
                at = part * size + side * (size // 2) + h * half
                pieces.append(w[:, at : at + half])
        at = 2 * size + h * HD
        pieces.append(w[:, at : at + HD])
    refs[count + 2][...] = jnp.concatenate(pieces, axis=1)
    for cp in moves:
        cp.wait()


def run_k4(arrays):
    vm = pl.BlockSpec(memory_space=pltpu.VMEM)
    hb = pl.BlockSpec(memory_space=pltpu.HBM)
    specs = [hb, hb] + [vm] * (len(arrays) - 2)
    return pl.pallas_call(
        k4_body,
        out_shape=tuple(jax.ShapeDtypeStruct(a.shape, a.dtype) for a in arrays),
        in_specs=specs,
        out_specs=tuple(specs),
        scratch_shapes=[pltpu.SemaphoreType.DMA((2,))],
        compiler_params=pltpu.CompilerParams(vmem_limit_bytes=16 * 1024 * 1024),
        name="results",
    )(*arrays)


def fast_shards(nd, tokens, bins, plan, w_qkv, w_out, w_up, w_down, w_time, cotangent):
    nb, tl, width = tokens.shape
    rows = 4 * tl
    feats = time_features(plan, bins).astype(BF).astype(F32)
    half = HD // 2
    inverse = np.exp(np.arange(half, dtype=np.float32) * np.float32(-math.log(10000.0) / half))
    angle = np.arange(rows, dtype=np.float32)[:, None] * inverse.astype(np.float32)[None, :]
    cs = np.tile(np.cos(angle.astype(np.float64)).astype(np.float32), (1, 128 // half))
    sn = np.tile(np.sin(angle.astype(np.float64)).astype(np.float32), (1, 128 // half))
    (
        modul, feats, full_qkv, full_out, full_up, full_down, normed, qkv, lse, attn_heads, attn_rows,
        cot_all, act, slope, htwo, mid,
    ) = run_k1(
        nd, tokens, w_time, feats, w_qkv, w_out, w_up, w_down, cs, sn, cotangent
    )
    grad_up, grad_out, d_mid, base, osend, d_heads, dsc_two, sum_down = run_k2(
        nd, act, slope, htwo, mid, attn_rows, cot_all, modul, full_out, full_up, full_down
    )
    output, grad_tokens, sum_qkv, sum_out, sum_up, grad_time = run_k3(
        nd, qkv, lse, attn_heads, d_heads, full_qkv, normed, tokens, modul, cs, sn, d_mid, base,
        osend, grad_up, grad_out, dsc_two, feats,
    )
    return tuple(
        run_k4((output, grad_tokens, sum_qkv, sum_out, sum_up, sum_down, grad_time))
    )


def solution(mesh):
    nd, ns = mesh.shape["dp"], mesh.shape["seq"]
    fast = nd == 8 and ns == 4
    return jax.shard_map(
        functools.partial(fast_shards, nd) if fast else shards,
        mesh=mesh,
        in_specs=(
            P("dp", "seq", None),
            P("dp"),
            P(),
            P("dp", "seq"),
            P("seq", "dp"),
            P("dp", "seq"),
            P("seq", "dp"),
            P(("dp", "seq"), None),
            P("dp", "seq", None),
        ),
        out_specs=(
            P("dp", "seq", None),
            P("dp", "seq", None),
            P("dp", "seq"),
            P("seq", "dp"),
            P("dp", "seq"),
            P("seq", "dp"),
            P(("dp", "seq"), None),
        ),
        check_vma=False,
    )
```

```python
import functools
import math

import jax
import jax.numpy as jnp
import numpy as np
from jax import lax
from jax.experimental import pallas as pl
from jax.experimental.pallas import tpu as pltpu
from jax.sharding import PartitionSpec as P

D = 1024
HD = 64
TF = 256
LEN = 1024


EPSILON = 1e-05
HIGHEST = lax.Precision.HIGHEST
ROOT_HALF = 0.7071067811865476
DENSITY = 0.3989422804014327


def time_features(plan, bins):
    table = jnp.arange(plan.shape[0], dtype=jnp.int32)
    picked = jnp.where(bins[:, None] == table[None, :], plan[None, :], 0.0)
    sigma = jnp.sum(picked, axis=1)
    level = 0.25 * jnp.log(sigma)
    count = TF // 2
    freqs = jnp.exp(jnp.arange(count, dtype=jnp.float32) * (math.log(1000.0) / count))
    angles = level[:, None] * freqs[None, :]
    return jnp.concatenate([jnp.sin(angles), jnp.cos(angles)], axis=1)


def normalize(field):
    centered = field - jnp.mean(field, axis=-1, keepdims=True)
    spread = jnp.mean(centered * centered, axis=-1, keepdims=True)
    inverse = lax.rsqrt(spread + EPSILON)
    return (centered * inverse, inverse)


def norm_backward(grad_scaled, normed, inverse, scale):
    grad_normed = grad_scaled * scale
    grad_scale = jnp.sum(grad_scaled * normed, axis=1)
    inner = jnp.mean(grad_normed * normed, axis=-1, keepdims=True)
    grad_field = inverse * (
        grad_normed - jnp.mean(grad_normed, axis=-1, keepdims=True) - normed * inner
    )
    return (grad_field, grad_scale)


def rotate(field, cosine, sine):
    half = HD // 2
    first = field[..., :half]
    second = field[..., half:]
    return jnp.concatenate(
        [first * cosine - second * sine, second * cosine + first * sine], axis=-1
    )


def rotary_tables(places):
    half = HD // 2
    inverse = jnp.exp(jnp.arange(half, dtype=jnp.float32) * (-math.log(10000.0) / half))
    angle = places[:, None] * inverse[None, :]
    return (jnp.cos(angle)[:, None, None, :], jnp.sin(angle)[:, None, None, :])


def pack_heads(h_one, qkv_weight, cosine, sine):
    seqs, rows, width = h_one.shape
    raw = jnp.einsum("std,de->ste", h_one, qkv_weight, preferred_element_type=jnp.float32)
    local_heads = qkv_weight.shape[1] // (3 * HD)
    raw = raw.reshape(seqs, rows, local_heads, 3, HD)
    turned = rotate(raw[:, :, :, 0:2], cosine, sine)
    packed = jnp.concatenate([turned, raw[:, :, :, 2:3]], axis=3).astype(jnp.bfloat16)
    return packed.reshape(seqs, rows, local_heads * 3 * HD)


def unpack_grads(grad_packed, cosine, sine):
    seqs, rows, width = grad_packed.shape
    local_heads = width // (3 * HD)
    grad_fields = grad_packed.reshape(seqs, rows, local_heads, 3, HD).astype(jnp.float32)
    unturned = rotate(grad_fields[:, :, :, 0:2], cosine, -sine)
    grad_raw = jnp.concatenate([unturned, grad_fields[:, :, :, 2:3]], axis=3).astype(jnp.bfloat16)
    return grad_raw.reshape(seqs, rows, width)


def gelu_slope(upper):
    return 0.5 * (1.0 + lax.erf(upper * ROOT_HALF)) + upper * DENSITY * jnp.exp(
        -0.5 * upper * upper
    )


def attend_sequence(fields):
    local_heads = fields.shape[1]
    block = min(512, LEN)
    count = LEN // block
    keys = fields[:, :, 1]
    values = fields[:, :, 2]
    query_blocks = fields[:, :, 0].reshape(count, block, local_heads, HD)

    def attend_one_block(query_blk):
        scores = jnp.einsum(
            "qhd,khd->hqk", query_blk, keys, preferred_element_type=jnp.float32
        ) * HD ** (-0.5)
        top = jnp.max(scores, axis=-1, keepdims=True)
        expo = jnp.exp(scores - top)
        totals = jnp.sum(expo, axis=-1, keepdims=True)
        probs = (expo / totals).astype(jnp.bfloat16)
        result = jnp.einsum("hqk,khd->qhd", probs, values, preferred_element_type=jnp.float32)
        return (result.astype(jnp.bfloat16), (top + jnp.log(totals))[:, :, 0])

    results, logsums = lax.map(attend_one_block, query_blocks)
    logsums = jnp.transpose(logsums, (1, 0, 2)).reshape(local_heads, LEN)
    return (results.reshape(LEN, local_heads, HD), logsums)


def attend_all(packed_heads):
    items = packed_heads.shape[0]
    local_heads = packed_heads.shape[2] // (3 * HD)
    fields = packed_heads.reshape(items, LEN, local_heads, 3, HD)
    results, logsums = lax.map(attend_sequence, fields)
    return (results.reshape(items, LEN, local_heads * HD), logsums)


def back_sequence(pieces):
    fields, logsums, grad_heads = pieces
    local_heads = fields.shape[1]
    block = min(512, LEN)
    count = LEN // block
    keys = fields[:, :, 1]
    values = fields[:, :, 2]
    query_blocks = fields[:, :, 0].reshape(count, block, local_heads, HD)
    grad_blocks = grad_heads.reshape(count, block, local_heads, HD)
    sum_blocks = jnp.transpose(logsums.reshape(local_heads, count, block), (1, 0, 2))

    def back_one_block(carry, piece):
        key_acc, value_acc = carry
        query_blk, grad_blk, sum_blk = piece
        scores = jnp.einsum(
            "qhd,khd->hqk", query_blk, keys, preferred_element_type=jnp.float32
        ) * HD ** (-0.5)
        probs = jnp.exp(scores - sum_blk[:, :, None])
        grad_probs = jnp.einsum(
            "qhd,khd->hqk", grad_blk, values, preferred_element_type=jnp.float32
        )
        inner = jnp.sum(probs * grad_probs, axis=-1, keepdims=True)
        grad_scores = (probs * (grad_probs - inner)).astype(jnp.bfloat16)
        grad_query = jnp.einsum(
            "hqk,khd->qhd", grad_scores, keys, preferred_element_type=jnp.float32
        ) * HD ** (-0.5)
        key_acc = key_acc + jnp.einsum(
            "hqk,qhd->khd", grad_scores, query_blk, preferred_element_type=jnp.float32
        ) * HD ** (-0.5)
        value_acc = value_acc + jnp.einsum(
            "hqk,qhd->khd", probs.astype(jnp.bfloat16), grad_blk, preferred_element_type=jnp.float32
        )
        return ((key_acc, value_acc), grad_query)

    empty = jnp.zeros((LEN, local_heads, HD), jnp.float32)
    (grad_keys, grad_values), grad_queries = lax.scan(
        back_one_block, (empty, empty), (query_blocks, grad_blocks, sum_blocks)
    )
    grad_queries = grad_queries.reshape(LEN, local_heads, HD)
    return jnp.stack([grad_queries, grad_keys, grad_values], axis=2).astype(jnp.bfloat16)


def back_all(packed_heads, logsums, grad_heads):
    items = packed_heads.shape[0]
    local_heads = packed_heads.shape[2] // (3 * HD)
    fields = packed_heads.reshape(items, LEN, local_heads, 3, HD)
    grads = grad_heads.reshape(items, LEN, local_heads, HD)
    result = lax.map(back_sequence, (fields, logsums, grads))
    return result.reshape(items, LEN, local_heads * 3 * HD)


def data_layer(
    tokens, cotangent, w_qkv, w_up, w_out, w_down, scale_one, scale_two, norm_one, inverse_one
):
    seqs, local_len, width = tokens.shape
    wide = (
        lax.all_gather(w_qkv, "seq", axis=1, tiled=True),
        lax.all_gather(w_up, "seq", axis=1, tiled=True),
        lax.all_gather(w_out, "seq", axis=0, tiled=True),
        lax.all_gather(w_down, "seq", axis=0, tiled=True),
    )
    full_qkv, full_up, full_out, full_down = (
        lax.all_gather(wide[0], "dp", axis=0, tiled=True),
        lax.all_gather(wide[1], "dp", axis=0, tiled=True),
        lax.all_gather(wide[2], "dp", axis=1, tiled=True),
        lax.all_gather(wide[3], "dp", axis=1, tiled=True),
    )
    field = tokens.astype(jnp.float32)
    h_one = (norm_one * scale_one).astype(jnp.bfloat16)
    places = (lax.axis_index("seq") * local_len + jnp.arange(local_len, dtype=jnp.int32)).astype(
        jnp.float32
    )
    cosine, sine = rotary_tables(places)
    packed = pack_heads(h_one, full_qkv, cosine, sine)
    packed_heads = lax.all_to_all(packed, "seq", split_axis=2, concat_axis=1, tiled=True)
    results, logsums = attend_all(packed_heads)
    back_tokens = lax.all_to_all(results, "seq", split_axis=1, concat_axis=2, tiled=True)
    middle = field + jnp.einsum(
        "std,de->ste", back_tokens, full_out, preferred_element_type=jnp.float32
    )
    norm_two, inverse_two = normalize(middle)
    h_two = (norm_two * scale_two).astype(jnp.bfloat16)
    upper = jnp.einsum("std,df->stf", h_two, full_up, preferred_element_type=jnp.float32)
    active = jax.nn.gelu(upper, approximate=False).astype(jnp.bfloat16)
    output = (
        middle + jnp.einsum("stf,fd->std", active, full_down, preferred_element_type=jnp.float32)
    ).astype(jnp.bfloat16)
    grad_down = jnp.einsum("stf,std->fd", active, cotangent, preferred_element_type=jnp.float32)
    grad_active = jnp.einsum(
        "std,fd->stf", cotangent, full_down, preferred_element_type=jnp.float32
    )
    grad_upper = (grad_active * gelu_slope(upper)).astype(jnp.bfloat16)
    grad_up = jnp.einsum("std,stf->df", h_two, grad_upper, preferred_element_type=jnp.float32)
    grad_htwo = jnp.einsum("stf,df->std", grad_upper, full_up, preferred_element_type=jnp.float32)
    grad_middle, grad_scale_two = norm_backward(grad_htwo, norm_two, inverse_two, scale_two)
    grad_middle = grad_middle + cotangent.astype(jnp.float32)
    grad_branch = grad_middle.astype(jnp.bfloat16)
    grad_out = jnp.einsum(
        "std,ste->de", back_tokens, grad_branch, preferred_element_type=jnp.float32
    )
    grad_attended = jnp.einsum(
        "ste,de->std", grad_branch, full_out, preferred_element_type=jnp.float32
    ).astype(jnp.bfloat16)
    grad_heads = lax.all_to_all(grad_attended, "seq", split_axis=2, concat_axis=1, tiled=True)
    grad_packed_heads = back_all(packed_heads, logsums, grad_heads)
    grad_packed = lax.all_to_all(grad_packed_heads, "seq", split_axis=1, concat_axis=2, tiled=True)
    grad_raw = unpack_grads(grad_packed, cosine, sine)
    grad_qkv = jnp.einsum("std,ste->de", h_one, grad_raw, preferred_element_type=jnp.float32)
    grad_hone = jnp.einsum("ste,de->std", grad_raw, full_qkv, preferred_element_type=jnp.float32)
    grad_field, grad_scale_one = norm_backward(grad_hone, norm_one, inverse_one, scale_one)
    grad_tokens = (grad_middle + grad_field).astype(jnp.bfloat16)
    partial_sums = (
        lax.psum_scatter(
            grad_qkv.astype(jnp.bfloat16), "dp", scatter_dimension=0, tiled=True
        ).astype(jnp.float32),
        lax.psum_scatter(
            grad_up.astype(jnp.bfloat16), "dp", scatter_dimension=0, tiled=True
        ).astype(jnp.float32),
        lax.psum_scatter(
            grad_out.astype(jnp.bfloat16), "dp", scatter_dimension=1, tiled=True
        ).astype(jnp.float32),
        lax.psum_scatter(
            grad_down.astype(jnp.bfloat16), "dp", scatter_dimension=1, tiled=True
        ).astype(jnp.float32),
    )
    sums = (
        lax.psum_scatter(
            partial_sums[0].astype(jnp.bfloat16), "seq", scatter_dimension=1, tiled=True
        ).astype(jnp.float32),
        lax.psum_scatter(
            partial_sums[1].astype(jnp.bfloat16), "seq", scatter_dimension=1, tiled=True
        ).astype(jnp.float32),
        lax.psum_scatter(
            partial_sums[2].astype(jnp.bfloat16), "seq", scatter_dimension=0, tiled=True
        ).astype(jnp.float32),
        lax.psum_scatter(
            partial_sums[3].astype(jnp.bfloat16), "seq", scatter_dimension=0, tiled=True
        ).astype(jnp.float32),
    )
    return (output, grad_tokens, grad_scale_one, grad_scale_two, sums)


def shards(tokens, bins, plan, w_qkv, w_out, w_up, w_down, w_time, cotangent):
    feats = time_features(plan, bins).astype(jnp.bfloat16)
    full_time = lax.all_gather(w_time, ("dp", "seq"), axis=0, tiled=True)
    modul = jnp.dot(feats, full_time, preferred_element_type=jnp.float32)
    scale_one = 1.0 + modul[:, None, :D]
    scale_two = 1.0 + modul[:, None, D:]
    norm_one, inverse_one = normalize(tokens.astype(jnp.float32))
    output, grad_tokens, grad_scale_one, grad_scale_two, sums = data_layer(
        tokens, cotangent, w_qkv, w_up, w_out, w_down, scale_one, scale_two, norm_one, inverse_one
    )
    grad_scales = jnp.concatenate([grad_scale_one, grad_scale_two], axis=1)
    grad_time = jnp.dot(feats.astype(jnp.float32).T, grad_scales, precision=HIGHEST)
    time_sum = lax.psum_scatter(grad_time, ("dp", "seq"), scatter_dimension=0, tiled=True)
    return (output, grad_tokens, sums[0], sums[2], sums[1], sums[3], time_sum)


BF = jnp.bfloat16
F32 = jnp.float32
MESHID = pl.DeviceIdType.MESH
QUERY_SCALE = HD**-0.5 / math.log(2.0)
VMEM_LIMIT = 60 * 1024 * 1024


def mm(a, b):
    return lax.dot_general(a, b, (((1,), (0,)), ((), ())), preferred_element_type=F32)


def mm_nt(a, b):
    return lax.dot_general(a, b, (((1,), (1,)), ((), ())), preferred_element_type=F32)


def mm_tn(a, b):
    return lax.dot_general(a, b, (((0,), (0,)), ((), ())), preferred_element_type=F32)


def peers():
    g = lax.axis_index("dp")
    s = lax.axis_index("seq")
    core = lax.rem(s, 2)
    return g, s, core, s + 1 - 2 * core, lax.rem(s + 2, 4), 3 - s


def remote(src, dst, ss, rs, i, dev):
    return pltpu.make_async_remote_copy(
        src_ref=src,
        dst_ref=dst,
        send_sem=ss.at[i],
        recv_sem=rs.at[i],
        device_id=dev,
        device_id_type=MESHID,
    )


def greet(devices):
    barrier = pltpu.get_barrier_semaphore()
    for dev in devices:
        pl.semaphore_signal(barrier, inc=1, device_id=dev, device_id_type=MESHID)
    pl.semaphore_wait(barrier, len(devices))


def moments(field):
    centered = field - jnp.mean(field, axis=-1, keepdims=True)
    spread = jnp.mean(centered * centered, axis=-1, keepdims=True)
    inverse = lax.rsqrt(spread + EPSILON)
    return centered * inverse, inverse


def ring_place(g):
    z, y = g // 2, lax.rem(g, 2)
    return z + y * (7 - 2 * z)


def ring_index(p):
    p = lax.rem(p + 16, 8)
    return 2 * p + (p // 4) * (15 - 4 * p)


WAYS = (1, -1)


class Gather:
    def __init__(self, own, view, ss, rs, first):
        self.own, self.view, self.ss, self.rs, self.first = own, view, ss, rs, first

    def hop(self, k, way):
        g, s = lax.axis_index("dp"), lax.axis_index("seq")
        p = ring_place(g)
        j = ring_index(p - way * (k - 1))
        half = None if k < 4 else (0 if way > 0 else 1)
        dst = self.view(j, half)
        src = self.own if k == 1 else dst
        i = self.first + 2 * (k - 1) + (way < 0)
        return remote(src, dst, self.ss, self.rs, i, (ring_index(p + way), s))

    def start(self):
        for way in WAYS:
            self.hop(1, way).start()

    def forward(self, k):
        for way in WAYS:
            self.hop(k - 1, way).wait_recv()
            self.hop(k, way).start()

    def arrive(self):
        for way in WAYS:
            self.hop(4, way).wait_recv()

    def drain(self):
        for k in (1, 2, 3, 4):
            for way in WAYS:
                self.hop(k, way).wait_send()


class Scatter:
    def __init__(self, view, halves, wholes, ss, rs, first):
        self.view, self.halves, self.wholes = view, halves, wholes
        self.ss, self.rs, self.first = ss, rs, first

    def hop(self, k, way):
        g, s = lax.axis_index("dp"), lax.axis_index("seq")
        p = ring_place(g)
        side = 0 if way > 0 else 1
        j = ring_index(p + way * (5 - k))
        src = self.view(j, side if k == 1 else None)
        dst = self.halves.at[side] if k == 1 else self.wholes.at[3 * side + k - 2]
        i = self.first + 2 * (k - 1) + side
        return remote(src, dst, self.ss, self.rs, i, (ring_index(p + way), s))

    def start(self):
        for way in WAYS:
            self.hop(1, way).start()

    def forward(self, k):
        p = ring_place(lax.axis_index("dp"))
        for way in WAYS:
            side = 0 if way > 0 else 1
            self.hop(k - 1, way).wait_recv()
            got = self.halves.at[side] if k == 2 else self.wholes.at[3 * side + k - 3]
            mine = self.view(ring_index(p + way * (5 - k)), side if k == 2 else None)
            mine[...] = (mine[...].astype(F32) + got[...].astype(F32)).astype(BF)
            self.hop(k, way).start()

    def result(self):
        for way in WAYS:
            self.hop(4, way).wait_recv()
        mine = self.view(lax.axis_index("dp"), None)
        return mine[...].astype(F32) + (self.wholes[2].astype(F32) + self.wholes[5].astype(F32))

    def drain(self):
        for k in (1, 2, 3, 4):
            for way in WAYS:
                self.hop(k, way).wait_send()


def rows_of(ref, half, size):
    return ref if half is None else ref.at[half * (size // 2) : (half + 1) * (size // 2)]


def ordering(heads):
    half, size = HD // 2, heads * HD
    to = lax.broadcasted_iota(jnp.int32, (1, 3 * size), 1)
    part, at = to // size, lax.rem(to, size)
    side, rest = at // (size // 2), lax.rem(at, size // 2)
    turned = (rest // half) * (3 * HD) + part * HD + side * half + lax.rem(rest, half)
    plain = (at // HD) * (3 * HD) + 2 * HD + lax.rem(at, HD)
    source = jnp.where(part == 2, plain, turned)
    rows = lax.broadcasted_iota(jnp.int32, (3 * size, 3 * size), 0)
    return jnp.where(rows == source, 1.0, 0.0).astype(BF)


def k1_body(
    tok, wt, feats, w_qkv, w_out, w_up, w_down, cs, sn, cot,
    modul, feats_out, wq_out, out_all, up_all, down_all, n_out, qkv_out, lse, attn_heads, attn_rows, cot_all,
    act_out, slope_out, htwo_out, mid_out,
    tokv, wtime, pbuf, vt, cotv, wq, nv, qkv, attn, outv, upv, act, slope, htwo, mids, csv, snv,
    ks, ls, ss, rs, gs, gr, fs_, fr_, os_,
):
    g, s, core, s1, s2, s3 = peers()
    p = ring_place(g)
    nb, tl = tok.shape[0], tok.shape[1]
    rows = 4 * tl
    blk = 256
    nq = rows // blk
    heads = attn.shape[3] // HD
    nr, nc = w_out.shape[0], w_out.shape[1]

    def lanes(j, size):
        return pl.ds(pl.multiple_of(j * size, size), size)

    def view_out(other):
        def view(j, half):
            lo, size = (0, nr) if half is None else (half * (nr // 2), nr // 2)
            return outv.at[pl.ds(pl.multiple_of(other * nr + lo, size), size), lanes(j, nc)]

        return view

    def view_down(j, half):
        size = w_down.shape[0]
        lo, n = (0, size) if half is None else (half * (size // 2), size // 2)
        return down_all.at[lo : lo + n, lanes(j, w_down.shape[1])]

    def view_rows(ref, size):
        def view(j, half):
            lo, n = (0, size) if half is None else (half * (size // 2), size // 2)
            return ref.at[pl.ds(pl.multiple_of(j * size + lo, n), n)]

        return view

    def view_time(j, half):
        return wtime.at[j] if half is None else wtime.at[j, :, half * D : (half + 1) * D]

    def view_qkv(side):
        size = w_qkv.shape[0]

        def view(j, half):
            lo, n = (0, size // 2) if half is None else (half * (size // 4), size // 4)
            at = pl.multiple_of(j * size + side * (size // 2) + lo, n)
            return wq.at[pl.ds(at, n)]

        return view

    here = view_out(s)(g, None)
    time_ring = Gather(wt, view_time, gs, gr, 0)
    part = w_qkv.shape[0] // 2
    qkv_rings = [
        Gather(view_qkv(i)(g, None), view_qkv(i), gs, gr, 8 + 40 * i)
        for i in range(2)
    ]
    up_ring = Gather(w_up, view_rows(upv, w_up.shape[0]), gs, gr, 16)
    down_ring = Gather(w_down, view_down, gs, gr, 24)
    out_ring = Gather(w_out, view_out(s), gs, gr, 32)
    far_ring = Gather(view_out(s2)(g, None), view_out(s2), gs, gr, 40)

    local = [
        pltpu.make_async_copy(tok, tokv.at[:, s], ls.at[0]),
        pltpu.make_async_copy(cot, cotv, ls.at[5]),
        pltpu.make_async_copy(w_up, view_rows(upv, w_up.shape[0])(g, None), ls.at[2]),
        pltpu.make_async_copy(w_down, view_down(g, None), ls.at[3]),
        pltpu.make_async_copy(w_out, here, ls.at[4]),
        pltpu.make_async_copy(cs, csv, ls.at[6]),
        pltpu.make_async_copy(sn, snv, ls.at[7]),
    ]
    greet([(g, s1), (g, s2), (g, s3), (ring_index(p + 1), s), (ring_index(p - 1), s)])
    time_ring.start()
    pair_out = remote(w_out, here, ss, rs, 0, (g, s2))
    pair_out.start()
    far = [remote(tok.at[b], tokv.at[b, s], ss, rs, 1 + b, (g, s2)) for b in range(nb)]
    far[0].start()
    ordered = mm(w_qkv[...], ordering(heads)).astype(BF)
    wq[pl.ds(pl.multiple_of(g * w_qkv.shape[0], w_qkv.shape[0]), w_qkv.shape[0])] = ordered
    for ring in qkv_rings:
        ring.start()
    near = []
    for b in range(nb):
        cp = remote(tok.at[b], tokv.at[b, s], ss, rs, 3 + b, (g, s1))
        cp.start()
        near.append(cp)
    for cp in local:
        cp.start()
    wtime[g] = wt[...]
    pieces = [(0, 0, tl // 4), (0, tl // 4, tl)] + [(b, 0, tl) for b in range(1, nb)]

    def cot_piece(k):
        b, lo, hi = pieces[k]
        return remote(
            cotv.at[b, lo:hi], cot_all.at[b, s, lo:hi], ss, rs, 18 + k, (g, s2)
        )

    local[1].wait()
    cot_far = [cot_piece(k) for k in range(len(pieces))]
    cot_far[0].start()
    for k in (2, 3, 4):
        time_ring.forward(k)
        for ring in qkv_rings:
            ring.forward(k)
    up_ring.start()
    out_ring.start()
    pair_out.wait_recv()
    far_ring.start()
    time_ring.arrive()
    depth = wt.shape[0]
    feats_out[...] = feats[...]
    lane_t = lax.broadcasted_iota(jnp.int32, (depth, TF), 1)
    row_t = lax.broadcasted_iota(jnp.int32, (depth, TF), 0)
    sums = [jnp.zeros((depth, 2 * D), F32) for _ in range(nb)]
    for d in range(wtime.shape[0]):
        hit = lane_t == row_t + (4 * d + s) * depth
        weights = wtime[d].astype(F32)
        for b in range(nb):
            column = jnp.sum(jnp.where(hit, feats[b : b + 1], 0.0), axis=1, keepdims=True)
            sums[b] = sums[b] + weights * column
    pbuf[0] = jnp.concatenate([jnp.sum(v, axis=0, keepdims=True) for v in sums], axis=0)
    small = []
    for e, other in ((1, s1), (2, s2), (3, s3)):
        cp = remote(pbuf.at[0], pbuf.at[e], ss, rs, 4 + e, (g, other))
        cp.start()
        small.append(cp)
    far[1].start()
    cot_far[1].start()
    passed = [
        remote(tokv.at[b, s2], tokv.at[b, s2], ss, rs, 8 + b, (g, s1)) for b in range(nb)
    ]
    cot_near = [remote(cotv.at[b], cot_all.at[b, s], ss, rs, 12 + b, (g, s1)) for b in range(nb)]
    cot_pass = [
        remote(cot_all.at[b, s2], cot_all.at[b, s2], ss, rs, 14 + b, (g, s1)) for b in range(nb)
    ]
    far[0].wait_recv()
    passed[0].start()
    for c in small:
        c.wait_recv()
    modul[...] = (pbuf[0] + pbuf[1]) + (pbuf[2] + pbuf[3])
    for ring in qkv_rings:
        ring.arrive()
    for i in (0, 5, 6):
        local[i].wait()
    keep_w = pltpu.make_async_copy(wq, wq_out, ls.at[8])
    keep_w.start()
    keep_cot = pltpu.make_async_copy(cotv, cot_all.at[:, s], ls.at[9])
    keep_cot.start()

    def attn_copy(kind, it):
        b, q = it // nq, lax.rem(it, nq)
        r = pl.ds(pl.multiple_of(q * blk, blk), blk)
        ref = attn.at[b, s2 if kind == 2 else s, r]
        return remote(ref, ref, fs_.at[kind], fr_.at[kind], it, (g, s2 if kind == 0 else s1))

    lane = lax.broadcasted_iota(jnp.int32, (1, 2 * 128), 1)

    def keep_fields(b):
        return (
            pltpu.make_async_copy(nv.at[b], n_out.at[b], ks.at[0, b]),
            pltpu.make_async_copy(qkv.at[b], qkv_out.at[b], ks.at[1, b]),
        )

    def project(b):
        scale = 1.0 + modul[pl.ds(b, 1), :D]

        def one(i, _):
            r = pl.ds(pl.multiple_of(i * blk, blk), blk)
            normed, _inv = moments(tokv[b, i].astype(F32))
            nv[b, r] = normed.astype(BF)
            raw = mm((normed * scale).astype(BF), wq[...])
            c, n = csv[r], snv[r]
            qa, qb = raw[:, :128] * QUERY_SCALE, raw[:, 128:256] * QUERY_SCALE
            ka, kb = raw[:, 256:384], raw[:, 384:512]
            qkv[b, 0, r] = jnp.concatenate([qa * c - qb * n, qb * c + qa * n], axis=1).astype(BF)
            qkv[b, 1, r] = jnp.concatenate([ka * c - kb * n, kb * c + ka * n], axis=1).astype(BF)
            qkv[b, 2, r] = raw[:, 512:].astype(BF)
            return 0

        lax.fori_loop(0, nq, one, 0)

    def pass_attn(lo, hi):
        def forward(it, _):
            attn_copy(0, it).wait_recv()
            attn_copy(2, it).start()
            return 0

        lax.fori_loop(lo, hi, forward, 0)

    def arrive_attn(lo, hi):
        def forward(it, _):
            attn_copy(1, it).wait_recv()
            attn_copy(2, it).wait_recv()
            return 0

        lax.fori_loop(lo, hi, forward, 0)

    def tokens_of(b):
        near[b].wait_recv()
        passed[b].wait_recv()

    def second_tokens():
        far[1].wait_recv()
        passed[1].start()

    def step(it, _):
        b, q = it // nq, lax.rem(it, nq)
        for i in range(nb):

            @pl.when(it == i * nq)
            def _(i=i):
                tokens_of(i)

        def at(events):
            for when, action in events:

                @pl.when(it == when)
                def _(action=action):
                    action()

        def up_out(k):
            up_ring.forward(k)
            out_ring.forward(k)
            far_ring.forward(k)

        at(((4, lambda: up_out(4)), (4, down_ring.start)))

        @pl.when(q == 0)
        def _():
            project(b)
            vt[...] = qkv[b, 2].T
            for cp in keep_fields(b):
                cp.start()

        at(
            (
                (0, lambda: up_out(2)),
                (2, lambda: up_out(3)),
                (2, second_tokens),
                (6, lambda: pass_attn(0, nq)),
                (7, lambda: down_ring.forward(2)),
            )
        )
        r = pl.ds(pl.multiple_of(q * blk, blk), blk)
        query, keys = qkv[b, 0, r], qkv[b, 1]
        outs, stats = [], []
        masked = jnp.concatenate(
            [
                jnp.where(lax.rem(lane, 128) // 32 == h, query, jnp.zeros_like(query))
                for h in range(heads)
            ],
            axis=0,
        )
        both = mm_nt(keys, masked)
        tops = jnp.max(both, axis=0, keepdims=True)
        expo = jnp.exp2(both - tops)
        totals = jnp.sum(expo, axis=0, keepdims=True)
        expo = expo.astype(BF)
        shares = 1.0 / totals
        for h in range(heads):
            c = slice(h * blk, (h + 1) * blk)
            outs.append(mm(vt[h * HD : (h + 1) * HD], expo[:, c]) * shares[:, c])
            stats.append(tops[:, c] + jnp.log2(totals[:, c]))
        attn[b, s, r] = jnp.concatenate(outs, axis=0).T.astype(BF)
        lse[b, :, r] = jnp.concatenate(stats + [jnp.zeros((8 - heads, blk), F32)], axis=0)
        attn_copy(0, it).start()
        attn_copy(1, it).start()
        return 0

    lax.fori_loop(0, nb * nq, step, 0)
    for cp in cot_far[2:] + cot_near:
        cp.start()
    keep = pltpu.make_async_copy(attn.at[:, s], attn_heads, ls.at[10])
    keep.start()
    out_ring.arrive()
    far_ring.arrive()
    local[4].wait()
    cross = []
    for e, other in ((0, s), (1, s2)):
        ref = outv.at[pl.ds(pl.multiple_of(other * nr, nr), nr)]
        cp = remote(ref, ref, ss, rs, 16 + e, (g, s1))
        cp.start()
        cross.append(cp)
    up_ring.arrive()
    local[2].wait()
    for cp in cross:
        cp.wait_recv()
    arrive_attn(0, nq)
    keep_out = pltpu.make_async_copy(outv, out_all, ls.at[11])
    keep_out.start()
    keep_up = pltpu.make_async_copy(upv, up_all, ls.at[12])
    keep_up.start()

    def keep_block(i):
        return (
            pltpu.make_async_copy(act.at[i], act_out.at[i], os_.at[0, i]),
            pltpu.make_async_copy(slope.at[i], slope_out.at[i], os_.at[1, i]),
            pltpu.make_async_copy(htwo.at[i], htwo_out.at[i], os_.at[2, i]),
        )

    def feed(i, _):
        b, owner = i // 4, lax.rem(i, 4)
        for when, action in (
            (1, lambda: down_ring.forward(3)),
            (3, lambda: pass_attn(nq, 2 * nq)),
            (4, lambda: arrive_attn(nq, 2 * nq)),
            (4, lambda: down_ring.forward(4)),
        ):

            @pl.when(i == when)
            def _(action=action):
                action()

        scale = 1.0 + modul[pl.ds(b, 1), D:]
        r = pl.ds(pl.multiple_of(owner * tl, tl), tl)
        joined = jnp.concatenate([attn[b, j, r] for j in range(4)], axis=1)
        mid = tokv[b, owner].astype(F32) + mm(joined, outv[...])
        normed, _inv = moments(mid)
        h = (normed * scale).astype(BF)
        upper = mm(h, upv[...])
        phi = 0.5 * (1.0 + lax.erf(upper * ROOT_HALF))
        act[i] = (upper * phi).astype(BF)
        slope[i] = (phi + upper * (DENSITY * jnp.exp(-0.5 * upper * upper))).astype(BF)
        htwo[i] = h

        @pl.when(owner == s)
        def _():
            mids[b] = mid

        for cp in keep_block(i):
            cp.start()
        return 0

    lax.fori_loop(0, 4 * nb, feed, 0)
    keep_mid = pltpu.make_async_copy(mids, mid_out, ls.at[13])
    keep_mid.start()
    own_rows = pl.ds(pl.multiple_of(s * tl, tl), tl)
    keep_rows = pltpu.make_async_copy(attn.at[:, :, own_rows], attn_rows, ls.at[14])
    keep_rows.start()
    for b in range(nb):
        for k, piece in enumerate(pieces):
            if piece[0] == b:
                cot_far[k].wait_recv()
        cot_pass[b].start()

    def finish(it, _):
        attn_copy(0, it).wait_send()
        attn_copy(1, it).wait_send()
        attn_copy(2, it).wait_send()
        return 0

    lax.fori_loop(0, nb * nq, finish, 0)

    def kept(i, _):
        for cp in keep_block(i):
            cp.wait()
        return 0

    lax.fori_loop(0, 4 * nb, kept, 0)
    down_ring.arrive()
    for cp in cot_near + cot_pass:
        cp.wait()
    for cp in cot_far + far + near + passed + small + cross + [pair_out]:
        cp.wait_send()
    for ring in [time_ring, up_ring, down_ring, out_ring, far_ring] + qkv_rings:
        ring.drain()
    local[3].wait()
    for cp in (keep_cot, keep, keep_w, keep_out, keep_up, keep_mid, keep_rows):
        cp.wait()
    for b in range(nb):
        for cp in keep_fields(b):
            cp.wait()


def run_k1(nd, tokens, w_time, feats, w_qkv, w_out, w_up, w_down, cs, sn, cot):
    nb, tl, width = tokens.shape
    rows = 4 * tl
    cols = w_qkv.shape[1] // 3
    hidden = w_up.shape[1]
    vm = pl.BlockSpec(memory_space=pltpu.VMEM)
    hb = pl.BlockSpec(memory_space=pl.ANY)
    steps = nb * (rows // 256)
    sds = jax.ShapeDtypeStruct
    dma = pltpu.SemaphoreType.DMA
    v = pltpu.VMEM
    return pl.pallas_call(
        k1_body,
        out_shape=(
            sds((nb, 2 * width), F32),
            sds((nb, TF), F32),
            sds((width, 3 * cols), BF),
            sds((width, width), BF),
            sds((width, hidden), BF),
            sds((hidden, width), BF),
            sds((nb, rows, width), BF),
            sds((nb, 3, rows, cols), BF),
            sds((nb, 8, rows), F32),
            sds((nb, rows, cols), BF),
            sds((nb, 4, tl, cols), BF),
            sds((nb, 4, tl, width), BF),
            sds((4 * nb, tl, hidden), BF),
            sds((4 * nb, tl, hidden), BF),
            sds((4 * nb, tl, width), BF),
            sds((nb, tl, width), F32),
        ),
        in_specs=[hb, vm, vm, vm, vm, vm, vm, hb, hb, hb],
        out_specs=(vm, vm, hb, hb, hb, hb, hb, hb, vm) + (hb,) * 7,
        scratch_shapes=[
            v((nb, 4, tl, width), BF),
            v((nd,) + w_time.shape, BF),
            v((4, nb, 2 * width), F32),
            v((cols, rows), BF),
            v((nb, tl, width), BF),
            v((width, 3 * cols), BF),
            v((nb, rows, width), BF),
            v((nb, 3, rows, cols), BF),
            v((nb, 4, rows, cols), BF),
            v((width, width), BF),
            v((width, hidden), BF),
            v((4 * nb, tl, hidden), BF),
            v((4 * nb, tl, hidden), BF),
            v((4 * nb, tl, width), BF),
            v((nb, tl, width), F32),
            v(cs.shape, F32),
            v(sn.shape, F32),
            dma((2, nb)),
            dma((15,)),
            dma((22,)),
            dma((22,)),
            dma((56,)),
            dma((56,)),
            dma((3, steps)),
            dma((3, steps)),
            dma((3, 4 * nb)),
        ],
        compiler_params=pltpu.CompilerParams(
            collective_id=0, has_side_effects=True, vmem_limit_bytes=VMEM_LIMIT
        ),
        name="attention_forward",
    )(tokens, w_time, feats, w_qkv, w_out, w_up, w_down, cs, sn, cot)


def k2_body(
    act_h, slope_h, htwo_h, mid_h, attn_h, cot_h, modul, w_out_h, w_up_h, w_down_h,
    grad_up, grad_out, d_mid_h, base_h, osend_h, d_heads, dsc, s_down,
    act, dup, htwo, mids, attn, cot, w_out, w_up, w_down, d_mid, base, osend,
    pa, pb_, ra, rb, xs, xr, dat, stage, gdv, down_h, down_w,
    ls, ss, rs, os_, ins, keeps, bs, gs, gr,
):
    g, s, core, s1, s2, s3 = peers()
    p = ring_place(g)
    chip = s // 2
    nb, tl = cot.shape[0], cot.shape[2]

    def pull(jp, which):
        phase, b = jp // nb, lax.rem(jp, nb)
        where = chip + (1 - phase) * (1 - 2 * chip)
        owner = 2 * where + (1 - core if which == 0 else core)
        i = b * 4 + owner
        k = 2 * jp + which
        return (
            pltpu.make_async_copy(cot_h.at[b, owner], cot.at[b, owner], bs.at[0, k]),
            pltpu.make_async_copy(slope_h.at[i], dup.at[i], bs.at[1, k]),
            pltpu.make_async_copy(act_h.at[i], act.at[i], bs.at[2, k]),
        )

    loads = []
    for i, (src, dst) in enumerate(
        (
            (w_down_h, w_down), (w_up_h, w_up),
            (mid_h, mids), (w_out_h, w_out), (htwo_h, htwo), (attn_h, attn),
        )
    ):
        loads.append(pltpu.make_async_copy(src, dst, ins.at[i]))
    first = pull(0, 0)
    loads[0].start()
    for cp in first:
        cp.start()
    loads[1].start()
    greet([(g, s1), (g, s2), (g, s3), (ring_index(p + 1), s), (ring_index(p - 1), s)])
    hidden = act.shape[2]
    pc = s_down.shape[1]

    def view_down(j, half):
        lo, n = (0, hidden) if half is None else (half * (hidden // 2), hidden // 2)
        return gdv.at[lo : lo + n, pl.ds(pl.multiple_of(j * pc, pc), pc)]

    down_ring = Scatter(view_down, down_h, down_w, gs, gr, 0)

    def back_part(b, owner):
        i = b * 4 + owner
        d_act = mm_nt(cot[b, owner], w_down[...])
        d_up = (d_act * dup[i].astype(F32)).astype(BF)
        dup[i] = d_up
        return mm_nt(d_up, w_up[...])

    def back_copy(jp):
        return remote(pa.at[jp], ra.at[jp], ss, rs, jp, (g, s1))

    def out_copy(jp):
        return remote(pb_.at[jp], rb.at[jp], ss, rs, 4 + jp, (g, s1))

    def far_copy(b):
        return remote(xs.at[b], xr.at[b], ss, rs, 8 + b, (g, s2))

    def place(jp):
        phase, b = jp // nb, lax.rem(jp, nb)
        return phase, b, chip + (1 - phase) * (1 - 2 * chip)

    def give(jp, _):
        phase, b, where = place(jp)

        @pl.when(phase == 0)
        def _():
            for cp in pull(jp, 0):
                cp.wait()

        pa[jp] = back_part(b, 2 * where + 1 - core).astype(BF)
        back_copy(jp).start()
        return 0

    def take(jp, _):
        phase, b, where = place(jp)

        @pl.when(phase == 0)
        def _():
            for cp in pull(jp, 1):
                cp.wait()

        dh = back_part(b, 2 * where + core)
        back_copy(jp).wait_recv()
        dh = dh + ra[jp].astype(F32)

        @pl.when(phase == 0)
        def _():
            xs[b] = dh.astype(BF)
            far_copy(b).start()

        @pl.when(phase == 1)
        def _():
            d_mid[b] = dh

        return 0

    def give_out(jp, _):
        _phase, b, where = place(jp)
        pb_[jp] = mm(act[b * 4 + 2 * where + 1 - core], w_down[...]).astype(BF)
        out_copy(jp).start()
        return 0

    def take_out(jp, _):
        phase, b, where = place(jp)
        out = mm(act[b * 4 + 2 * where + core], w_down[...])
        out_copy(jp).wait_recv()
        out = out + rb[jp].astype(F32)

        @pl.when(phase == 0)
        def _():
            osend[b] = out.astype(BF)

        @pl.when(phase == 1)
        def _():
            base[b] = out + mids[b]

        return 0

    def down_grads(i, _):
        r = pl.ds(pl.multiple_of(i * 256, 256), 256)
        left = act[:, :, r].reshape(4 * nb * tl, 256)
        gdv[r] = mm_tn(left, cot[...].reshape(4 * nb * tl, D)).astype(BF)
        return 0

    def up_copy(i):
        r = pl.ds(pl.multiple_of(i * 256, 256), 256)
        return pltpu.make_async_copy(stage.at[i], grad_up.at[r], os_.at[i])

    def up_grads(i, _):
        r = pl.ds(pl.multiple_of(i * 256, 256), 256)
        left = htwo[:, :, r].reshape(4 * nb * tl, 256)
        stage[i] = mm_tn(left, dup[...].reshape(4 * nb * tl, hidden)).astype(BF)
        up_copy(i).start()
        return 0

    def spread(e, other, b):
        return remote(dat.at[other, b], d_heads.at[s, b], ss, rs, 10 + 2 * e + b, (g, other))

    def tail(b, _):
        scale = 1.0 + modul[pl.ds(b, 1), D:]
        far_copy(b).wait_recv()
        dh = d_mid[b] + xr[b].astype(F32)
        normed, inverse = moments(mids[b])
        dsc[pl.ds(b, 1)] = jnp.sum(dh * normed, axis=0, keepdims=True)
        dn = dh * scale
        inner = jnp.mean(dn * normed, axis=-1, keepdims=True)
        dm = cot[b, s].astype(F32) + inverse * (
            dn - jnp.mean(dn, axis=-1, keepdims=True) - normed * inner
        )
        d_mid[b] = dm
        branch = mm_nt(dm.astype(BF), w_out[...]).astype(BF)
        for j in range(4):
            dat[j, b] = branch[:, j * 256 : (j + 1) * 256]
        for e, other in ((0, s2), (1, s3), (2, s1)):
            spread(e, other, b).start()
        return 0

    for which in (0, 1):
        for jp in range(nb):
            if jp + which:
                for cp in pull(jp, which):
                    cp.start()
    for cp in loads[:2]:
        cp.wait()
    half = D // 512
    lax.fori_loop(0, nb, give, 0)
    for jp in range(nb, 2 * nb):
        for which in (0, 1):
            for cp in pull(jp, which):
                cp.start()
    for cp in loads[2:]:
        cp.start()
    lax.fori_loop(0, nb, take, 0)
    lax.fori_loop(0, nb, give_out, 0)
    lax.fori_loop(0, nb, take_out, 0)
    for jp in range(nb, 2 * nb):
        for which in (0, 1):
            for cp in pull(jp, which):
                cp.wait()
    lax.fori_loop(0, hidden // 256, down_grads, 0)
    down_ring.start()
    for cp in loads[2:]:
        cp.wait()
    lax.fori_loop(nb, 2 * nb, give, 0)
    lax.fori_loop(nb, 2 * nb, take, 0)
    down_ring.forward(2)
    lax.fori_loop(0, nb - 1, tail, 0)
    lax.fori_loop(nb, 2 * nb, give_out, 0)
    lax.fori_loop(nb, 2 * nb, take_out, 0)
    down_ring.forward(3)
    lax.fori_loop(0, half, up_grads, 0)
    lax.fori_loop(nb - 1, nb, tail, 0)
    lax.fori_loop(half, 2 * half, up_grads, 0)
    keep_all = []
    for i, (src, dst) in enumerate(
        ((d_mid, d_mid_h), (base, base_h), (osend, osend_h), (dat.at[s], d_heads.at[s]))
    ):
        cp = pltpu.make_async_copy(src, dst, keeps.at[i])
        cp.start()
        keep_all.append(cp)
    down_ring.forward(4)
    branch = d_mid[...].astype(BF).reshape(nb * tl, D)
    for j in range(4):
        left = jnp.concatenate([attn[b, j] for b in range(nb)], axis=0)
        up_copy(j).wait()
        stage[j] = mm_tn(left, branch).astype(BF)
        pltpu.make_async_copy(stage.at[j], grad_out.at[j], os_.at[j]).start()

    def done(jp, _):
        back_copy(jp).wait_send()
        out_copy(jp).wait_send()
        return 0

    lax.fori_loop(0, 2 * nb, done, 0)
    s_down[...] = down_ring.result()
    down_ring.drain()
    for b in range(nb):
        far_copy(b).wait_send()
        for e, other in ((0, s2), (1, s3), (2, s1)):
            spread(e, other, b).wait()
    for j in range(4):
        pltpu.make_async_copy(stage.at[j], grad_out.at[j], os_.at[j]).wait()
    for cp in keep_all:
        cp.wait()


def run_k2(nd, act, slope, htwo, mid, attn_rows, cot_all, modul, w_out, w_up, w_down):
    nb, _, tl, width = cot_all.shape
    hidden = w_up.shape[1]
    cols = attn_rows.shape[3]
    pc = width // nd
    vm = pl.BlockSpec(memory_space=pltpu.VMEM)
    hb = pl.BlockSpec(memory_space=pl.ANY)
    sds = jax.ShapeDtypeStruct
    v = pltpu.VMEM
    dma = pltpu.SemaphoreType.DMA
    return pl.pallas_call(
        k2_body,
        out_shape=(
            sds((width, hidden), BF),
            sds((4, cols, width), BF),
            sds((nb, tl, width), F32),
            sds((nb, tl, width), F32),
            sds((nb, tl, width), BF),
            sds((4, nb, tl, cols), BF),
            sds((nb, width), F32),
            sds((hidden, pc), F32),
        ),
        in_specs=[hb, hb, hb, hb, hb, hb, vm, hb, hb, hb],
        out_specs=(hb, hb, hb, hb, hb, hb, vm, vm),
        scratch_shapes=[
            v(act.shape, BF),
            v(slope.shape, BF),
            v(htwo.shape, BF),
            v(mid.shape, F32),
            v(attn_rows.shape, BF),
            v(cot_all.shape, BF),
            v(w_out.shape, BF),
            v(w_up.shape, BF),
            v(w_down.shape, BF),
            v((nb, tl, width), F32),
            v((nb, tl, width), F32),
            v((nb, tl, width), BF),
            v((2 * nb, tl, width), BF),
            v((2 * nb, tl, width), BF),
            v((2 * nb, tl, width), BF),
            v((2 * nb, tl, width), BF),
            v((nb, tl, width), BF),
            v((nb, tl, width), BF),
            v((4, nb, tl, cols), BF),
            v((4, 256, width), BF),
            v((hidden, width), BF),
            v((2, hidden // 2, pc), BF),
            v((6, hidden, pc), BF),
            dma,
            dma((16,)),
            dma((16,)),
            dma((4,)),
            dma((6,)),
            dma((4,)),
            dma((3, 4 * nb)),
            dma((8,)),
            dma((8,)),
        ],
        compiler_params=pltpu.CompilerParams(
            collective_id=1, has_side_effects=True, vmem_limit_bytes=VMEM_LIMIT
        ),
        name="feed_forward",
    )(act, slope, htwo, mid, attn_rows, cot_all, modul, w_out, w_up, w_down)


def k3_body(
    fields_h, lse, attn_h, d_heads_h, w_h, normed_h, tok_h, modul, cs_h, sn_h, d_mid_h, base_h, osend,
    g_up, g_out, dsc_h, feats,
    output, grad_tok, s_qkv, s_out, s_up, s_time,
    orecv, dqt, draw, pa, ra, xs, xr, sumh, dhb,
    vu, vo, vq, oa, ob, ox, osum, up_h, up_w, out_h, out_w, qkv_h, qkv_w,
    dpart, tx, dall, qkv, own, d_heads, w, normed_one, tok, cs, sn, d_mid, base, dsc_two,
    ins, ls, ss, rs, gs, gr,
):
    g, s, core, s1, s2, s3 = peers()
    chip = s // 2
    p = ring_place(g)
    nd = dall.shape[0]
    loads = [
        pltpu.make_async_copy(g_up, vu, ls.at[0]),
        pltpu.make_async_copy(g_out, oa, ls.at[1]),
    ]
    pulls = []
    for i, (src, dst) in enumerate(
        (
            (fields_h.at[0], qkv.at[0]), (d_heads_h.at[:, 0], d_heads.at[:, 0]),
            (attn_h.at[0], own.at[0]), (cs_h, cs), (sn_h, sn),
            (fields_h.at[1], qkv.at[1]), (d_heads_h.at[:, 1], d_heads.at[:, 1]),
            (attn_h.at[1], own.at[1]),
            (w_h, w), (normed_h, normed_one), (tok_h, tok), (d_mid_h, d_mid), (base_h, base),
            (dsc_h, dsc_two),
        )
    ):
        pulls.append(pltpu.make_async_copy(src, dst, ins.at[i]))
    for cp in pulls[:5]:
        cp.start()
    for cp in loads:
        cp.start()
    others = [(lax.rem(g + d, nd), s) for d in range(1, nd)]
    greet([(g, s1), (g, s2)] + others)
    nb, tl = tok.shape[0], tok.shape[1]
    rows, cols = own.shape[1], own.shape[2]
    heads = cols // HD
    blk = 256
    nk = rows // blk
    pc = D // nd

    def lanes(j, size):
        return pl.ds(pl.multiple_of(j * size, size), size)

    def view_cols(ref, size):
        def view(j, half):
            lo, n = (0, size) if half is None else (half * (size // 2), size // 2)
            return ref.at[lo : lo + n, lanes(j, pc)]

        return view

    def view_rows(ref):
        def view(j, half):
            lo, n = (0, pc) if half is None else (half * (pc // 2), pc // 2)
            return ref.at[pl.ds(pl.multiple_of(j * pc + lo, n), n)]

        return view

    up_ring = Scatter(view_rows(vu), up_h, up_w, gs, gr, 16)
    out_rings = [
        Scatter(view_cols(vo.at[i], vo.shape[1]), out_h.at[i], out_w.at[i], gs, gr, 8 * i)
        for i in range(2)
    ]
    def view_qkv(side):
        wide = vq.shape[1] // 2

        def view(j, half):
            lo, n = (0, pc) if half is None else (half * (pc // 2), pc // 2)
            return vq.at[
                pl.ds(pl.multiple_of(j * pc + lo, n), n), side * wide : (side + 1) * wide
            ]

        return view

    qkv_rings = [
        Scatter(view_qkv(i), qkv_h.at[i], qkv_w.at[i], gs, gr, 24 + 16 * i) for i in range(2)
    ]

    def qkv_forward(k):
        for ring in qkv_rings:
            ring.forward(k)

    loads[0].wait()
    up_ring.start()
    back = []
    for b in range(nb):
        cp = remote(osend.at[b], orecv.at[b], ss, rs, b, (g, s2))
        cp.start()
        back.append(cp)
    loads[1].wait()
    cross = []
    for i in range(2):
        cp = remote(oa.at[2 * i + 1 - core], ob.at[i], ss, rs, 8 + i, (g, s1))
        cp.start()
        cross.append(cp)
    over = remote(osum, ox, ss, rs, 10, (g, s2))

    def out_pair():
        for i in range(2):
            cross[i].wait_recv()
            vo[i] = (oa[2 * i + core].astype(F32) + ob[i].astype(F32)).astype(BF)
            out_rings[i].start()

    def out_forward(k):
        for ring in out_rings:
            ring.forward(k)

    lane = lax.broadcasted_iota(jnp.int32, (1, cols), 1)

    def near_copy(b, phase):
        i = 2 * b + phase
        return remote(pa.at[i], ra.at[i], ss, rs, 2 + i, (g, s1))

    def far_copy(b):
        return remote(xs.at[b], xr.at[b], ss, rs, 6 + b, (g, s2))

    for cp in pulls[:5]:
        cp.wait()
    for cp in pulls[5:]:
        cp.start()

    def grads(side):
        wide = vq.shape[1] // 2
        c = slice(side * wide, (side + 1) * wide)

        def one(i, _):
            r = pl.ds(pl.multiple_of(i * 256, 256), 256)
            left = jnp.concatenate(
                [
                    (normed_one[b, :, r].astype(F32) * (1.0 + modul[b : b + 1, r])).astype(BF)
                    for b in range(nb)
                ],
                axis=0,
            )
            vq[r, c] = mm_tn(left, draw[:, :, c].reshape(nb * rows, wide)).astype(BF)
            return 0

        lax.fori_loop(0, D // 256, one, 0)
        qkv_rings[side].start()

    def sequence(b, _):
        @pl.when(b == 1)
        def _():
            for cp in pulls[5:8]:
                cp.wait()

        for j in range(4):
            dhb[j * tl : (j + 1) * tl] = d_heads[j, b]
        query = qkv[b, 0]
        d_out = dhb[...]
        prod = d_out.astype(F32) * own[b].astype(F32)
        prod = prod.T
        delta = jnp.concatenate(
            [jnp.sum(prod[h * HD : (h + 1) * HD], axis=0, keepdims=True) for h in range(heads)],
            axis=0,
        )
        dqt[...] = jnp.zeros_like(dqt)

        def keys_block(i, _):
            it = b * nk + i
            for when, act in (
                (1, out_pair),
                (2, lambda: up_ring.forward(2)),
                (3, lambda: out_forward(2)),
                (4, lambda: up_ring.forward(3)),
                (5, lambda: out_forward(3)),
                (6, lambda: up_ring.forward(4)),
                (7, lambda: out_forward(4)),
            ):

                @pl.when(it == when)
                def _(act=act):
                    act()

            r = pl.ds(pl.multiple_of(i * blk, blk), blk)
            keys, values = qkv[b, 1, r], qkv[b, 2, r]
            dk = jnp.zeros((blk, cols), F32)
            dv = jnp.zeros((blk, cols), F32)
            for h in range(heads):
                mask = lax.rem(lane, 128) // 32 == h
                mask_v = lane // HD == h
                km = jnp.where(mask, keys, jnp.zeros_like(keys))
                vmask = jnp.where(mask_v, values, jnp.zeros_like(values))
                probs = jnp.exp2(mm_nt(km, query) - lse[b, h : h + 1])
                d_probs = mm_nt(vmask, d_out)
                ds = (probs * (d_probs - delta[h : h + 1])).astype(BF)
                dv = jnp.where(mask_v, mm(probs.astype(BF), d_out), dv)
                dk = jnp.where(mask, mm(ds, query), dk)
                dqt[...] += mm_tn(km, ds)
            c, n = cs[r] * math.log(2.0), sn[r] * math.log(2.0)
            da, db = dk[:, :128], dk[:, 128:]
            draw[b, r, 256:512] = jnp.concatenate([da * c + db * n, db * c - da * n], axis=1).astype(BF)
            draw[b, r, 512:768] = dv.astype(BF)
            return 0

        lax.fori_loop(0, nk, keys_block, 0)
        dq = dqt[...].T * 0.125
        da, db = dq[:, :128], dq[:, 128:]
        c, n = cs[...], sn[...]
        draw[b, :, 0:256] = jnp.concatenate([da * c + db * n, db * c - da * n], axis=1).astype(BF)

        @pl.when(b == 0)
        def _():
            for cp in pulls[8:]:
                cp.wait()
            dpart[0, :, :D] = jnp.zeros((nb, D), F32)

        def part(owner):
            r = pl.ds(pl.multiple_of(owner * tl, tl), tl)
            res = mm_nt(draw[b, r], w[...])
            dpart[0, pl.ds(b, 1), :D] += jnp.sum(
                res * normed_one[b, r].astype(F32), axis=0, keepdims=True
            )
            return res

        for phase in range(2):
            where = chip if phase else 1 - chip
            pa[2 * b + phase] = part(2 * where + 1 - core).astype(BF)
            near_copy(b, phase).start()
        kept = part(2 * (1 - chip) + core)
        near_copy(b, 0).wait_recv()
        xs[b] = (kept + ra[2 * b].astype(F32)).astype(BF)
        far_copy(b).start()

        @pl.when(b == nb - 1)
        def _():
            grads(0)
            grads(1)

        kept = part(2 * chip + core)
        near_copy(b, 1).wait_recv()
        sumh[b] = kept + ra[2 * b + 1].astype(F32)
        return 0

    lax.fori_loop(0, nb, sequence, 0)
    dpart[0, :, D:] = dsc_two[...]
    small = [remote(dpart.at[0], dpart.at[1], ss, rs, 11, (g, s1))]
    small[0].start()
    first_out, second_out = out_rings[0].result(), out_rings[1].result()
    osum[...] = jnp.where(chip == 0, second_out, first_out).astype(BF)
    own_out = jnp.where(chip == 0, first_out, second_out)
    over.start()
    qkv_forward(2)
    small[0].wait_recv()
    dall[0, :, : 2 * D] = dpart[0] + dpart[1]
    dall[0, :, 2 * D :] = feats[...]
    wide = [remote(dall.at[0], dall.at[d], ss, rs, 12 + d, others[d - 1]) for d in range(1, nd)]
    for cp in wide:
        cp.start()
    for b in range(nb):
        back[b].wait_recv()
        output[b] = (base[b] + orecv[b].astype(F32)).astype(BF)
    s_up[...] = up_ring.result()
    qkv_forward(3)

    def tail(b, _):
        scale = 1.0 + modul[pl.ds(b, 1), :D]
        far_copy(b).wait_recv()
        normed, inverse = moments(tok[b].astype(F32))
        dn = (sumh[b] + xr[b].astype(F32)) * scale
        inner = jnp.mean(dn * normed, axis=-1, keepdims=True)
        grad_tok[b] = (
            d_mid[b]
            + inverse * (dn - jnp.mean(dn, axis=-1, keepdims=True) - normed * inner)
        ).astype(BF)
        return 0

    lax.fori_loop(0, nb - 1, tail, 0)
    qkv_forward(4)
    lax.fori_loop(nb - 1, nb, tail, 0)
    over.wait_recv()
    s_out[...] = own_out + ox[...].astype(F32)
    for cp in wide:
        cp.wait_recv()
    depth = s_time.shape[0]
    lane_t = lax.broadcasted_iota(jnp.int32, (depth, TF), 1)
    row_t = lax.broadcasted_iota(jnp.int32, (depth, TF), 0)
    mine = jnp.zeros((depth, 2 * D), F32)
    theirs = jnp.zeros((depth, 2 * D), F32)
    for d in range(nd):
        for b in range(nb):
            row = dall[d, b : b + 1]
            for which, other in ((0, s), (1, s2)):
                hit = lane_t == row_t + (4 * g + other) * depth
                column = jnp.sum(jnp.where(hit, row[:, 2 * D :], 0.0), axis=1, keepdims=True)
                if which:
                    theirs = theirs + column * row[:, : 2 * D]
                else:
                    mine = mine + column * row[:, : 2 * D]
    tx[0] = theirs
    swap = remote(tx.at[0], tx.at[1], ss, rs, 12, (g, s2))
    swap.start()
    s_qkv[...] = jnp.concatenate([ring.result() for ring in qkv_rings], axis=1)
    swap.wait_recv()
    s_time[...] = mine + tx[1]
    for b in range(nb):
        back[b].wait_send()
        far_copy(b).wait_send()
        for phase in range(2):
            near_copy(b, phase).wait_send()
    for cp in cross + small + wide + [over, swap]:
        cp.wait_send()
    for ring in out_rings + qkv_rings + [up_ring]:
        ring.drain()


def run_k3(
    nd, qkv, lse, attn_heads, d_heads, w, normed, tokens, modul, cs, sn, d_mid, base, osend,
    g_up, g_out, dsc_two, feats,
):
    nb, tl, width = tokens.shape
    rows, cols = attn_heads.shape[1], attn_heads.shape[2]
    hidden = g_up.shape[1]
    pc = width // nd
    vm = pl.BlockSpec(memory_space=pltpu.VMEM)
    hb = pl.BlockSpec(memory_space=pl.ANY)
    sds = jax.ShapeDtypeStruct
    v = pltpu.VMEM
    dma = pltpu.SemaphoreType.DMA
    return pl.pallas_call(
        k3_body,
        out_shape=(
            sds((nb, tl, width), BF),
            sds((nb, tl, width), BF),
            sds((pc, 3 * cols), F32),
            sds((cols, pc), F32),
            sds((pc, hidden), F32),
            sds((TF // (4 * nd), 2 * width), F32),
        ),
        in_specs=[hb, vm, hb, hb, hb, hb, hb, vm, hb, hb, hb, hb, hb, hb, hb, pl.BlockSpec(memory_space=pltpu.HBM), vm],
        out_specs=(vm,) * 6,
        scratch_shapes=[
            v((nb, tl, width), BF),
            v((cols, rows), F32),
            v((nb, rows, 3 * cols), BF),
            v((2 * nb, tl, width), BF),
            v((2 * nb, tl, width), BF),
            v((nb, tl, width), BF),
            v((nb, tl, width), BF),
            v((nb, tl, width), F32),
            v((rows, cols), BF),
            v((width, hidden), BF),
            v((2, cols, width), BF),
            v((width, 3 * cols), BF),
            v((4, cols, width), BF),
            v((2, cols, width), BF),
            v((cols, pc), BF),
            v((cols, pc), BF),
            v((2, pc // 2, hidden), BF),
            v((6, pc, hidden), BF),
            v((2, 2, cols // 2, pc), BF),
            v((2, 6, cols, pc), BF),
            v((2, 2, pc // 2, 3 * cols // 2), BF),
            v((2, 6, pc, 3 * cols // 2), BF),
            v((2, nb, 2 * width), F32),
            v((2, TF // (4 * nd), 2 * width), F32),
            v((nd, nb, 2 * width + TF), F32),
            v(qkv.shape, BF),
            v((nb, rows, cols), BF),
            v(d_heads.shape, BF),
            v(w.shape, BF),
            v(normed.shape, BF),
            v(tokens.shape, BF),
            v(cs.shape, F32),
            v(sn.shape, F32),
            v(d_mid.shape, F32),
            v(base.shape, F32),
            v(dsc_two.shape, F32),
            dma((14,)),
            dma((2,)),
            dma((20,)),
            dma((20,)),
            dma((48,)),
            dma((48,)),
        ],
        compiler_params=pltpu.CompilerParams(
            collective_id=2, has_side_effects=True, vmem_limit_bytes=52 * 1024 * 1024
        ),
        name="attention_backward",
    )(
        qkv, lse, attn_heads, d_heads, w, normed, tokens, modul, cs, sn, d_mid, base, osend,
        g_up, g_out, dsc_two, feats,
    )


def k4_body(*refs):
    *refs, sems = refs
    count = len(refs) // 2
    moves = []
    for i in range(2):
        moves.append(pltpu.make_async_copy(refs[i], refs[count + i], sems.at[i]))
        moves[i].start()
    for i in range(3, count):
        refs[count + i][...] = refs[i][...]
    w = refs[2][...]
    heads = w.shape[1] // (3 * HD)
    half, size = HD // 2, heads * HD
    pieces = []
    for h in range(heads):
        for part in (0, 1):
            for side in (0, 1):
                at = part * size + side * (size // 2) + h * half
                pieces.append(w[:, at : at + half])
        at = 2 * size + h * HD
        pieces.append(w[:, at : at + HD])
    refs[count + 2][...] = jnp.concatenate(pieces, axis=1)
    for cp in moves:
        cp.wait()


def run_k4(arrays):
    vm = pl.BlockSpec(memory_space=pltpu.VMEM)
    hb = pl.BlockSpec(memory_space=pltpu.HBM)
    specs = [hb, hb] + [vm] * (len(arrays) - 2)
    return pl.pallas_call(
        k4_body,
        out_shape=tuple(jax.ShapeDtypeStruct(a.shape, a.dtype) for a in arrays),
        in_specs=specs,
        out_specs=tuple(specs),
        scratch_shapes=[pltpu.SemaphoreType.DMA((2,))],
        compiler_params=pltpu.CompilerParams(vmem_limit_bytes=16 * 1024 * 1024),
        name="results",
    )(*arrays)


def fast_shards(nd, tokens, bins, plan, w_qkv, w_out, w_up, w_down, w_time, cotangent):
    nb, tl, width = tokens.shape
    rows = 4 * tl
    feats = time_features(plan, bins).astype(BF).astype(F32)
    half = HD // 2
    inverse = np.exp(np.arange(half, dtype=np.float32) * np.float32(-math.log(10000.0) / half))
    angle = np.arange(rows, dtype=np.float32)[:, None] * inverse.astype(np.float32)[None, :]
    cs = np.tile(np.cos(angle.astype(np.float64)).astype(np.float32), (1, 128 // half))
    sn = np.tile(np.sin(angle.astype(np.float64)).astype(np.float32), (1, 128 // half))
    (
        modul, feats, full_qkv, full_out, full_up, full_down, normed, qkv, lse, attn_heads, attn_rows,
        cot_all, act, slope, htwo, mid,
    ) = run_k1(
        nd, tokens, w_time, feats, w_qkv, w_out, w_up, w_down, cs, sn, cotangent
    )
    grad_up, grad_out, d_mid, base, osend, d_heads, dsc_two, sum_down = run_k2(
        nd, act, slope, htwo, mid, attn_rows, cot_all, modul, full_out, full_up, full_down
    )
    output, grad_tokens, sum_qkv, sum_out, sum_up, grad_time = run_k3(
        nd, qkv, lse, attn_heads, d_heads, full_qkv, normed, tokens, modul, cs, sn, d_mid, base,
        osend, grad_up, grad_out, dsc_two, feats,
    )
    return tuple(
        run_k4((output, grad_tokens, sum_qkv, sum_out, sum_up, sum_down, grad_time))
    )


def solution(mesh):
    nd, ns = mesh.shape["dp"], mesh.shape["seq"]
    fast = nd == 8 and ns == 4
    return jax.shard_map(
        functools.partial(fast_shards, nd) if fast else shards,
        mesh=mesh,
        in_specs=(
            P("dp", "seq", None),
            P("dp"),
            P(),
            P("dp", "seq"),
            P("seq", "dp"),
            P("dp", "seq"),
            P("seq", "dp"),
            P(("dp", "seq"), None),
            P("dp", "seq", None),
        ),
        out_specs=(
            P("dp", "seq", None),
            P("dp", "seq", None),
            P("dp", "seq"),
            P("seq", "dp"),
            P("dp", "seq"),
            P("seq", "dp"),
            P(("dp", "seq"), None),
        ),
        check_vma=False,
    )
```
